32 devices in a mesh: fsdp: 8 (over z, core), seq: 4 (over y, x).
Axes of the slice: x: 2, y: 2, z: 4, core: 2. Of those that a mesh axis runs over, the one named last changes fastest.
Arguments:
- tokens: bfloat16 [8, 1024, 2048], P('fsdp', 'seq'), may hold values from -6 to 6
- segments: int32 [8, 1024], P('fsdp'), may hold values from -1 to 513, as said below
- buckets: int32 [2047], replicated, may hold values from 0 to 31, as said below
- w_query: bfloat16 [2048, 2048], P('fsdp'), may hold values from -0.0625 to 0.0625
- w_key: bfloat16 [2048, 2048], P('fsdp'), may hold values from -0.0625 to 0.0625
- w_value: bfloat16 [2048, 2048], P('fsdp'), may hold values from -0.125 to 0.125
- w_attn_out: bfloat16 [2048, 2048], P('fsdp'), may hold values from -0.5 to 0.5
- gain_attn: bfloat16 [2048], P('fsdp'), may hold values from 0.25 to 1.75
- rel_table: float32 [32, 32], replicated, may hold values from -4 to 4
- w_gate: bfloat16 [2048, 5120], P('fsdp'), may hold values from -0.125 to 0.125
- w_up: bfloat16 [2048, 5120], P('fsdp'), may hold values from -0.125 to 0.125
- w_down: bfloat16 [2048, 5120], P('fsdp'), may hold values from -0.078125 to 0.078125
- gain_ffn: bfloat16 [2048], P('fsdp'), may hold values from 0.25 to 1.75
- out_grad: bfloat16 [8, 1024, 2048], P('fsdp', 'seq'), may hold values from -6 to 6
Outputs:
- layer_out: bfloat16 [8, 1024, 2048], P('fsdp', 'seq')
- input_grad: bfloat16 [8, 1024, 2048], P('fsdp', 'seq')
- w_query_grad: float32 [2048, 2048], P('fsdp')
- w_key_grad: float32 [2048, 2048], P('fsdp')
- w_value_grad: float32 [2048, 2048], P('fsdp')
- w_attn_out_grad: float32 [2048, 2048], P('fsdp')
- gain_attn_grad: float32 [2048], P('fsdp')
- rel_table_grad: float32 [32, 32], P('fsdp')
- w_gate_grad: float32 [2048, 5120], P('fsdp')
- w_up_grad: float32 [2048, 5120], P('fsdp')
- w_down_grad: float32 [2048, 5120], P('fsdp')
- gain_ffn_grad: float32 [2048], P('fsdp')
- rms_stats: float32 [3], replicated
The draws below stay inside these ranges and needn't reach their ends.
Inputs may be any that keep to these rules, and one draw needn't show every extreme that they name: `segments`: in each row the numbers never decrease before the padding, which is the last 1 to 128 tokens with -1; each row's last document before the padding has the number 2 * 256 + 1. One document of each row begins within the row's first 256 tokens and ends within its last 257 tokens, with at least one short document after it; the other documents are short, of heavy-tailed lengths. Entry 1023 + r holds the bucket of the offset r = key position - query position: buckets 0 to 15 for r <= 0, the others for r > 0, not falling as |r| grows on each side; every bucket occurs.
All inputs are finite; a program needn't handle non-finite values.
Results may differ from the reference program's by a relative error of at most 0.019.
Values may be sent and summed in bfloat16 or wider, within the bound.
No kernel may reach another device: no remote copies, remote signals or barrier semaphores. Data moves between devices by JAX's collectives and lax.ppermute only.
A program may use at most 704 MiB of HBM per device.

```python
from functools import partial
import jax
import jax.numpy as jnp
from jax import lax

D = 2048
H = 32
DH = 64
FF = 5120
NB = 32
TOK_DEV = 256
ROW = 1024
ROWS = 8


def packed_numbers(key):
    parts = jax.random.split(key, 5)
    begin = jax.random.randint(parts[0], (), 1, TOK_DEV)
    padding = jax.random.randint(parts[1], (), 1, TOK_DEV // 2 + 1)
    finish = ROW - padding - jax.random.randint(parts[2], (), 1, TOK_DEV // 2 + 1)
    head_lengths = 1 + 256 // jax.random.randint(parts[3], (TOK_DEV,), 1, 257)
    tail_lengths = 1 + 256 // jax.random.randint(parts[4], (TOK_DEV,), 1, 257)
    head_ends = jnp.cumsum(head_lengths)
    tail_ends = jnp.cumsum(tail_lengths)
    position = jnp.arange(ROW, dtype=jnp.int32)
    head_ids = jnp.sum(head_ends[None, :] <= position[:, None], axis=1)
    long_id = jnp.sum(head_ends <= begin - 1) + 1
    tail_index = jnp.sum(tail_ends[None, :] <= (position - finish)[:, None], axis=1)
    last_index = jnp.sum(tail_ends <= ROW - padding - 1 - finish)
    tail_ids = 2 * TOK_DEV + 1 - last_index + tail_index
    numbers = jnp.where(position < begin, head_ids, jnp.where(position < finish, long_id, tail_ids))
    return jnp.where(position >= ROW - padding, -1, numbers).astype(jnp.int32)


def draw_segments(key, part):
    key = jax.random.fold_in(key, 11)
    return jax.vmap(packed_numbers)(jax.random.split(key, ROWS))


def draw_buckets(key, part):
    key = jax.random.fold_in(key, 23)
    first_key, second_key = jax.random.split(key)
    halfway = NB // 2
    behind = jax.random.permutation(first_key, ROW - 1)[:halfway - 1] + 1
    ahead = jax.random.permutation(second_key, ROW - 2)[:halfway - 1] + 2
    offset = jnp.arange(2 * ROW - 1, dtype=jnp.int32) - (ROW - 1)
    distance = jnp.abs(offset)
    lower = jnp.sum(distance[:, None] >= behind[None, :], axis=1)
    upper = halfway + jnp.sum(distance[:, None] >= ahead[None, :], axis=1)
    return jnp.where(offset > 0, upper, lower).astype(jnp.int32)


def shard_levels(own_key, dims, cuts, least, largest):
    def one(dim, blocks):
        draws = jax.random.uniform(jax.random.fold_in(jax.random.fold_in(own_key, 6), dim), (blocks,), jnp.float32, least / len(cuts), largest / len(cuts))
        return jnp.repeat(jnp.exp(draws), dims[dim] // blocks).reshape((-1,) + (1,) * (len(dims) - dim - 1))

    level = one(*cuts[0])
    for cut in cuts[1:]:
        level = level * one(*cut)
    return level


def bell_draw(own_key, dims, deviation, most, cuts=(), kind=jnp.bfloat16):
    level = shard_levels(own_key, dims, cuts, -0.22, 0.18) if cuts else 1.0
    values = jax.random.normal(own_key, dims, jnp.float32) * deviation * level
    return jnp.minimum(jnp.maximum(values, -most), most).astype(kind)


def setup_inputs(seed: int = 0) -> dict:
    keys = jax.random.split(jax.random.key(seed), 15)
    return {
        "tokens": bell_draw(keys[0], (ROWS, ROW, D), 1.0, 6.0, ((0, 8), (1, 4))),
        "segments": draw_segments(jax.random.fold_in(keys[14], 71), 0),
        "buckets": draw_buckets(jax.random.fold_in(keys[14], 71), 0),
        "w_query": bell_draw(keys[3], (D, D), (4 * D) ** -0.5, 0.0625, ((0, 8),)),
        "w_key": bell_draw(keys[4], (D, D), (4 * D) ** -0.5, 0.0625, ((0, 8),)),
        "w_value": bell_draw(keys[5], (D, D), D ** -0.5, 0.125, ((0, 8),)),
        "w_attn_out": bell_draw(keys[6], (D, D), (D // 16) ** -0.5, 0.5, ((0, 8),)),
        "gain_attn": jnp.clip(1.0 + 0.15 * jax.random.normal(keys[7], (D,), jnp.float32), 0.25, 1.75).astype(jnp.bfloat16),
        "rel_table": bell_draw(keys[8], (H, NB), 1.0, 4.0, (), jnp.float32),
        "w_gate": bell_draw(keys[9], (D, FF), D ** -0.5, 0.125, ((0, 8),)),
        "w_up": bell_draw(keys[10], (D, FF), D ** -0.5, 0.125, ((0, 8),)),
        "w_down": bell_draw(keys[11], (D, FF), FF ** -0.5, 0.078125, ((0, 8),)),
        "gain_ffn": jnp.clip(1.0 + 0.15 * jax.random.normal(keys[12], (D,), jnp.float32), 0.25, 1.75).astype(jnp.bfloat16),
        "out_grad": bell_draw(keys[13], (ROWS, ROW, D), 1.0, 6.0, ((0, 8), (1, 4))),
    }


@jax.custom_vjp
def low(v):
    return lax.optimization_barrier(v.astype(jnp.bfloat16)).astype(jnp.float32)

@jax.custom_vjp
def low_back(v):
    return v

def low_keep(v):
    return (low(v), None)

def low_pass(kept, grad):
    return (grad,)

def back_keep(v):
    return (v, None)

def back_low(kept, grad):
    return (low(grad),)
low.defvjp(low_keep, low_pass)
low_back.defvjp(back_keep, back_low)
EPSILON = 1e-06
PRECISE = lax.Precision.HIGHEST
MASKED_SCORE = -1e+30

def matmul(left, right):
    return jnp.dot(left, right, precision=PRECISE)

def rms_norm(stream, gain):
    return stream * lax.rsqrt(lax.optimization_barrier(jnp.mean(stream * stream, axis=-1, keepdims=True)) + EPSILON) * gain

def attend_block(pieces, key_rows, value_rows, segment_row, bucket_list, table):
    query_block, segment_block, first_row = pieces
    row_length = segment_row.shape[0]
    block_rows = query_block.shape[0]
    offsets = jnp.arange(row_length, dtype=jnp.int32)[None, :] - (first_row + jnp.arange(block_rows, dtype=jnp.int32))[:, None] + (row_length - 1)
    relative = table[:, bucket_list[offsets]]
    scores = low_back(jnp.einsum('qhd,khd->hqk', query_block, key_rows, precision=PRECISE)) + relative
    allowed = segment_block[:, None] == segment_row[None, :]
    scores = jnp.where(allowed[None, :, :], scores, MASKED_SCORE)
    weights = low(jax.nn.softmax(scores, axis=-1))
    return jnp.einsum('hqk,khd->qhd', weights, value_rows, precision=PRECISE)

def attend_row(pieces, bucket_list, table):
    query_rows, key_rows, value_rows, segment_row = pieces
    row_length = segment_row.shape[0]
    block_rows = min(512, row_length)
    blocks = row_length // block_rows
    stepper = jax.checkpoint(partial(attend_block, key_rows=key_rows, value_rows=value_rows, segment_row=segment_row, bucket_list=bucket_list, table=table))
    starts = jnp.arange(blocks, dtype=jnp.int32) * block_rows
    context = lax.map(stepper, (query_rows.reshape(blocks, block_rows, H, DH), segment_row.reshape(blocks, block_rows), starts))
    return context.reshape(row_length, H, DH)

def forward(stream, query_w, key_w, value_w, output_w, attn_gain, table, gate_w, up_w, down_w, ffn_gain, segments, bucket_list):
    flat = stream.reshape(-1, D)
    attn_input = low(rms_norm(flat, attn_gain))
    queries = low_back(low(matmul(attn_input, query_w)))
    keys_all = low_back(low(matmul(attn_input, key_w)))
    values_all = low_back(low(matmul(attn_input, value_w)))
    head_shape = (ROWS, ROW, H, DH)
    context = lax.map(partial(attend_row, bucket_list=bucket_list, table=table), (queries.reshape(head_shape), keys_all.reshape(head_shape), values_all.reshape(head_shape), segments))
    context = low_back(low(context.reshape(-1, D)))
    attn_out = low_back(matmul(context, output_w.T))
    resid = flat + attn_out
    ffn_input = low(rms_norm(resid, ffn_gain))
    gate = low_back(matmul(ffn_input, gate_w))
    up_proj = low_back(matmul(ffn_input, up_w))
    hidden = low(jax.nn.gelu(gate, approximate=True) * up_proj)
    ff_out = low_back(matmul(hidden, down_w.T))
    result = resid + ff_out
    valid = (segments.reshape(-1) >= 0).astype(jnp.float32)
    valid_count = jnp.sum(valid)

    def root_mean(branch):
        return jnp.sqrt(jnp.sum(valid * lax.optimization_barrier(jnp.sum(branch * branch, axis=-1))) / (valid_count * D))
    stats = jnp.stack([root_mean(result), root_mean(attn_out), root_mean(ff_out)])
    return (result, stats)

def reference(tokens, segments, buckets, w_query, w_key, w_value, w_attn_out, gain_attn, rel_table, w_gate, w_up, w_down, gain_ffn, out_grad):

    def layer(stream, query_w, key_w, value_w, output_w, attn_gain, table, gate_w, up_w, down_w, ffn_gain):
        return forward(stream, query_w, key_w, value_w, output_w, attn_gain, table, gate_w, up_w, down_w, ffn_gain, segments, buckets)
    result, pull, stats = jax.vjp(layer, tokens.astype(jnp.float32), w_query.astype(jnp.float32), w_key.astype(jnp.float32), w_value.astype(jnp.float32), w_attn_out.astype(jnp.float32), gain_attn.astype(jnp.float32), rel_table.astype(jnp.float32), w_gate.astype(jnp.float32), w_up.astype(jnp.float32), w_down.astype(jnp.float32), gain_ffn.astype(jnp.float32), has_aux=True)
    grads = pull(out_grad.astype(jnp.float32).reshape(-1, D))
    layer_out = result.reshape(ROWS, ROW, D).astype(jnp.bfloat16)
    input_grad = grads[0].astype(jnp.bfloat16)
    return (layer_out, input_grad, grads[1], grads[2], grads[3], grads[4], grads[5], grads[6], grads[7], grads[8], grads[9], grads[10], stats)
```

```python
import functools

import jax
import jax.numpy as jnp
from jax import lax
from jax.experimental import pallas as pl
from jax.experimental.pallas import tpu as pltpu
from jax.sharding import PartitionSpec as P

DH = 64


EPSILON = 1e-06
PRECISE = lax.Precision.HIGHEST
MASKED_SCORE = -1e30
TILE = 128
PAIR = 2 * DH
VMEM_BYTES = 56 * 1024 * 1024


def rows_dot(left, right):
    return lax.dot_general(
        left, right, (((0,), (0,)), ((), ())), preferred_element_type=jnp.float32
    )


def cols_dot(left, right):
    return lax.dot_general(
        left, right, (((1,), (1,)), ((), ())), preferred_element_type=jnp.float32
    )


def norm_back(grad_hat, normed, scale):
    return scale * (grad_hat - normed * jnp.mean(grad_hat * normed, axis=-1, keepdims=True))


def gated_unit(gate, up_proj):
    return jax.nn.gelu(gate, approximate=True) * up_proj


def half_lanes(shape, which):
    lane = lax.broadcasted_iota(jnp.int32, shape, 1)
    return (lane < DH) if which == 0 else (lane >= DH)

def fold_rows(tile):
    return jnp.sum(tile.reshape(tile.shape[0] // 8, 8, tile.shape[1]), axis=0)

def forward_kernel(block, q_ref, k_ref, v_ref, row_ref, col_ref, bias_ref, ctx_ref, e_ref, inv_ref, strip_ref, score_ref):
    length = q_ref.shape[0]
    tiles = length // TILE
    width = 2 * length
    reach = length - TILE
    values_t = jnp.transpose(v_ref[...])
    for head in range(2):
        wide = jnp.broadcast_to(bias_ref[0, head : head + 1, :], (TILE, width))
        strip_ref[head] = pltpu.roll(wide, width - (TILE - 1), 1, stride=1, stride_axis=0)
    def one_block(index, carry):
        first = pl.multiple_of(index * block, block)
        q_block = q_ref[pl.ds(first, block), :]
        segment_q = row_ref[:, pl.ds(first, block)]
        outs = []
        for head in range(2):
            q_head = jnp.where(half_lanes(q_block.shape, head), q_block, jnp.zeros_like(q_block))
            raw = cols_dot(k_ref[...], q_head)
            highest = jnp.full((8, block), -jnp.inf, jnp.float32)
            for tile in range(tiles):
                bias = strip_ref[head, :, pl.ds(pl.multiple_of(first + (reach - TILE * tile), TILE), block)]
                segment_k = jnp.concatenate([col_ref[tile * TILE : (tile + 1) * TILE, :]] * (block // TILE), axis=1)
                score = jnp.where(segment_k == segment_q, raw[tile * TILE : (tile + 1) * TILE, :] + bias, MASKED_SCORE)
                score_ref[tile * TILE : (tile + 1) * TILE, :] = score
                highest = jnp.maximum(highest, jnp.max(score.reshape(TILE // 8, 8, block), axis=0))
            top = jnp.max(highest, axis=0, keepdims=True)
            total = jnp.zeros((8, block), jnp.float32)
            for tile in range(tiles):
                exponent = jnp.exp(score_ref[tile * TILE : (tile + 1) * TILE, :] - top)
                total = total + fold_rows(exponent)
                e_ref[head, tile * TILE : (tile + 1) * TILE, pl.ds(first, block)] = exponent.astype(jnp.bfloat16)
            inverse = 1.0 / jnp.sum(total, axis=0, keepdims=True)
            inv_ref[head, :, pl.ds(first, block)] = inverse
            context = jnp.dot(values_t[head * DH : (head + 1) * DH, :], e_ref[head, :, pl.ds(first, block)], preferred_element_type=jnp.float32)
            outs.append(context * inverse)
        ctx_ref[pl.ds(first, block), :] = jnp.transpose(jnp.concatenate(outs, axis=0)).astype(jnp.bfloat16)
        return carry
    lax.fori_loop(0, length // block, one_block, 0)

def attention_forward(q, k, v, segment_row, segment_wide, bias_line, heads, block):
    length = q.shape[0]
    pair = pl.BlockSpec((length, PAIR), lambda i: (0, i))
    return pl.pallas_call(
        functools.partial(forward_kernel, block),
        grid=(heads // 2,),
        in_specs=[pair, pair, pair,
                  pl.BlockSpec((1, length), lambda i: (0, 0)),
                  pl.BlockSpec((length, TILE), lambda i: (0, 0)),
                  pl.BlockSpec((1, 2, 2 * length), lambda i: (i, 0, 0))],
        out_specs=[pair,
                   pl.BlockSpec((2, length, length), lambda i: (i, 0, 0)),
                   pl.BlockSpec((2, 1, length), lambda i: (i, 0, 0))],
        out_shape=[jax.ShapeDtypeStruct((length, heads * DH), jnp.bfloat16),
                   jax.ShapeDtypeStruct((heads, length, length), jnp.bfloat16),
                   jax.ShapeDtypeStruct((heads, 1, length), jnp.float32)],
        scratch_shapes=[pltpu.VMEM((2, TILE, 2 * length), jnp.float32), pltpu.VMEM((length, block), jnp.float32)],
        compiler_params=pltpu.CompilerParams(vmem_limit_bytes=VMEM_BYTES),
        name="attention_forward",
    )(q, k, v, segment_row, segment_wide, bias_line)

def backward_kernel(block, q_ref, k_ref, v_ref, d_ref, e_ref, inv_ref, dq_ref, dk_ref, dv_ref, line_ref, strip_ref, prob_ref, low_ref, dk_sum, dv_sum):
    length = q_ref.shape[0]
    tiles = length // TILE
    width = 2 * length
    reach = length - TILE
    keys_t = jnp.transpose(k_ref[...])
    strip_ref[...] = jnp.zeros_like(strip_ref)
    dk_sum[...] = jnp.zeros_like(dk_sum)
    dv_sum[...] = jnp.zeros_like(dv_sum)
    def one_block(index, carry):
        first = pl.multiple_of(index * block, block)
        q_block = q_ref[pl.ds(first, block), :]
        d_block = d_ref[pl.ds(first, block), :]
        outs = []
        for head in range(2):
            mask = half_lanes(q_block.shape, head)
            q_head = jnp.where(mask, q_block, jnp.zeros_like(q_block))
            d_head = jnp.where(mask, d_block, jnp.zeros_like(d_block))
            prob_ref[...] = cols_dot(v_ref[...], d_head)
            total = jnp.zeros((8, block), jnp.float32)
            for tile in range(tiles):
                rows = slice(tile * TILE, (tile + 1) * TILE)
                total = total + fold_rows(e_ref[head, rows, pl.ds(first, block)].astype(jnp.float32) * prob_ref[rows, :])
            centre = jnp.sum(total, axis=0, keepdims=True) * inv_ref[head, :, pl.ds(first, block)]
            for tile in range(tiles):
                rows = slice(tile * TILE, (tile + 1) * TILE)
                grad = e_ref[head, rows, pl.ds(first, block)].astype(jnp.float32) * (prob_ref[rows, :] - centre)
                place = pl.ds(pl.multiple_of(first + (reach - TILE * tile), TILE), block)
                strip_ref[head, :, place] = strip_ref[head, :, place] + grad
                low_ref[rows, :] = grad.astype(jnp.bfloat16)
            dk_sum[...] += jnp.dot(low_ref[...], q_head, preferred_element_type=jnp.float32)
            dv_sum[...] += jnp.dot(e_ref[head, :, pl.ds(first, block)], d_head, preferred_element_type=jnp.float32)
            outs.append(jnp.dot(keys_t[head * DH : (head + 1) * DH, :], low_ref[...], preferred_element_type=jnp.float32))
        dq_ref[pl.ds(first, block), :] = jnp.transpose(jnp.concatenate(outs, axis=0)).astype(jnp.bfloat16)
        return carry
    lax.fori_loop(0, length // block, one_block, 0)
    dk_ref[...] = dk_sum[...].astype(jnp.bfloat16)
    dv_ref[...] = dv_sum[...].astype(jnp.bfloat16)
    for head in range(2):
        turned = strip_ref[head]
        while turned.shape[0] > 1:
            half = turned.shape[0] // 2
            turned = pltpu.roll(turned[:half], half, 1) + turned[half:]
        line_ref[0, head : head + 1, :] = turned

def attention_backward(q, k, v, d, e, inv, heads, block):
    length = q.shape[0]
    pair = pl.BlockSpec((length, PAIR), lambda i: (0, i))
    rows = jax.ShapeDtypeStruct((length, heads * DH), jnp.bfloat16)
    return pl.pallas_call(
        functools.partial(backward_kernel, block),
        grid=(heads // 2,),
        in_specs=[pair, pair, pair, pair,
                  pl.BlockSpec((2, length, length), lambda i: (i, 0, 0)),
                  pl.BlockSpec((2, 1, length), lambda i: (i, 0, 0))],
        out_specs=[pair, pair, pair, pl.BlockSpec((1, 2, 2 * length), lambda i: (i, 0, 0))],
        out_shape=[rows, rows, rows, jax.ShapeDtypeStruct((heads // 2, 2, 2 * length), jnp.float32)],
        scratch_shapes=[pltpu.VMEM((2, TILE, 2 * length), jnp.float32), pltpu.VMEM((length, block), jnp.float32),
                        pltpu.VMEM((length, block), jnp.bfloat16), pltpu.VMEM((length, PAIR), jnp.float32), pltpu.VMEM((length, PAIR), jnp.float32)],
        compiler_params=pltpu.CompilerParams(vmem_limit_bytes=VMEM_BYTES),
        name="attention_backward",
    )(q, k, v, d, e, inv)


def on_device(
    tokens,
    segments,
    buckets,
    w_query,
    w_key,
    w_value,
    w_attn_out,
    gain_attn,
    rel_table,
    w_gate,
    w_up,
    w_down,
    gain_ffn,
    out_grad,
):
    token_rows = tokens.shape[1]
    model_width = tokens.shape[2]
    ffn_width = w_gate.shape[1]
    segment_row = segments[0]
    row_length = segment_row.shape[0]
    block = min(256, row_length)
    seq_count = lax.axis_size("seq")
    fsdp_count = lax.axis_size("fsdp")
    seq_place = lax.axis_index("seq")
    fsdp_place = lax.axis_index("fsdp")
    head_count = model_width // seq_count // DH
    table_rows = jnp.pad(buckets[::-1], (0, 1), constant_values=-1)
    bucket_table = (
        table_rows[:, None] == jnp.arange(rel_table.shape[1], dtype=jnp.int32)[None, :]
    ).astype(jnp.float32)
    local_table = lax.dynamic_slice_in_dim(rel_table, seq_place * head_count, head_count, 0)
    bias_line = jnp.dot(local_table, jnp.transpose(bucket_table), precision=PRECISE)
    bias_line = bias_line.reshape(head_count // 2, 2, 2 * row_length)
    segment_wide = jnp.broadcast_to(segment_row[:, None], (row_length, TILE))
    stream = tokens[0].astype(jnp.float32)
    scale_attn = lax.rsqrt(jnp.mean(stream * stream, axis=-1, keepdims=True) + EPSILON)
    normed_attn = stream * scale_attn
    upstream = out_grad[0].astype(jnp.float32)
    ff_grad = upstream.astype(jnp.bfloat16)
    column_count = model_width // seq_count
    unit_count = ffn_width // seq_count

    def columns(weight, count):
        return lax.dynamic_slice_in_dim(weight, seq_place * count, count, 1)

    sliced = (
        lax.all_gather(gain_attn, "fsdp", axis=0, tiled=True),
        lax.all_gather(gain_ffn, "fsdp", axis=0, tiled=True),
        lax.all_gather(columns(w_query, column_count), "fsdp", axis=0, tiled=True),
        lax.all_gather(columns(w_key, column_count), "fsdp", axis=0, tiled=True),
        lax.all_gather(columns(w_value, column_count), "fsdp", axis=0, tiled=True),
        lax.all_gather(columns(w_attn_out, column_count), "fsdp", axis=0, tiled=True),
        lax.all_gather(columns(w_gate, unit_count), "fsdp", axis=0, tiled=True),
        lax.all_gather(columns(w_up, unit_count), "fsdp", axis=0, tiled=True),
        lax.all_gather(columns(w_down, unit_count), "fsdp", axis=0, tiled=True),
    )
    attn_gain, ffn_gain, query_w, key_w, value_w, output_w, gate_w, up_w, down_w = sliced

    def whole_row(piece):
        return lax.all_gather(piece, "seq", axis=0, tiled=True)

    def token_sum(term):
        return lax.psum_scatter(
            term(jnp.int32(0), lax.axis_size("seq") * token_rows),
            "seq",
            scatter_dimension=0,
            tiled=True,
        )

    attn_input = (normed_attn * attn_gain.astype(jnp.float32)).astype(jnp.bfloat16)
    attn_rows = whole_row(attn_input)
    query_rows = (
        jnp.dot(attn_rows, query_w, preferred_element_type=jnp.float32)
        .astype(jnp.bfloat16)
    )
    key_rows = (
        jnp.dot(attn_rows, key_w, preferred_element_type=jnp.float32)
        .astype(jnp.bfloat16)
    )
    value_rows = (
        jnp.dot(attn_rows, value_w, preferred_element_type=jnp.float32)
        .astype(jnp.bfloat16)
    )
    context, exponents, inverse = attention_forward(
        query_rows, key_rows, value_rows, segments, segment_wide, bias_line, head_count, block
    )

    def attn_term(first_row, row_count):
        return cols_dot(context, output_w)

    attn_out = token_sum(attn_term)
    resid = stream + attn_out
    scale_ffn = lax.rsqrt(jnp.mean(resid * resid, axis=-1, keepdims=True) + EPSILON)
    normed_ffn = resid * scale_ffn
    ffn_input = (normed_ffn * ffn_gain.astype(jnp.float32)).astype(jnp.bfloat16)
    ffn_rows = whole_row(ffn_input)
    gate = jnp.dot(ffn_rows, gate_w, preferred_element_type=jnp.float32)
    up_proj = jnp.dot(ffn_rows, up_w, preferred_element_type=jnp.float32)
    hidden = gated_unit(gate, up_proj).astype(jnp.bfloat16)

    def down_term(first_row, row_count):
        return cols_dot(hidden, down_w)

    ff_out = token_sum(down_term)
    result = resid + ff_out
    ff_grad_rows = whole_row(ff_grad)
    hidden_grad = jnp.dot(ff_grad_rows, down_w, preferred_element_type=jnp.float32)
    unused, pull = jax.vjp(gated_unit, gate, up_proj)
    gate_grad, up_grad = pull(hidden_grad)
    gate_grad = gate_grad.astype(jnp.bfloat16)
    up_grad = up_grad.astype(jnp.bfloat16)

    def pair_term(first_row, row_count):
        return cols_dot(gate_grad, gate_w) + cols_dot(up_grad, up_w)

    ffn_in_grad = token_sum(pair_term)
    gain_ffn_part = jnp.sum(ffn_in_grad * normed_ffn, axis=0)
    resid_grad = upstream + norm_back(
        ffn_in_grad * ffn_gain.astype(jnp.float32), normed_ffn, scale_ffn
    )
    attn_grad = resid_grad.astype(jnp.bfloat16)
    attn_grad_rows = whole_row(attn_grad)
    inverse_rows = jnp.repeat(jnp.transpose(inverse[:, 0, :]), DH, axis=1)
    context_grad = (
        jnp.dot(attn_grad_rows, output_w, preferred_element_type=jnp.float32) * inverse_rows
    ).astype(jnp.bfloat16)
    query_back, key_back, value_back, line_grad = attention_backward(
        query_rows, key_rows, value_rows, context_grad, exponents, inverse, head_count, block
    )

    def triple_term(first_row, row_count):
        return (
            cols_dot(query_back, query_w)
            + cols_dot(key_back, key_w)
            + cols_dot(value_back, value_w)
        )

    attn_in_grad = token_sum(triple_term)
    gain_attn_part = jnp.sum(attn_in_grad * normed_attn, axis=0)
    stream_grad = resid_grad + norm_back(
        attn_in_grad * attn_gain.astype(jnp.float32), normed_attn, scale_attn
    )
    owned = lax.psum_scatter(
        jnp.concatenate(
            [
                rows_dot(attn_rows, query_back),
                rows_dot(attn_rows, key_back),
                rows_dot(attn_rows, value_back),
                rows_dot(attn_grad_rows, context),
                rows_dot(ffn_rows, gate_grad),
                rows_dot(ffn_rows, up_grad),
                rows_dot(ff_grad_rows, hidden),
            ],
            axis=1,
        ).astype(jnp.bfloat16),
        "fsdp",
        scatter_dimension=0,
        tiled=True,
    ).astype(jnp.float32)
    widths = [column_count] * 4 + [unit_count] * 3
    edges = [0]
    for width in widths:
        edges.append(edges[-1] + width)
    pieces = tuple((owned[:, edges[place] : edges[place + 1]] for place in range(7)))
    gathered = (
        lax.all_gather(pieces[0].astype(jnp.bfloat16), "seq", axis=1, tiled=True).astype(
            jnp.float32
        ),
        lax.all_gather(pieces[1].astype(jnp.bfloat16), "seq", axis=1, tiled=True).astype(
            jnp.float32
        ),
        lax.all_gather(pieces[2].astype(jnp.bfloat16), "seq", axis=1, tiled=True).astype(
            jnp.float32
        ),
        lax.all_gather(pieces[3].astype(jnp.bfloat16), "seq", axis=1, tiled=True).astype(
            jnp.float32
        ),
        lax.all_gather(pieces[4].astype(jnp.bfloat16), "seq", axis=1, tiled=True).astype(
            jnp.float32
        ),
        lax.all_gather(pieces[5].astype(jnp.bfloat16), "seq", axis=1, tiled=True).astype(
            jnp.float32
        ),
        lax.all_gather(pieces[6].astype(jnp.bfloat16), "seq", axis=1, tiled=True).astype(
            jnp.float32
        ),
    )
    weight_grads = list(gathered)
    own_segments = lax.dynamic_slice_in_dim(segment_row, seq_place * token_rows, token_rows, 0)
    valid = (own_segments >= 0).astype(jnp.float32)
    stat_terms = jnp.stack(
        [
            jnp.sum(valid * jnp.sum(result * result, axis=-1)),
            jnp.sum(valid * jnp.sum(attn_out * attn_out, axis=-1)),
            jnp.sum(valid * jnp.sum(ff_out * ff_out, axis=-1)),
            jnp.sum(valid),
        ]
    )
    table_part = jnp.dot(
        line_grad.reshape(head_count, 2 * row_length), bucket_table, precision=PRECISE
    )
    full_table = lax.dynamic_update_slice_in_dim(
        jnp.zeros(rel_table.shape, jnp.float32), table_part, seq_place * head_count, 0
    )
    summed = lax.psum((gain_attn_part, gain_ffn_part, full_table, stat_terms), ("fsdp", "seq"))
    stat_totals = summed[3]
    rms_stats = jnp.sqrt(stat_totals[0:3] / (stat_totals[3] * model_width))
    gain_rows = model_width // fsdp_count
    table_rows = rel_table.shape[0] // fsdp_count
    gain_attn_grad = lax.dynamic_slice_in_dim(summed[0], fsdp_place * gain_rows, gain_rows, 0)
    gain_ffn_grad = lax.dynamic_slice_in_dim(summed[1], fsdp_place * gain_rows, gain_rows, 0)
    rel_table_grad = lax.dynamic_slice_in_dim(summed[2], fsdp_place * table_rows, table_rows, 0)
    return (
        result.astype(jnp.bfloat16)[None],
        stream_grad.astype(jnp.bfloat16)[None],
        weight_grads[0],
        weight_grads[1],
        weight_grads[2],
        weight_grads[3],
        gain_attn_grad,
        rel_table_grad,
        weight_grads[4],
        weight_grads[5],
        weight_grads[6],
        gain_ffn_grad,
        rms_stats,
    )


def solution(mesh):
    in_specs = (
        P("fsdp", "seq", None),
        P("fsdp", None),
        P(),
        P("fsdp", None),
        P("fsdp", None),
        P("fsdp", None),
        P("fsdp", None),
        P("fsdp"),
        P(),
        P("fsdp", None),
        P("fsdp", None),
        P("fsdp", None),
        P("fsdp"),
        P("fsdp", "seq", None),
    )
    out_specs = (
        P("fsdp", "seq", None),
        P("fsdp", "seq", None),
        P("fsdp", None),
        P("fsdp", None),
        P("fsdp", None),
        P("fsdp", None),
        P("fsdp"),
        P("fsdp", None),
        P("fsdp", None),
        P("fsdp", None),
        P("fsdp", None),
        P("fsdp"),
        P(),
    )
    return jax.shard_map(
        on_device, mesh=mesh, in_specs=in_specs, out_specs=out_specs, check_vma=False
    )
```

```python
import functools

import jax
import jax.numpy as jnp
from jax import lax
from jax.experimental import pallas as pl
from jax.experimental.pallas import tpu as pltpu
from jax.sharding import PartitionSpec as P

DH = 64


EPSILON = 1e-06
PRECISE = lax.Precision.HIGHEST
MASKED_SCORE = -1e30
TILE = 128
PAIR = 2 * DH
GELU_SCALE = 0.7978845608
GELU_CUBE = 0.044715
VMEM_BYTES = 56 * 1024 * 1024


def rows_dot(left, right):
    return lax.dot_general(
        left, right, (((0,), (0,)), ((), ())), preferred_element_type=jnp.float32
    )


def cols_dot(left, right):
    return lax.dot_general(
        left, right, (((1,), (1,)), ((), ())), preferred_element_type=jnp.float32
    )


def norm_back(grad_hat, normed, scale):
    return scale * (grad_hat - normed * jnp.mean(grad_hat * normed, axis=-1, keepdims=True))


def half_lanes(shape, which):
    lane = lax.broadcasted_iota(jnp.int32, shape, 1)
    return (lane < DH) if which == 0 else (lane >= DH)


def fold_rows(tile):
    return jnp.sum(tile.reshape(tile.shape[0] // 8, 8, tile.shape[1]), axis=0)


def whole_place(row, token_rows, place):
    return jnp.bitwise_xor(row // token_rows, place) * token_rows + row % token_rows


def forward_kernel(
    block,
    token_rows,
    place_ref,
    qkv_ref,
    row_ref,
    col_ref,
    bias_ref,
    ctx_ref,
    e_ref,
    inv_ref,
    strip_ref,
    score_ref,
):
    length = qkv_ref.shape[0]
    q_ref = qkv_ref.at[:, :PAIR]
    k_ref = qkv_ref.at[:, PAIR : 2 * PAIR]
    v_ref = qkv_ref.at[:, 2 * PAIR :]
    tiles = length // TILE
    width = 2 * length
    reach = length - TILE
    place = place_ref[0]
    key_places = [
        pl.multiple_of(whole_place(tile * TILE, token_rows, place), TILE) for tile in range(tiles)
    ]
    values_t = jnp.transpose(v_ref[...])
    for head in range(2):
        wide = jnp.broadcast_to(bias_ref[0, head : head + 1, :], (TILE, width))
        strip_ref[head] = pltpu.roll(wide, width - (TILE - 1), 1, stride=1, stride_axis=0)

    def one_block(index, carry):
        first = pl.multiple_of(index * block, block)
        query_place = pl.multiple_of(whole_place(first, token_rows, place), block)
        q_block = q_ref[pl.ds(first, block), :]
        segment_q = row_ref[:, pl.ds(query_place, block)]
        outs = []
        for head in range(2):
            q_head = jnp.where(half_lanes(q_block.shape, head), q_block, jnp.zeros_like(q_block))
            raw = cols_dot(k_ref[...], q_head)
            highest = jnp.full((8, block), -jnp.inf, jnp.float32)
            for tile in range(tiles):
                rows = slice(tile * TILE, (tile + 1) * TILE)
                offset = pl.multiple_of(query_place + (reach - key_places[tile]), TILE)
                bias = strip_ref[head, :, pl.ds(offset, block)]
                segment_k = col_ref[pl.ds(key_places[tile], TILE), :]
                segment_k = jnp.concatenate([segment_k] * (block // TILE), axis=1)
                score = jnp.where(segment_k == segment_q, raw[rows, :] + bias, MASKED_SCORE)
                score_ref[rows, :] = score
                highest = jnp.maximum(
                    highest, jnp.max(score.reshape(TILE // 8, 8, block), axis=0)
                )
            top = jnp.max(highest, axis=0, keepdims=True)
            total = jnp.zeros((8, block), jnp.float32)
            for tile in range(tiles):
                rows = slice(tile * TILE, (tile + 1) * TILE)
                exponent = jnp.exp(score_ref[rows, :] - top)
                total = total + fold_rows(exponent)
                e_ref[head, rows, pl.ds(first, block)] = exponent.astype(jnp.bfloat16)
            inverse = 1.0 / jnp.sum(total, axis=0, keepdims=True)
            inv_ref[head, :, pl.ds(first, block)] = inverse
            context = jnp.dot(
                values_t[head * DH : (head + 1) * DH, :],
                e_ref[head, :, pl.ds(first, block)],
                preferred_element_type=jnp.float32,
            )
            outs.append(context * inverse)
        ctx_ref[pl.ds(first, block), :] = jnp.transpose(jnp.concatenate(outs, axis=0)).astype(
            jnp.bfloat16
        )
        return carry

    lax.fori_loop(0, length // block, one_block, 0)


def attention_forward(qkv, place, segment_row, segment_wide, bias_line, heads, token_rows):
    length = qkv.shape[0]
    block = min(256, token_rows)
    pairs = heads // 2
    return pl.pallas_call(
        functools.partial(forward_kernel, block, token_rows),
        grid=(pairs,),
        in_specs=[
            pl.BlockSpec(memory_space=pltpu.SMEM),
            pl.BlockSpec((length, 3 * PAIR), lambda i: (0, i)),
            pl.BlockSpec((1, length), lambda i: (0, 0)),
            pl.BlockSpec((length, TILE), lambda i: (0, 0)),
            pl.BlockSpec((1, 2, 2 * length), lambda i: (i, 0, 0)),
        ],
        out_specs=[
            pl.BlockSpec((length, PAIR), lambda i: (0, i)),
            pl.BlockSpec((2, length, length), lambda i: (i, 0, 0)),
            pl.BlockSpec((2, 1, length), lambda i: (i, 0, 0)),
        ],
        out_shape=[
            jax.ShapeDtypeStruct((length, heads * DH), jnp.bfloat16),
            jax.ShapeDtypeStruct((heads, length, length), jnp.bfloat16),
            jax.ShapeDtypeStruct((heads, 1, length), jnp.float32),
        ],
        scratch_shapes=[
            pltpu.VMEM((2, TILE, 2 * length), jnp.float32),
            pltpu.VMEM((length, block), jnp.float32),
        ],
        compiler_params=pltpu.CompilerParams(vmem_limit_bytes=VMEM_BYTES),
        cost_estimate=pl.CostEstimate(
            flops=16 * heads * length * length * DH,
            bytes_accessed=2 * heads * length * length,
            transcendentals=heads * length * length,
        ),
        name="attention_forward",
    )(place, qkv, segment_row, segment_wide, bias_line)


def backward_kernel(
    block,
    token_rows,
    place_ref,
    qkv_ref,
    d_ref,
    e_ref,
    inv_ref,
    grad_ref,
    line_ref,
    strip_ref,
    prob_ref,
    low_ref,
    dk_sum,
    dv_sum,
):
    length = qkv_ref.shape[0]
    q_ref = qkv_ref.at[:, :PAIR]
    k_ref = qkv_ref.at[:, PAIR : 2 * PAIR]
    v_ref = qkv_ref.at[:, 2 * PAIR :]
    tiles = length // TILE
    reach = length - TILE
    place = place_ref[0]
    key_places = [whole_place(tile * TILE, token_rows, place) for tile in range(tiles)]
    keys_t = jnp.transpose(k_ref[...])
    strip_ref[...] = jnp.zeros_like(strip_ref)
    dk_sum[...] = jnp.zeros_like(dk_sum)
    dv_sum[...] = jnp.zeros_like(dv_sum)

    def one_block(index, carry):
        first = pl.multiple_of(index * block, block)
        query_place = whole_place(first, token_rows, place)
        q_block = q_ref[pl.ds(first, block), :]
        d_block = d_ref[pl.ds(first, block), :]
        outs = []
        for head in range(2):
            mask = half_lanes(q_block.shape, head)
            q_head = jnp.where(mask, q_block, jnp.zeros_like(q_block))
            inverse = inv_ref[head, :, pl.ds(first, block)]
            scale = jnp.transpose(jnp.broadcast_to(inverse, (PAIR, block)))
            d_head = jnp.where(mask, d_block.astype(jnp.float32) * scale, 0.0)
            d_head = d_head.astype(jnp.bfloat16)
            prob_ref[...] = cols_dot(v_ref[...], d_head)
            total = jnp.zeros((8, block), jnp.float32)
            for tile in range(tiles):
                rows = slice(tile * TILE, (tile + 1) * TILE)
                exponent = e_ref[head, rows, pl.ds(first, block)].astype(jnp.float32)
                total = total + fold_rows(exponent * prob_ref[rows, :])
            centre = jnp.sum(total, axis=0, keepdims=True) * inverse
            for tile in range(tiles):
                rows = slice(tile * TILE, (tile + 1) * TILE)
                exponent = e_ref[head, rows, pl.ds(first, block)].astype(jnp.float32)
                grad = exponent * (prob_ref[rows, :] - centre)
                offset = pl.multiple_of(query_place + (reach - key_places[tile]), TILE)
                at = pl.ds(offset, block)
                strip_ref[head, :, at] = strip_ref[head, :, at] + grad
                low_ref[rows, :] = grad.astype(jnp.bfloat16)
            dk_sum[...] += jnp.dot(low_ref[...], q_head, preferred_element_type=jnp.float32)
            dv_sum[...] += jnp.dot(
                e_ref[head, :, pl.ds(first, block)], d_head, preferred_element_type=jnp.float32
            )
            outs.append(
                jnp.dot(
                    keys_t[head * DH : (head + 1) * DH, :],
                    low_ref[...],
                    preferred_element_type=jnp.float32,
                )
            )
        grad_ref[pl.ds(first, block), :PAIR] = jnp.transpose(jnp.concatenate(outs, axis=0)).astype(
            jnp.bfloat16
        )
        return carry

    lax.fori_loop(0, length // block, one_block, 0)
    grad_ref[:, PAIR : 2 * PAIR] = dk_sum[...].astype(jnp.bfloat16)
    grad_ref[:, 2 * PAIR :] = dv_sum[...].astype(jnp.bfloat16)
    for head in range(2):
        turned = strip_ref[head]
        while turned.shape[0] > 1:
            half = turned.shape[0] // 2
            turned = pltpu.roll(turned[:half], half, 1) + turned[half:]
        line_ref[0, head : head + 1, :] = turned


def attention_backward(qkv, place, d, e, inv, heads, token_rows):
    length = qkv.shape[0]
    block = min(256, token_rows)
    pairs = heads // 2
    triple = pl.BlockSpec((length, 3 * PAIR), lambda i: (0, i))
    return pl.pallas_call(
        functools.partial(backward_kernel, block, token_rows),
        grid=(pairs,),
        in_specs=[
            pl.BlockSpec(memory_space=pltpu.SMEM),
            triple,
            pl.BlockSpec((length, PAIR), lambda i: (0, i)),
            pl.BlockSpec((2, length, length), lambda i: (i, 0, 0)),
            pl.BlockSpec((2, 1, length), lambda i: (i, 0, 0)),
        ],
        out_specs=[triple, pl.BlockSpec((1, 2, 2 * length), lambda i: (i, 0, 0))],
        out_shape=[
            jax.ShapeDtypeStruct((length, 3 * heads * DH), jnp.bfloat16),
            jax.ShapeDtypeStruct((pairs, 2, 2 * length), jnp.float32),
        ],
        scratch_shapes=[
            pltpu.VMEM((2, TILE, 2 * length), jnp.float32),
            pltpu.VMEM((length, block), jnp.float32),
            pltpu.VMEM((length, block), jnp.bfloat16),
            pltpu.VMEM((length, PAIR), jnp.float32),
            pltpu.VMEM((length, PAIR), jnp.float32),
        ],
        compiler_params=pltpu.CompilerParams(vmem_limit_bytes=VMEM_BYTES),
        cost_estimate=pl.CostEstimate(
            flops=40 * heads * length * length * DH,
            bytes_accessed=2 * heads * length * length,
            transcendentals=0,
        ),
        name="attention_backward",
    )(place, qkv, d, e, inv)


def swap(piece, axis, step):
    return lax.ppermute(piece, axis, [(i, i ^ step) for i in range(lax.axis_size(axis))])


def gather_pieces(piece, relay=True):
    count = lax.axis_size("seq")
    if count != 4 or not relay:
        return [[piece]] + [[swap(piece, "seq", step)] for step in range(1, count)]
    half = piece.shape[0] // 2
    first = swap(piece, "seq", 1)
    second = swap(piece, "seq", 2)
    third_upper = swap(second[:half], "seq", 1)
    third_lower = swap(first[half:], "seq", 2)
    return [[piece], [first], [second], [third_upper, third_lower]]


def gather_rows(piece):
    return jnp.concatenate([part for parts in gather_pieces(piece) for part in parts], axis=0)


def scatter_terms(rows, weights):
    size = rows.shape[0] // lax.axis_size("seq")
    return cols_dot(rows[size:], weights).astype(jnp.bfloat16)


def scatter_begin(terms):
    count = lax.axis_size("seq")
    size = terms.shape[0] // (count - 1)
    if count != 4:
        return tuple(
            swap(terms[k * size : (k + 1) * size], "seq", k + 1) for k in range(count - 1)
        )
    upper = swap(terms[2 * size : 2 * size + size // 2], "seq", 1)
    lower = swap(terms[2 * size + size // 2 :], "seq", 2)
    return upper, lower


def scatter_add(terms, received):
    if lax.axis_size("seq") != 4:
        return received
    size = terms.shape[0] // 3
    upper, lower = (part.astype(jnp.float32) for part in received)
    first = terms[:size].astype(jnp.float32) + jnp.pad(lower, ((size // 2, 0), (0, 0)))
    second = terms[size : 2 * size].astype(jnp.float32) + jnp.pad(upper, ((0, size // 2), (0, 0)))
    return first.astype(jnp.bfloat16), second.astype(jnp.bfloat16)


def scatter_end(sums):
    if lax.axis_size("seq") != 4:
        return sums
    return swap(sums[0], "seq", 1), swap(sums[1], "seq", 2)


def scatter_own(rows, weights, received):
    own = cols_dot(rows[: rows.shape[0] // lax.axis_size("seq")], weights)
    return own + sum(part.astype(jnp.float32) for part in received)


def scatter_sum(rows, weights):
    terms = scatter_terms(rows, weights)
    return scatter_own(rows, weights, scatter_end(scatter_add(terms, scatter_begin(terms))))


def total_sum(values, axis):
    count = lax.axis_size(axis)
    level = [values] + [swap(values, axis, step) for step in range(1, count)]
    while len(level) > 1:
        level = [level[i] + level[i + 1] for i in range(0, len(level), 2)]
    return level[0]


def feed_forward_kernel(tile, x_ref, w_ref, act_ref, gelu_ref, slope_ref):
    rows = x_ref.shape[0]
    chunk = min(512, rows)
    for start in range(0, rows, chunk):
        at = slice(start, start + chunk)
        both = jnp.dot(x_ref[at, :], w_ref[...], preferred_element_type=jnp.float32)
        gate, up = both[:, :tile], both[:, tile:]
        square = gate * gate
        tanh = jnp.tanh(GELU_SCALE * gate * (1.0 + GELU_CUBE * square))
        half_up = 0.5 * (1.0 + tanh)
        gelu = gate * half_up
        bend = 0.5 * GELU_SCALE * gate * (1.0 - tanh * tanh) * (1.0 + 3.0 * GELU_CUBE * square)
        act_ref[at, :] = (gelu * up).astype(jnp.bfloat16)
        gelu_ref[at, :] = gelu.astype(jnp.bfloat16)
        slope_ref[at, :] = (up * (half_up + bend)).astype(jnp.bfloat16)


def feed_forward(rows, weights, tile):
    length, model_width = rows.shape
    units = weights.shape[1] // 2
    block = pl.BlockSpec((length, tile), lambda j: (0, j))
    return pl.pallas_call(
        functools.partial(feed_forward_kernel, tile),
        grid=(units // tile,),
        in_specs=[
            pl.BlockSpec((length, model_width), lambda j: (0, 0)),
            pl.BlockSpec((model_width, 2 * tile), lambda j: (0, j)),
        ],
        out_specs=[block, block, block],
        out_shape=[
            jax.ShapeDtypeStruct((length, units), jnp.bfloat16),
            jax.ShapeDtypeStruct((length, units), jnp.bfloat16),
            jax.ShapeDtypeStruct((length, units), jnp.bfloat16),
        ],
        compiler_params=pltpu.CompilerParams(vmem_limit_bytes=VMEM_BYTES),
        cost_estimate=pl.CostEstimate(
            flops=4 * length * model_width * units,
            bytes_accessed=4 * model_width * units + 10 * length * units,
            transcendentals=length * units,
        ),
        name="feed_forward",
    )(rows, weights)


def feed_forward_back_kernel(tile, d_ref, w_ref, gelu_ref, slope_ref, grad_ref):
    rows = d_ref.shape[0]
    chunk = min(512, rows)
    for start in range(0, rows, chunk):
        at = slice(start, start + chunk)
        grad = jnp.dot(d_ref[at, :], w_ref[...], preferred_element_type=jnp.float32)
        grad_ref[at, :tile] = (grad * slope_ref[at, :].astype(jnp.float32)).astype(jnp.bfloat16)
        grad_ref[at, tile:] = (grad * gelu_ref[at, :].astype(jnp.float32)).astype(jnp.bfloat16)


def feed_forward_back(grad_rows, weights, gelu, slope, tile):
    length, model_width = grad_rows.shape
    units = weights.shape[1]
    block = pl.BlockSpec((length, tile), lambda j: (0, j))
    return pl.pallas_call(
        functools.partial(feed_forward_back_kernel, tile),
        grid=(units // tile,),
        in_specs=[
            pl.BlockSpec((length, model_width), lambda j: (0, 0)),
            pl.BlockSpec((model_width, tile), lambda j: (0, j)),
            block,
            block,
        ],
        out_specs=pl.BlockSpec((length, 2 * tile), lambda j: (0, j)),
        out_shape=jax.ShapeDtypeStruct((length, 2 * units), jnp.bfloat16),
        compiler_params=pltpu.CompilerParams(vmem_limit_bytes=VMEM_BYTES),
        cost_estimate=pl.CostEstimate(
            flops=2 * length * model_width * units,
            bytes_accessed=2 * model_width * units + 12 * length * units,
            transcendentals=0,
        ),
        name="feed_forward_back",
    )(grad_rows, weights, gelu, slope)


def place_kernel(moves, count, widths, place_ref, *refs):
    pieces, outs = refs[:count], refs[count:]
    for step in range(count):
        owner = jnp.bitwise_xor(place_ref[0], step)
        for out, source, target, size in moves:
            at = pl.multiple_of(owner * widths[out] + target, TILE)
            block = pieces[step][:, source : source + size]
            outs[out][:, pl.ds(at, size)] = block.astype(jnp.float32)


def place_columns(parts, place, moves, widths):
    pieces = [part[0] if len(part) == 1 else jnp.concatenate(part, axis=0) for part in parts]
    count = len(pieces)
    rows, width = pieces[0].shape
    block = min(64, rows)
    return pl.pallas_call(
        functools.partial(place_kernel, moves, count, widths),
        grid=(rows // block,),
        in_specs=[pl.BlockSpec(memory_space=pltpu.SMEM)]
        + [pl.BlockSpec((block, width), lambda i: (i, 0))] * count,
        out_specs=[pl.BlockSpec((block, count * size), lambda i: (i, 0)) for size in widths],
        out_shape=[jax.ShapeDtypeStruct((rows, count * size), jnp.float32) for size in widths],
        compiler_params=pltpu.CompilerParams(vmem_limit_bytes=VMEM_BYTES),
        cost_estimate=pl.CostEstimate(
            flops=0, bytes_accessed=6 * rows * count * width, transcendentals=0
        ),
        name="place_columns",
    )(place, *pieces)


def take_kernel(moves, count, place_ref, *refs):
    out_ref = refs[count]
    for which, source, target, size in moves:
        out_ref[:, source : source + size] = refs[which][:, target : target + size]


def take_columns(place, weights, moves, counts):
    rows = weights[0].shape[0]
    block = min(64, rows)
    width = sum(counts)

    def chosen(count):
        return pl.BlockSpec((block, count), lambda i, place_ref: (i, place_ref[0]))

    return pl.pallas_call(
        functools.partial(take_kernel, moves, len(weights)),
        grid_spec=pltpu.PrefetchScalarGridSpec(
            num_scalar_prefetch=1,
            grid=(rows // block,),
            in_specs=[chosen(count) for count in counts],
            out_specs=pl.BlockSpec((block, width), lambda i, place_ref: (i, 0)),
        ),
        out_shape=jax.ShapeDtypeStruct((rows, width), weights[0].dtype),
        compiler_params=pltpu.CompilerParams(vmem_limit_bytes=VMEM_BYTES),
        cost_estimate=pl.CostEstimate(flops=0, bytes_accessed=4 * rows * width, transcendentals=0),
        name="take_columns",
    )(place, *weights)


def split_kernel(core_ref, own_in, other_in, own_ref, other_ref):
    own_ref[...] = own_in[...]
    other_ref[...] = other_in[...]


def split_columns(rows, core, groups):
    length, width = rows.shape
    size = width // groups

    def chosen(side):
        return pl.BlockSpec(
            (length, size), lambda i, core_ref: (0, 2 * i + jnp.bitwise_xor(core_ref[0], side))
        )

    half = jax.ShapeDtypeStruct((length, width // 2), rows.dtype)
    block = pl.BlockSpec((length, size), lambda i, core_ref: (0, i))
    return pl.pallas_call(
        split_kernel,
        grid_spec=pltpu.PrefetchScalarGridSpec(
            num_scalar_prefetch=1,
            grid=(groups // 2,),
            in_specs=[chosen(0), chosen(1)],
            out_specs=[block, block],
        ),
        out_shape=[half, half],
        compiler_params=pltpu.CompilerParams(vmem_limit_bytes=VMEM_BYTES),
        cost_estimate=pl.CostEstimate(flops=0, bytes_accessed=4 * length * width, transcendentals=0),
        name="split_columns",
    )(core, rows, rows)


def both(*values):
    return lax.optimization_barrier(values)


def add_low(sums, added):
    return (sums + added.astype(jnp.float32)).astype(jnp.bfloat16)


def on_device(
    tokens,
    segments,
    buckets,
    w_query,
    w_key,
    w_value,
    w_attn_out,
    gain_attn,
    rel_table,
    w_gate,
    w_up,
    w_down,
    gain_ffn,
    out_grad,
):
    token_rows = tokens.shape[1]
    model_width = tokens.shape[2]
    ffn_width = w_gate.shape[1]
    segment_row = segments[0]
    row_length = segment_row.shape[0]
    seq_count = lax.axis_size("seq")
    fsdp_count = lax.axis_size("fsdp")
    seq_place = lax.axis_index("seq")
    fsdp_place = lax.axis_index("fsdp")
    place = seq_place.astype(jnp.int32).reshape(1)
    head_count = model_width // seq_count // DH
    column_count = model_width // seq_count
    unit_count = ffn_width // seq_count

    tile = 256 if unit_count % 256 == 0 else 128
    pairs = head_count // 2

    def gather_weights(piece):
        return lax.all_gather(piece, "fsdp", axis=0, tiled=True)

    qkv_moves = [
        (which, (3 * pair + which) * PAIR, pair * PAIR, PAIR)
        for pair in range(pairs)
        for which in range(3)
    ] + [(3, 3 * column_count, 0, column_count)]
    unit_moves = [
        (which, (2 * block + which) * tile, block * tile, tile)
        for block in range(unit_count // tile)
        for which in range(2)
    ]
    attn_part = take_columns(
        place, (w_query, w_key, w_value, w_attn_out), qkv_moves, [column_count] * 4
    )
    attn_w = gather_weights(attn_part)
    gains = lax.all_gather(jnp.stack([gain_attn, gain_ffn]), "fsdp", axis=1, tiled=True)
    attn_gain = gains[0].astype(jnp.float32)
    ffn_gain = gains[1].astype(jnp.float32)
    qkv_w = attn_w[:, : 3 * column_count]
    output_w = attn_w[:, 3 * column_count :]

    table_rows = jnp.pad(buckets[::-1], (0, 1), constant_values=-1)
    bucket_table = (
        table_rows[:, None] == jnp.arange(rel_table.shape[1], dtype=jnp.int32)[None, :]
    ).astype(jnp.float32)
    local_table = lax.dynamic_slice_in_dim(rel_table, seq_place * head_count, head_count, 0)
    bias_line = jnp.dot(local_table, jnp.transpose(bucket_table), precision=PRECISE)
    bias_line = bias_line.reshape(head_count // 2, 2, 2 * row_length)
    segment_wide = jnp.broadcast_to(segment_row[:, None], (row_length, TILE))

    stream = tokens[0].astype(jnp.float32)
    scale_attn = lax.rsqrt(jnp.mean(stream * stream, axis=-1, keepdims=True) + EPSILON)
    normed_attn = stream * scale_attn
    upstream = out_grad[0].astype(jnp.float32)

    stream_rows = gather_rows(tokens[0])
    gate_up_part = take_columns(place, (w_gate, w_up), unit_moves, [unit_count] * 2)
    gate_up_part, stream_rows = both(gate_up_part, stream_rows)
    gate_up_w = gather_weights(gate_up_part)
    stream_rows = stream_rows.astype(jnp.float32)
    rows_scale = lax.rsqrt(jnp.mean(stream_rows * stream_rows, axis=-1, keepdims=True) + EPSILON)
    attn_rows = (stream_rows * rows_scale * attn_gain).astype(jnp.bfloat16)
    ff_grad_rows = gather_rows(out_grad[0])
    attn_rows, ff_grad_rows = both(attn_rows, ff_grad_rows)

    qkv = jnp.dot(attn_rows, qkv_w, preferred_element_type=jnp.float32).astype(jnp.bfloat16)
    down_part, qkv = both(
        lax.dynamic_slice_in_dim(w_down, seq_place * unit_count, unit_count, 1), qkv
    )
    down_w = gather_weights(down_part)
    context, exponents, inverse = attention_forward(
        qkv, place, segments, segment_wide, bias_line, head_count, token_rows
    )

    attn_out = scatter_sum(context, output_w)
    chips = fsdp_count // 2
    core = (fsdp_place % 2).astype(jnp.int32).reshape(1)
    groups = [[2 * chip + side for chip in range(chips)] for side in range(2)]

    def scatter_grads(grads, axis_index_groups=None):
        return lax.psum_scatter(
            grads,
            "fsdp",
            scatter_dimension=0,
            tiled=True,
            axis_index_groups=axis_index_groups,
        )

    ff_grad_own, ff_grad_other = split_columns(ff_grad_rows, core, fsdp_count)
    ff_grad_own, ff_grad_other, attn_out = both(ff_grad_own, ff_grad_other, attn_out)
    resid = stream + attn_out
    scale_ffn = lax.rsqrt(jnp.mean(resid * resid, axis=-1, keepdims=True) + EPSILON)
    normed_ffn = resid * scale_ffn
    ffn_rows = gather_rows((normed_ffn * ffn_gain).astype(jnp.bfloat16))

    hidden, gelu, slope = feed_forward(ffn_rows, gate_up_w, tile)

    down_away = rows_dot(ff_grad_other, hidden).astype(jnp.bfloat16)
    down_away, hidden = both(down_away, hidden)
    down_added = swap(down_away, "fsdp", 1)
    ff_away = scatter_terms(hidden, down_w)
    ff_away, gelu = both(ff_away, gelu)
    ff_far = scatter_begin(ff_away)
    unit_grad = feed_forward_back(ff_grad_rows, down_w, gelu, slope, tile)
    ffn_in_away = scatter_terms(unit_grad, gate_up_w)
    ffn_in_away, hidden, unit_grad = both(ffn_in_away, hidden, unit_grad)
    ffn_in_far = scatter_begin(ffn_in_away)
    down_grad = add_low(rows_dot(ff_grad_own, hidden), down_added)
    ffn_own, ffn_other = split_columns(ffn_rows, core, fsdp_count)
    down_grad, unit_grad = both(down_grad, unit_grad)
    down_owned = scatter_grads(down_grad, groups)
    gate_up_away = rows_dot(ffn_other, unit_grad).astype(jnp.bfloat16)
    gate_up_away, *ffn_in_far = both(gate_up_away, *ffn_in_far)
    gate_up_added = swap(gate_up_away, "fsdp", 1)
    ffn_in_sums = scatter_add(ffn_in_away, ffn_in_far)
    *ffn_in_sums, unit_grad = both(*ffn_in_sums, unit_grad)
    ffn_in_parts = scatter_end(ffn_in_sums)
    gate_up_grad = add_low(rows_dot(ffn_own, unit_grad), gate_up_added)
    gate_up_grad, unit_grad, *ffn_in_parts = both(gate_up_grad, unit_grad, *ffn_in_parts)
    gate_up_owned = scatter_grads(gate_up_grad, groups)
    ffn_in_grad = scatter_own(unit_grad, gate_up_w, ffn_in_parts)

    gain_ffn_part = jnp.sum(ffn_in_grad * normed_ffn, axis=0)
    resid_grad = upstream + norm_back(ffn_in_grad * ffn_gain, normed_ffn, scale_ffn)
    attn_grad_rows = gather_rows(resid_grad.astype(jnp.bfloat16))
    ff_sums = scatter_add(ff_away, ff_far)
    attn_grad_rows, *ff_sums = both(attn_grad_rows, *ff_sums)
    context_grad = jnp.dot(
        attn_grad_rows, output_w, preferred_element_type=jnp.float32
    ).astype(jnp.bfloat16)
    context_grad, down_owned, *ff_sums = both(context_grad, down_owned, *ff_sums)
    ff_parts = scatter_end(ff_sums)
    down_pieces = gather_pieces(down_owned, relay=False)
    qkv_grad, line_grad = attention_backward(
        qkv, place, context_grad, exponents, inverse, head_count, token_rows
    )
    qkv_grad, ff_parts, down_pieces = both(qkv_grad, ff_parts, down_pieces)
    attn_grads = rows_dot(attn_rows, qkv_grad).astype(jnp.bfloat16)
    attn_grads, context, qkv_grad = both(attn_grads, context, qkv_grad)
    attn_owned = scatter_grads(attn_grads)
    output_grad = rows_dot(attn_grad_rows, context).astype(jnp.bfloat16)
    output_grad, qkv_grad, hidden = both(output_grad, qkv_grad, hidden)
    output_owned = scatter_grads(output_grad)
    attn_in_away = scatter_terms(qkv_grad, qkv_w)
    attn_in_away, gate_up_owned, qkv_grad = both(attn_in_away, gate_up_owned, qkv_grad)
    attn_in_far = scatter_begin(attn_in_away)
    gate_up_pieces = gather_pieces(gate_up_owned)
    attn_in_parts = scatter_end(scatter_add(attn_in_away, attn_in_far))
    attn_in_grad = scatter_own(qkv_grad, qkv_w, attn_in_parts)
    gain_attn_part = jnp.sum(attn_in_grad * normed_attn, axis=0)
    stream_grad = resid_grad + norm_back(attn_in_grad * attn_gain, normed_attn, scale_attn)
    ff_out = scatter_own(hidden, down_w, ff_parts)
    result = resid + ff_out

    (down_out,) = place_columns(down_pieces, place, [(0, 0, 0, unit_count)], [unit_count])
    gate_out, up_out = place_columns(gate_up_pieces, place, unit_moves, [unit_count] * 2)

    own_segments = lax.dynamic_slice_in_dim(segment_row, seq_place * token_rows, token_rows, 0)
    valid = (own_segments >= 0).astype(jnp.float32)
    stat_terms = jnp.stack(
        [
            jnp.sum(valid * jnp.sum(result * result, axis=-1)),
            jnp.sum(valid * jnp.sum(attn_out * attn_out, axis=-1)),
            jnp.sum(valid * jnp.sum(ff_out * ff_out, axis=-1)),
            jnp.sum(valid),
        ]
    )
    table_part = jnp.dot(
        line_grad.reshape(head_count, 2 * row_length), bucket_table, precision=PRECISE
    )
    full_table = lax.dynamic_update_slice_in_dim(
        jnp.zeros(rel_table.shape, jnp.float32), table_part, seq_place * head_count, 0
    )
    packed = jnp.concatenate(
        [gain_attn_part, gain_ffn_part, full_table.reshape(-1), jnp.pad(stat_terms, (0, 124))]
    ).reshape(-1, 128)
    summed = total_sum(total_sum(packed, "seq"), "fsdp").reshape(-1)
    attn_owned, summed, result, stream_grad, down_out, gate_out, up_out = both(
        attn_owned, summed, result, stream_grad, down_out, gate_out, up_out
    )
    attn_pieces = gather_pieces(attn_owned)
    query_out, key_out, value_out = place_columns(
        attn_pieces, place, qkv_moves[:-1], [column_count] * 3
    )
    output_owned, attn_pieces = both(output_owned, attn_pieces)
    (output_out,) = place_columns(
        gather_pieces(output_owned), place, [(0, 0, 0, column_count)], [column_count]
    )
    table_end = 2 * model_width + rel_table.size
    stat_totals = summed[table_end : table_end + 4]
    rms_stats = jnp.sqrt(stat_totals[0:3] / (stat_totals[3] * model_width))
    gain_rows = model_width // fsdp_count
    table_rows = rel_table.shape[0] // fsdp_count
    gain_attn_grad = lax.dynamic_slice_in_dim(summed, fsdp_place * gain_rows, gain_rows, 0)
    gain_ffn_grad = lax.dynamic_slice_in_dim(
        summed, model_width + fsdp_place * gain_rows, gain_rows, 0
    )
    rel_table_grad = lax.dynamic_slice_in_dim(
        summed[2 * model_width : table_end].reshape(rel_table.shape),
        fsdp_place * table_rows,
        table_rows,
        0,
    )
    return (
        result.astype(jnp.bfloat16)[None],
        stream_grad.astype(jnp.bfloat16)[None],
        query_out,
        key_out,
        value_out,
        output_out,
        gain_attn_grad,
        rel_table_grad,
        gate_out,
        up_out,
        down_out,
        gain_ffn_grad,
        rms_stats,
    )


def solution(mesh):
    in_specs = (
        P("fsdp", "seq", None),
        P("fsdp", None),
        P(),
        P("fsdp", None),
        P("fsdp", None),
        P("fsdp", None),
        P("fsdp", None),
        P("fsdp"),
        P(),
        P("fsdp", None),
        P("fsdp", None),
        P("fsdp", None),
        P("fsdp"),
        P("fsdp", "seq", None),
    )
    out_specs = (
        P("fsdp", "seq", None),
        P("fsdp", "seq", None),
        P("fsdp", None),
        P("fsdp", None),
        P("fsdp", None),
        P("fsdp", None),
        P("fsdp"),
        P("fsdp", None),
        P("fsdp", None),
        P("fsdp", None),
        P("fsdp", None),
        P("fsdp"),
        P(),
    )
    return jax.shard_map(
        on_device, mesh=mesh, in_specs=in_specs, out_specs=out_specs, check_vma=False
    )
```

```python
import functools

import jax
import jax.numpy as jnp
from jax import lax
from jax.experimental import pallas as pl
from jax.experimental.pallas import tpu as pltpu
from jax.sharding import PartitionSpec as P

DH = 64


EPSILON = 1e-06
PRECISE = lax.Precision.HIGHEST
MASKED_SCORE = -1e30
TILE = 128
PAIR = 2 * DH
GELU_SCALE = 0.7978845608
GELU_CUBE = 0.044715
NO_COST = pl.CostEstimate(flops=0, bytes_accessed=0, transcendentals=0)
VMEM_BYTES = 56 * 1024 * 1024


def rows_dot(left, right):
    return lax.dot_general(
        left, right, (((0,), (0,)), ((), ())), preferred_element_type=jnp.float32
    )


def cols_dot(left, right):
    return lax.dot_general(
        left, right, (((1,), (1,)), ((), ())), preferred_element_type=jnp.float32
    )


def norm_back(grad_hat, normed, scale):
    return scale * (grad_hat - normed * jnp.mean(grad_hat * normed, axis=-1, keepdims=True))


def half_lanes(shape, which):
    lane = lax.broadcasted_iota(jnp.int32, shape, 1)
    return (lane < DH) if which == 0 else (lane >= DH)


def fold_rows(tile):
    return jnp.sum(tile.reshape(tile.shape[0] // 8, 8, tile.shape[1]), axis=0)


def query_block(length):
    return min(length, max(256, 2**20 // length))


def whole_place(row, token_rows, place):
    return jnp.bitwise_xor(row // token_rows, place) * token_rows + row % token_rows


def bias_offsets(first, block, length, token_rows, place, tile):
    reach = length - TILE
    key_place = whole_place(tile * TILE, token_rows, place)
    group = min(block, token_rows)
    return [
        pl.multiple_of(
            whole_place(first + start, token_rows, place) + (reach - key_place), TILE
        )
        for start in range(0, block, group)
    ], group


def forward_kernel(
    block,
    token_rows,
    place_ref,
    qkv_ref,
    row_ref,
    col_ref,
    bias_ref,
    ctx_ref,
    e_ref,
    inv_ref,
    strip_ref,
    score_ref,
):
    length = qkv_ref.shape[0]
    q_ref = qkv_ref.at[:, :PAIR]
    k_ref = qkv_ref.at[:, PAIR : 2 * PAIR]
    v_ref = qkv_ref.at[:, 2 * PAIR :]
    tiles = length // TILE
    width = 2 * length
    place = place_ref[0]
    group = min(block, token_rows)
    values_t = jnp.transpose(v_ref[...])
    for head in range(2):
        wide = jnp.broadcast_to(bias_ref[0, head : head + 1, :], (TILE, width))
        strip_ref[head] = pltpu.roll(wide, width - (TILE - 1), 1, stride=1, stride_axis=0)

    def one_block(first):
        q_block = q_ref[pl.ds(first, block), :]
        segment_q = jnp.concatenate(
            [
                row_ref[
                    :,
                    pl.ds(
                        pl.multiple_of(whole_place(first + start, token_rows, place), TILE), group
                    ),
                ]
                for start in range(0, block, group)
            ],
            axis=1,
        )
        outs = []
        for head in range(2):
            q_head = jnp.where(half_lanes(q_block.shape, head), q_block, jnp.zeros_like(q_block))
            raw = cols_dot(k_ref[...], q_head)
            highest = jnp.full((8, block), -jnp.inf, jnp.float32)
            for tile in range(tiles):
                rows = slice(tile * TILE, (tile + 1) * TILE)
                offsets, _ = bias_offsets(first, block, length, token_rows, place, tile)
                bias = jnp.concatenate(
                    [strip_ref[head, :, pl.ds(offset, group)] for offset in offsets], axis=1
                )
                key_place = whole_place(tile * TILE, token_rows, place)
                segment_k = col_ref[pl.ds(pl.multiple_of(key_place, TILE), TILE), :]
                segment_k = jnp.concatenate([segment_k] * (block // TILE), axis=1)
                score = jnp.where(segment_k == segment_q, raw[rows, :] + bias, MASKED_SCORE)
                score_ref[head, rows, :] = score
                highest = jnp.maximum(
                    highest, jnp.max(score.reshape(TILE // 8, 8, block), axis=0)
                )
            top = jnp.max(highest, axis=0, keepdims=True)
            total = jnp.zeros((8, block), jnp.float32)
            for tile in range(tiles):
                rows = slice(tile * TILE, (tile + 1) * TILE)
                exponent = jnp.exp(score_ref[head, rows, :] - top)
                total = total + fold_rows(exponent)
                e_ref[head, rows, pl.ds(first, block)] = exponent.astype(jnp.bfloat16)
            inverse = 1.0 / jnp.sum(total, axis=0, keepdims=True)
            inv_ref[head, :, pl.ds(first, block)] = inverse
            context = jnp.dot(
                values_t[head * DH : (head + 1) * DH, :],
                e_ref[head, :, pl.ds(first, block)],
                preferred_element_type=jnp.float32,
            )
            outs.append(context * inverse)
        ctx_ref[pl.ds(first, block), :] = jnp.transpose(jnp.concatenate(outs, axis=0)).astype(
            jnp.bfloat16
        )

    for_blocks(length // block, block, one_block)


def for_blocks(count, block, body):
    if count == 1:
        body(0)
        return

    def step(index, carry):
        body(pl.multiple_of(index * block, block))
        return carry

    lax.fori_loop(0, count, step, 0)


def attention_forward(qkv, place, segment_row, segment_wide, bias_line, heads, token_rows):
    length = qkv.shape[0]
    block = query_block(length)
    pairs = heads // 2
    return pl.pallas_call(
        functools.partial(forward_kernel, block, token_rows),
        grid=(pairs,),
        in_specs=[
            pl.BlockSpec(memory_space=pltpu.SMEM),
            pl.BlockSpec((length, 3 * PAIR), lambda i: (0, i)),
            pl.BlockSpec((1, length), lambda i: (0, 0)),
            pl.BlockSpec((length, TILE), lambda i: (0, 0)),
            pl.BlockSpec((1, 2, 2 * length), lambda i: (i, 0, 0)),
        ],
        out_specs=[
            pl.BlockSpec((length, PAIR), lambda i: (0, i)),
            pl.BlockSpec((2, length, length), lambda i: (i, 0, 0)),
            pl.BlockSpec((2, 1, length), lambda i: (i, 0, 0)),
        ],
        out_shape=[
            jax.ShapeDtypeStruct((length, heads * DH), jnp.bfloat16),
            jax.ShapeDtypeStruct((heads, length, length), jnp.bfloat16),
            jax.ShapeDtypeStruct((heads, 1, length), jnp.float32),
        ],
        scratch_shapes=[
            pltpu.VMEM((2, TILE, 2 * length), jnp.float32),
            pltpu.VMEM((2, length, block), jnp.float32),
        ],
        compiler_params=pltpu.CompilerParams(vmem_limit_bytes=VMEM_BYTES),
        cost_estimate=NO_COST,
        name="attention_forward",
    )(place, qkv, segment_row, segment_wide, bias_line)


def backward_kernel(
    block,
    token_rows,
    place_ref,
    qkv_ref,
    d_ref,
    e_ref,
    inv_ref,
    grad_ref,
    line_ref,
    strip_ref,
    prob_ref,
    low_ref,
    key_sum,
    value_sum,
):
    length = qkv_ref.shape[0]
    q_ref = qkv_ref.at[:, :PAIR]
    k_ref = qkv_ref.at[:, PAIR : 2 * PAIR]
    v_ref = qkv_ref.at[:, 2 * PAIR :]
    tiles = length // TILE
    place = place_ref[0]
    keys_t = jnp.transpose(k_ref[...])
    strip_ref[...] = jnp.zeros_like(strip_ref)
    key_sum[...] = jnp.zeros_like(key_sum)
    value_sum[...] = jnp.zeros_like(value_sum)

    def one_block(first):
        q_block = q_ref[pl.ds(first, block), :]
        d_block = d_ref[pl.ds(first, block), :]
        outs = []
        for head in range(2):
            mask = half_lanes(q_block.shape, head)
            q_head = jnp.where(mask, q_block, jnp.zeros_like(q_block))
            inverse = inv_ref[head, :, pl.ds(first, block)]
            scale = jnp.transpose(jnp.broadcast_to(inverse, (PAIR, block)))
            d_head = jnp.where(mask, d_block.astype(jnp.float32) * scale, 0.0)
            d_head = d_head.astype(jnp.bfloat16)
            prob_ref[head] = cols_dot(v_ref[...], d_head)
            value_sum[...] += jnp.dot(
                e_ref[head, :, pl.ds(first, block)], d_head, preferred_element_type=jnp.float32
            )
            total = jnp.zeros((8, block), jnp.float32)
            for tile in range(tiles):
                rows = slice(tile * TILE, (tile + 1) * TILE)
                exponent = e_ref[head, rows, pl.ds(first, block)].astype(jnp.float32)
                total = total + fold_rows(exponent * prob_ref[head, rows, :])
            centre = jnp.sum(total, axis=0, keepdims=True) * inverse
            for tile in range(tiles):
                rows = slice(tile * TILE, (tile + 1) * TILE)
                exponent = e_ref[head, rows, pl.ds(first, block)].astype(jnp.float32)
                grad = exponent * (prob_ref[head, rows, :] - centre)
                offsets, group = bias_offsets(first, block, length, token_rows, place, tile)
                for part, offset in enumerate(offsets):
                    at = pl.ds(offset, group)
                    strip_ref[head, :, at] = (
                        strip_ref[head, :, at] + grad[:, part * group : (part + 1) * group]
                    )
                low_ref[head, rows, :] = grad.astype(jnp.bfloat16)
            key_sum[...] += jnp.dot(low_ref[head], q_head, preferred_element_type=jnp.float32)
            outs.append(
                jnp.dot(
                    keys_t[head * DH : (head + 1) * DH, :],
                    low_ref[head],
                    preferred_element_type=jnp.float32,
                )
            )
        grad_ref[pl.ds(first, block), :PAIR] = jnp.transpose(
            jnp.concatenate(outs, axis=0)
        ).astype(jnp.bfloat16)

    for_blocks(length // block, block, one_block)
    grad_ref[:, PAIR : 2 * PAIR] = key_sum[...].astype(jnp.bfloat16)
    grad_ref[:, 2 * PAIR :] = value_sum[...].astype(jnp.bfloat16)
    for head in range(2):
        turned = strip_ref[head]
        while turned.shape[0] > 1:
            half = turned.shape[0] // 2
            turned = pltpu.roll(turned[:half], half, 1) + turned[half:]
        line_ref[0, head : head + 1, :] = turned


def attention_backward(qkv, place, d, e, inv, heads, token_rows):
    length = qkv.shape[0]
    block = query_block(length)
    pairs = heads // 2
    triple = pl.BlockSpec((length, 3 * PAIR), lambda i: (0, i))
    return pl.pallas_call(
        functools.partial(backward_kernel, block, token_rows),
        grid=(pairs,),
        in_specs=[
            pl.BlockSpec(memory_space=pltpu.SMEM),
            triple,
            pl.BlockSpec((length, PAIR), lambda i: (0, i)),
            pl.BlockSpec((2, length, length), lambda i: (i, 0, 0)),
            pl.BlockSpec((2, 1, length), lambda i: (i, 0, 0)),
        ],
        out_specs=[triple, pl.BlockSpec((1, 2, 2 * length), lambda i: (i, 0, 0))],
        out_shape=[
            jax.ShapeDtypeStruct((length, 3 * heads * DH), jnp.bfloat16),
            jax.ShapeDtypeStruct((pairs, 2, 2 * length), jnp.float32),
        ],
        scratch_shapes=[
            pltpu.VMEM((2, TILE, 2 * length), jnp.float32),
            pltpu.VMEM((2, length, block), jnp.float32),
            pltpu.VMEM((2, length, block), jnp.bfloat16),
            pltpu.VMEM((length, PAIR), jnp.float32),
            pltpu.VMEM((length, PAIR), jnp.float32),
        ],
        compiler_params=pltpu.CompilerParams(vmem_limit_bytes=VMEM_BYTES),
        cost_estimate=NO_COST,
        name="attention_backward",
    )(place, qkv, d, e, inv)


def swap(piece, axis, step):
    return lax.ppermute(piece, axis, [(i, i ^ step) for i in range(lax.axis_size(axis))])


def gather_begin(piece, relay=True):
    count = lax.axis_size("seq")
    steps = (1, 2) if count == 4 and relay else range(1, count)
    return tuple(swap(piece, "seq", step) for step in steps)


def gather_end(piece, near):
    if len(near) != 2:
        return [[part] for part in (piece, *near)]
    first, second = near
    half = piece.shape[0] // 2
    upper = swap(second[:half], "seq", 1)
    lower = swap(first[half:], "seq", 2)
    return [[piece], [first], [second], [upper, lower]]


def joined(parts):
    return jnp.concatenate([part for pieces in parts for part in pieces], axis=0)


def gather_rows(piece):
    return joined(gather_end(piece, gather_begin(piece)))


def low_dot(rows, weights):
    return cols_dot(rows, weights).astype(jnp.bfloat16)


def split_terms(terms):
    count = lax.axis_size("seq")
    size = terms.shape[0] // (count - 1)
    return (terms[: 2 * size], terms[2 * size :]) if count == 4 else (terms, None)


def scatter_begin(far):
    if far is None:
        return ()
    half = far.shape[0] // 2
    return swap(far[:half], "seq", 1), swap(far[half:], "seq", 2)


def scatter_add(near, passing):
    if not passing:
        size = near.shape[0] // (lax.axis_size("seq") - 1)
        return tuple(near[start : start + size] for start in range(0, near.shape[0], size))
    size = near.shape[0] // 2
    upper, lower = (part.astype(jnp.float32) for part in passing)
    first = near[:size].astype(jnp.float32) + jnp.pad(lower, ((size // 2, 0), (0, 0)))
    second = near[size:].astype(jnp.float32) + jnp.pad(upper, ((0, size // 2), (0, 0)))
    return first.astype(jnp.bfloat16), second.astype(jnp.bfloat16)


def scatter_end(sums):
    return tuple(swap(part, "seq", k + 1) for k, part in enumerate(sums))


def add_parts(own, received):
    return own + sum(part.astype(jnp.float32) for part in received)


def scatter_sum(rows, weights):
    size = rows.shape[0] // lax.axis_size("seq")
    near, far = split_terms(low_dot(rows[size:], weights))
    received = scatter_end(scatter_add(near, scatter_begin(far)))
    return add_parts(cols_dot(rows[:size], weights), received)


def total_sum(values, axis):
    count = lax.axis_size(axis)
    level = [values] + [swap(values, axis, step) for step in range(1, count)]
    while len(level) > 1:
        level = [level[i] + level[i + 1] for i in range(0, len(level), 2)]
    return level[0]


def feed_forward_kernel(tile, x_ref, w_ref, act_ref, gelu_ref, slope_ref):
    rows = x_ref.shape[0]
    chunk = min(512, rows)
    for start in range(0, rows, chunk):
        at = slice(start, start + chunk)
        both = jnp.dot(x_ref[at, :], w_ref[...], preferred_element_type=jnp.float32)
        gate, up = both[:, :tile], both[:, tile:]
        square = gate * gate
        tanh = jnp.tanh(GELU_SCALE * gate * (1.0 + GELU_CUBE * square))
        half_up = 0.5 * (1.0 + tanh)
        gelu = gate * half_up
        bend = 0.5 * GELU_SCALE * gate * (1.0 - tanh * tanh) * (1.0 + 3.0 * GELU_CUBE * square)
        act_ref[at, :] = (gelu * up).astype(jnp.bfloat16)
        gelu_ref[at, :] = gelu.astype(jnp.bfloat16)
        slope_ref[at, :] = (up * (half_up + bend)).astype(jnp.bfloat16)


def feed_forward(rows, weights, tile):
    length, model_width = rows.shape
    units = weights.shape[1] // 2
    block = pl.BlockSpec((length, tile), lambda j: (0, j))
    return pl.pallas_call(
        functools.partial(feed_forward_kernel, tile),
        grid=(units // tile,),
        in_specs=[
            pl.BlockSpec((length, model_width), lambda j: (0, 0)),
            pl.BlockSpec((model_width, 2 * tile), lambda j: (0, j)),
        ],
        out_specs=[block, block, block],
        out_shape=[
            jax.ShapeDtypeStruct((length, units), jnp.bfloat16),
            jax.ShapeDtypeStruct((length, units), jnp.bfloat16),
            jax.ShapeDtypeStruct((length, units), jnp.bfloat16),
        ],
        compiler_params=pltpu.CompilerParams(vmem_limit_bytes=VMEM_BYTES),
        cost_estimate=NO_COST,
        name="feed_forward",
    )(rows, weights)


def feed_forward_back_kernel(tile, d_ref, w_ref, gelu_ref, slope_ref, grad_ref):
    rows = d_ref.shape[0]
    chunk = min(512, rows)
    for start in range(0, rows, chunk):
        at = slice(start, start + chunk)
        grad = jnp.dot(d_ref[at, :], w_ref[...], preferred_element_type=jnp.float32)
        grad_ref[at, :tile] = (grad * slope_ref[at, :].astype(jnp.float32)).astype(jnp.bfloat16)
        grad_ref[at, tile:] = (grad * gelu_ref[at, :].astype(jnp.float32)).astype(jnp.bfloat16)


def feed_forward_back(grad_rows, weights, gelu, slope, tile):
    length, model_width = grad_rows.shape
    units = weights.shape[1]
    block = pl.BlockSpec((length, tile), lambda j: (0, j))
    return pl.pallas_call(
        functools.partial(feed_forward_back_kernel, tile),
        grid=(units // tile,),
        in_specs=[
            pl.BlockSpec((length, model_width), lambda j: (0, 0)),
            pl.BlockSpec((model_width, tile), lambda j: (0, j)),
            block,
            block,
        ],
        out_specs=pl.BlockSpec((length, 2 * tile), lambda j: (0, j)),
        out_shape=jax.ShapeDtypeStruct((length, 2 * units), jnp.bfloat16),
        compiler_params=pltpu.CompilerParams(vmem_limit_bytes=VMEM_BYTES),
        cost_estimate=NO_COST,
        name="feed_forward_back",
    )(grad_rows, weights, gelu, slope)


def place_kernel(moves, count, widths, place_ref, *refs):
    pieces, outs = refs[:count], refs[count:]
    for step in range(count):
        owner = jnp.bitwise_xor(place_ref[0], step)
        for out, source, target, size in moves:
            at = pl.multiple_of(owner * widths[out] + target, TILE)
            block = pieces[step][:, source : source + size]
            outs[out][:, pl.ds(at, size)] = block.astype(jnp.float32)


def place_columns(parts, place, moves, widths):
    pieces = [part[0] if len(part) == 1 else jnp.concatenate(part, axis=0) for part in parts]
    count = len(pieces)
    rows, width = pieces[0].shape
    block = min(64, rows)
    return pl.pallas_call(
        functools.partial(place_kernel, moves, count, widths),
        grid=(rows // block,),
        in_specs=[pl.BlockSpec(memory_space=pltpu.SMEM)]
        + [pl.BlockSpec((block, width), lambda i: (i, 0))] * count,
        out_specs=[pl.BlockSpec((block, count * size), lambda i: (i, 0)) for size in widths],
        out_shape=[jax.ShapeDtypeStruct((rows, count * size), jnp.float32) for size in widths],
        compiler_params=pltpu.CompilerParams(vmem_limit_bytes=VMEM_BYTES),
        cost_estimate=NO_COST,
        name="place_columns",
    )(place, *pieces)


def take_kernel(moves, count, place_ref, *refs):
    out_ref = refs[count]
    for which, source, target, size in moves:
        out_ref[:, source : source + size] = refs[which][:, target : target + size]


def take_columns(place, weights, moves, counts):
    rows = weights[0].shape[0]
    block = min(64, rows)
    width = sum(counts)

    def chosen(count):
        return pl.BlockSpec((block, count), lambda i, place_ref: (i, place_ref[0]))

    return pl.pallas_call(
        functools.partial(take_kernel, moves, len(weights)),
        grid_spec=pltpu.PrefetchScalarGridSpec(
            num_scalar_prefetch=1,
            grid=(rows // block,),
            in_specs=[chosen(count) for count in counts],
            out_specs=pl.BlockSpec((block, width), lambda i, place_ref: (i, 0)),
        ),
        out_shape=jax.ShapeDtypeStruct((rows, width), weights[0].dtype),
        compiler_params=pltpu.CompilerParams(vmem_limit_bytes=VMEM_BYTES),
        cost_estimate=NO_COST,
        name="take_columns",
    )(place, *weights)


def split_kernel(core_ref, own_in, other_in, own_ref, other_ref):
    own_ref[...] = own_in[...]
    other_ref[...] = other_in[...]


def split_columns(rows, core, groups):
    length, width = rows.shape
    size = width // groups

    def chosen(side):
        return pl.BlockSpec(
            (length, size), lambda i, core_ref: (0, 2 * i + jnp.bitwise_xor(core_ref[0], side))
        )

    half = jax.ShapeDtypeStruct((length, width // 2), rows.dtype)
    block = pl.BlockSpec((length, size), lambda i, core_ref: (0, i))
    return pl.pallas_call(
        split_kernel,
        grid_spec=pltpu.PrefetchScalarGridSpec(
            num_scalar_prefetch=1,
            grid=(groups // 2,),
            in_specs=[chosen(0), chosen(1)],
            out_specs=[block, block],
        ),
        out_shape=[half, half],
        compiler_params=pltpu.CompilerParams(vmem_limit_bytes=VMEM_BYTES),
        cost_estimate=NO_COST,
        name="split_columns",
    )(core, rows, rows)


def both(*values):
    return lax.optimization_barrier(values)


def add_low(sums, added):
    return (sums + added.astype(jnp.float32)).astype(jnp.bfloat16)


def on_device(
    tokens,
    segments,
    buckets,
    w_query,
    w_key,
    w_value,
    w_attn_out,
    gain_attn,
    rel_table,
    w_gate,
    w_up,
    w_down,
    gain_ffn,
    out_grad,
):
    token_rows = tokens.shape[1]
    model_width = tokens.shape[2]
    ffn_width = w_gate.shape[1]
    segment_row = segments[0]
    row_length = segment_row.shape[0]
    seq_count = lax.axis_size("seq")
    fsdp_count = lax.axis_size("fsdp")
    seq_place = lax.axis_index("seq")
    fsdp_place = lax.axis_index("fsdp")
    place = seq_place.astype(jnp.int32).reshape(1)
    head_count = model_width // seq_count // DH
    column_count = model_width // seq_count
    unit_count = ffn_width // seq_count

    tile = 256 if unit_count % 256 == 0 else 128
    pairs = head_count // 2

    def gather_weights(piece):
        return lax.all_gather(piece, "fsdp", axis=0, tiled=True)

    qkv_moves = [
        (which, (3 * pair + which) * PAIR, pair * PAIR, PAIR)
        for pair in range(pairs)
        for which in range(3)
    ] + [(3, 3 * column_count, 0, column_count)]
    unit_moves = [
        (which, (2 * block + which) * tile, block * tile, tile)
        for block in range(unit_count // tile)
        for which in range(2)
    ]
    attn_part = take_columns(
        place, (w_query, w_key, w_value, w_attn_out), qkv_moves, [column_count] * 4
    )
    attn_w = gather_weights(attn_part)
    gains = lax.all_gather(jnp.stack([gain_attn, gain_ffn]), "fsdp", axis=1, tiled=True)
    qkv_w = attn_w[:, : 3 * column_count]
    output_w = attn_w[:, 3 * column_count :]

    table_rows = jnp.pad(buckets[::-1], (0, 1), constant_values=-1)
    bucket_table = (
        table_rows[:, None] == jnp.arange(rel_table.shape[1], dtype=jnp.int32)[None, :]
    ).astype(jnp.float32)
    local_table = lax.dynamic_slice_in_dim(rel_table, seq_place * head_count, head_count, 0)
    bias_line = jnp.dot(local_table, jnp.transpose(bucket_table), precision=PRECISE)
    bias_line = bias_line.reshape(head_count // 2, 2, 2 * row_length)
    segment_wide = jnp.broadcast_to(segment_row[:, None], (row_length, TILE))

    stream = tokens[0].astype(jnp.float32)
    scale_attn = lax.rsqrt(jnp.mean(stream * stream, axis=-1, keepdims=True) + EPSILON)
    normed_attn = stream * scale_attn
    upstream = out_grad[0].astype(jnp.float32)

    stream_near = gather_begin(tokens[0])
    stream_near, gains = both(stream_near, gains)
    attn_gain = gains[0].astype(jnp.float32)
    ffn_gain = gains[1].astype(jnp.float32)
    stream_rows = joined(gather_end(tokens[0], stream_near))
    gate_up_part = take_columns(place, (w_gate, w_up), unit_moves, [unit_count] * 2)
    gate_up_part, stream_rows = both(gate_up_part, stream_rows)
    gate_up_w = gather_weights(gate_up_part)
    stream_rows = stream_rows.astype(jnp.float32)
    rows_scale = lax.rsqrt(jnp.mean(stream_rows * stream_rows, axis=-1, keepdims=True) + EPSILON)
    attn_rows = (stream_rows * rows_scale * attn_gain).astype(jnp.bfloat16)
    ff_grad_rows = gather_rows(out_grad[0])
    attn_rows, ff_grad_rows = both(attn_rows, ff_grad_rows)

    qkv = jnp.dot(attn_rows, qkv_w, preferred_element_type=jnp.float32).astype(jnp.bfloat16)
    down_part, qkv = both(
        lax.dynamic_slice_in_dim(w_down, seq_place * unit_count, unit_count, 1), qkv
    )
    down_w = gather_weights(down_part)
    context, exponents, inverse = attention_forward(
        qkv, place, segments, segment_wide, bias_line, head_count, token_rows
    )

    attn_out = scatter_sum(context, output_w)
    chips = fsdp_count // 2
    core = (fsdp_place % 2).astype(jnp.int32).reshape(1)
    groups = [[2 * chip + side for chip in range(chips)] for side in range(2)]

    def scatter_grads(grads, axis_index_groups=None):
        return lax.psum_scatter(
            grads,
            "fsdp",
            scatter_dimension=0,
            tiled=True,
            axis_index_groups=axis_index_groups,
        )

    resid = stream + attn_out
    scale_ffn = lax.rsqrt(jnp.mean(resid * resid, axis=-1, keepdims=True) + EPSILON)
    normed_ffn = resid * scale_ffn
    ffn_rows = gather_rows((normed_ffn * ffn_gain).astype(jnp.bfloat16))

    hidden, gelu, slope = feed_forward(ffn_rows, gate_up_w, tile)

    down_grad = rows_dot(ff_grad_rows, hidden).astype(jnp.bfloat16)
    ffn_own, ffn_other = split_columns(ffn_rows, core, fsdp_count)
    down_owned = scatter_grads(down_grad)
    down_grad, hidden, gelu, ffn_own, ffn_other = both(down_grad, hidden, gelu, ffn_own, ffn_other)
    away = row_length // seq_count
    passed = 3 * away if seq_count == 4 else row_length
    ff_far = low_dot(hidden[passed:], down_w) if seq_count == 4 else None
    ff_far, hidden, gelu = both(ff_far, hidden, gelu)
    ff_passing = scatter_begin(ff_far)
    unit_grad = feed_forward_back(ff_grad_rows, down_w, gelu, slope, tile)
    unit_terms = low_dot(unit_grad[away:], gate_up_w)
    unit_terms, unit_grad, ff_passing = both(unit_terms, unit_grad, ff_passing)
    unit_near, unit_far = split_terms(unit_terms)
    unit_passing = scatter_begin(unit_far)
    gate_up_away = rows_dot(ffn_other, unit_grad).astype(jnp.bfloat16)
    gate_up_away, unit_grad, unit_passing = both(gate_up_away, unit_grad, unit_passing)
    unit_sums = scatter_add(unit_near, unit_passing)
    unit_sums, unit_grad, gate_up_away = both(unit_sums, unit_grad, gate_up_away)
    unit_parts = scatter_end(unit_sums)
    gate_up_added = swap(gate_up_away, "fsdp", 1)
    gate_up_grad = add_low(rows_dot(ffn_own, unit_grad), gate_up_added)
    ffn_in_own = cols_dot(unit_grad[:away], gate_up_w)
    ffn_in_own, gate_up_grad, unit_parts = both(ffn_in_own, gate_up_grad, unit_parts)
    gate_up_owned = scatter_grads(gate_up_grad, groups)
    ffn_in_grad = add_parts(ffn_in_own, unit_parts)

    resid_grad = upstream + norm_back(ffn_in_grad * ffn_gain, normed_ffn, scale_ffn)
    attn_grad = resid_grad.astype(jnp.bfloat16)
    attn_grad, hidden, down_owned = both(attn_grad, hidden, down_owned)
    attn_grad_rows = gather_rows(attn_grad)
    ff_near = low_dot(hidden[away:passed], down_w)
    ff_sums = scatter_add(ff_near, ff_passing)
    attn_grad_rows, ff_sums, down_owned = both(attn_grad_rows, ff_sums, down_owned)
    context_grad = jnp.dot(
        attn_grad_rows, output_w, preferred_element_type=jnp.float32
    ).astype(jnp.bfloat16)
    ff_parts = scatter_end(ff_sums)
    down_near = gather_begin(down_owned, relay=False)
    qkv_grad, line_grad = attention_backward(
        qkv, place, context_grad, exponents, inverse, head_count, token_rows
    )
    attn_grads = rows_dot(attn_rows, qkv_grad).astype(jnp.bfloat16)
    attn_grads, context, qkv_grad, ff_parts, down_near, attn_grad_rows, gate_up_owned = both(
        attn_grads, context, qkv_grad, ff_parts, down_near, attn_grad_rows, gate_up_owned
    )
    attn_owned = scatter_grads(attn_grads)
    gate_up_near = gather_begin(gate_up_owned)
    output_own, output_other = split_columns(attn_grad_rows, core, fsdp_count)
    output_away = rows_dot(output_other, context).astype(jnp.bfloat16)
    qkv_terms = low_dot(qkv_grad[away:], qkv_w)
    qkv_terms, qkv_grad, output_away, output_own, down_near, hidden = both(
        qkv_terms, qkv_grad, output_away, output_own, down_near, hidden
    )
    qkv_near, qkv_far = split_terms(qkv_terms)
    qkv_passing = scatter_begin(qkv_far)
    output_added = swap(output_away, "fsdp", 1)
    attn_in_own = cols_dot(qkv_grad[:away], qkv_w)
    output_grad = add_low(rows_dot(output_own, context), output_added)
    attn_in_own, output_grad, qkv_passing, hidden, ffn_in_grad, gate_up_near, down_near = both(
        attn_in_own, output_grad, qkv_passing, hidden, ffn_in_grad, gate_up_near, down_near
    )
    output_owned = scatter_grads(output_grad, groups)
    qkv_sums = scatter_add(qkv_near, qkv_passing)
    qkv_sums, gate_up_near, down_near = both(qkv_sums, gate_up_near, down_near)
    attn_in_parts = scatter_end(qkv_sums)
    gate_up_pieces = gather_end(gate_up_owned, gate_up_near)
    down_pieces = gather_end(down_owned, down_near)
    ff_out = add_parts(cols_dot(hidden[:away], down_w), ff_parts)
    result = resid + ff_out
    gain_ffn_part = jnp.sum(ffn_in_grad * normed_ffn, axis=0)
    attn_owned, result, gain_ffn_part = both(attn_owned, result, gain_ffn_part)
    attn_near = gather_begin(attn_owned)
    attn_in_grad = add_parts(attn_in_own, attn_in_parts)
    gain_attn_part = jnp.sum(attn_in_grad * normed_attn, axis=0)
    stream_grad = resid_grad + norm_back(attn_in_grad * attn_gain, normed_attn, scale_attn)
    (down_out,) = place_columns(down_pieces, place, [(0, 0, 0, unit_count)], [unit_count])
    gate_out, up_out = place_columns(gate_up_pieces, place, unit_moves, [unit_count] * 2)

    own_segments = lax.dynamic_slice_in_dim(segment_row, seq_place * token_rows, token_rows, 0)
    valid = (own_segments >= 0).astype(jnp.float32)
    stat_terms = jnp.stack(
        [
            jnp.sum(valid * jnp.sum(result * result, axis=-1)),
            jnp.sum(valid * jnp.sum(attn_out * attn_out, axis=-1)),
            jnp.sum(valid * jnp.sum(ff_out * ff_out, axis=-1)),
            jnp.sum(valid),
        ]
    )
    table_part = jnp.dot(
        line_grad.reshape(head_count, 2 * row_length), bucket_table, precision=PRECISE
    )
    full_table = lax.dynamic_update_slice_in_dim(
        jnp.zeros(rel_table.shape, jnp.float32), table_part, seq_place * head_count, 0
    )
    packed = jnp.concatenate(
        [gain_attn_part, gain_ffn_part, full_table.reshape(-1), jnp.pad(stat_terms, (0, 124))]
    ).reshape(-1, 128)
    summed = total_sum(packed, "fsdp")
    attn_near, stream_grad, gain_attn_part, down_out, output_owned = both(
        attn_near, stream_grad, gain_attn_part, down_out, output_owned
    )
    output_near = gather_begin(output_owned, relay=False)
    attn_pieces = gather_end(attn_owned, attn_near)
    summed, attn_pieces, output_near, gate_out, up_out = both(
        summed, attn_pieces, output_near, gate_out, up_out
    )
    summed = total_sum(summed, "seq").reshape(-1)
    query_out, key_out, value_out = place_columns(
        attn_pieces, place, qkv_moves[:-1], [column_count] * 3
    )
    (output_out,) = place_columns(
        gather_end(output_owned, output_near),
        place,
        [(0, 0, 0, column_count)],
        [column_count],
    )
    table_end = 2 * model_width + rel_table.size
    stat_totals = summed[table_end : table_end + 4]
    rms_stats = jnp.sqrt(stat_totals[0:3] / (stat_totals[3] * model_width))
    gain_rows = model_width // fsdp_count
    table_rows = rel_table.shape[0] // fsdp_count
    gain_attn_grad = lax.dynamic_slice_in_dim(summed, fsdp_place * gain_rows, gain_rows, 0)
    gain_ffn_grad = lax.dynamic_slice_in_dim(
        summed, model_width + fsdp_place * gain_rows, gain_rows, 0
    )
    rel_table_grad = lax.dynamic_slice_in_dim(
        summed[2 * model_width : table_end].reshape(rel_table.shape),
        fsdp_place * table_rows,
        table_rows,
        0,
    )
    return (
        result.astype(jnp.bfloat16)[None],
        stream_grad.astype(jnp.bfloat16)[None],
        query_out,
        key_out,
        value_out,
        output_out,
        gain_attn_grad,
        rel_table_grad,
        gate_out,
        up_out,
        down_out,
        gain_ffn_grad,
        rms_stats,
    )


def solution(mesh):
    in_specs = (
        P("fsdp", "seq", None),
        P("fsdp", None),
        P(),
        P("fsdp", None),
        P("fsdp", None),
        P("fsdp", None),
        P("fsdp", None),
        P("fsdp"),
        P(),
        P("fsdp", None),
        P("fsdp", None),
        P("fsdp", None),
        P("fsdp"),
        P("fsdp", "seq", None),
    )
    out_specs = (
        P("fsdp", "seq", None),
        P("fsdp", "seq", None),
        P("fsdp", None),
        P("fsdp", None),
        P("fsdp", None),
        P("fsdp", None),
        P("fsdp"),
        P("fsdp", None),
        P("fsdp", None),
        P("fsdp", None),
        P("fsdp", None),
        P("fsdp"),
        P(),
    )
    return jax.shard_map(
        on_device, mesh=mesh, in_specs=in_specs, out_specs=out_specs, check_vma=False
    )
```

```python
import functools

import jax
import jax.numpy as jnp
from jax import lax
from jax.experimental import pallas as pl
from jax.experimental.pallas import tpu as pltpu
from jax.sharding import PartitionSpec as P

DH = 64


EPSILON = 1e-06
PRECISE = lax.Precision.HIGHEST
MASKED_SCORE = -1e30
TILE = 128
PAIR = 2 * DH
GELU_SCALE = 0.7978845608
GELU_CUBE = 0.044715
NO_COST = pl.CostEstimate(flops=0, bytes_accessed=0, transcendentals=0)
VMEM_BYTES = 56 * 1024 * 1024


def rows_dot(left, right):
    return lax.dot_general(
        left, right, (((0,), (0,)), ((), ())), preferred_element_type=jnp.float32
    )


def cols_dot(left, right):
    return lax.dot_general(
        left, right, (((1,), (1,)), ((), ())), preferred_element_type=jnp.float32
    )


def norm_back(grad_hat, normed, scale):
    return scale * (grad_hat - normed * jnp.mean(grad_hat * normed, axis=-1, keepdims=True))


def half_lanes(shape, which):
    lane = lax.broadcasted_iota(jnp.int32, shape, 1)
    return (lane < DH) if which == 0 else (lane >= DH)


def fold_rows(tile):
    return jnp.sum(tile.reshape(tile.shape[0] // 8, 8, tile.shape[1]), axis=0)


def query_block(length):
    return min(length, max(256, 2**20 // length))


def whole_place(row, token_rows, place):
    return jnp.bitwise_xor(row // token_rows, place) * token_rows + row % token_rows


def bias_offsets(first, block, length, token_rows, place, tile):
    reach = length - TILE
    key_place = whole_place(tile * TILE, token_rows, place)
    group = min(block, token_rows)
    return [
        pl.multiple_of(
            whole_place(first + start, token_rows, place) + (reach - key_place), TILE
        )
        for start in range(0, block, group)
    ], group


def forward_kernel(
    block,
    token_rows,
    place_ref,
    qkv_ref,
    row_ref,
    col_ref,
    bias_ref,
    ctx_ref,
    e_ref,
    inv_ref,
    strip_ref,
    score_ref,
):
    length = qkv_ref.shape[0]
    q_ref = qkv_ref.at[:, :PAIR]
    k_ref = qkv_ref.at[:, PAIR : 2 * PAIR]
    v_ref = qkv_ref.at[:, 2 * PAIR :]
    tiles = length // TILE
    width = 2 * length
    place = place_ref[0]
    group = min(block, token_rows)
    values_t = jnp.transpose(v_ref[...])
    for head in range(2):
        wide = jnp.broadcast_to(bias_ref[0, head : head + 1, :], (TILE, width))
        strip_ref[head] = pltpu.roll(wide, width - (TILE - 1), 1, stride=1, stride_axis=0)

    def one_block(first):
        q_block = q_ref[pl.ds(first, block), :]
        segment_q = jnp.concatenate(
            [
                row_ref[
                    :,
                    pl.ds(
                        pl.multiple_of(whole_place(first + start, token_rows, place), TILE), group
                    ),
                ]
                for start in range(0, block, group)
            ],
            axis=1,
        )
        outs = []
        for head in range(2):
            q_head = jnp.where(half_lanes(q_block.shape, head), q_block, jnp.zeros_like(q_block))
            raw = cols_dot(k_ref[...], q_head)
            highest = jnp.full((8, block), -jnp.inf, jnp.float32)
            for tile in range(tiles):
                rows = slice(tile * TILE, (tile + 1) * TILE)
                offsets, _ = bias_offsets(first, block, length, token_rows, place, tile)
                bias = jnp.concatenate(
                    [strip_ref[head, :, pl.ds(offset, group)] for offset in offsets], axis=1
                )
                key_place = whole_place(tile * TILE, token_rows, place)
                segment_k = col_ref[pl.ds(pl.multiple_of(key_place, TILE), TILE), :]
                segment_k = jnp.concatenate([segment_k] * (block // TILE), axis=1)
                score = jnp.where(segment_k == segment_q, raw[rows, :] + bias, MASKED_SCORE)
                score_ref[head, rows, :] = score
                highest = jnp.maximum(
                    highest, jnp.max(score.reshape(TILE // 8, 8, block), axis=0)
                )
            top = jnp.max(highest, axis=0, keepdims=True)
            total = jnp.zeros((8, block), jnp.float32)
            for tile in range(tiles):
                rows = slice(tile * TILE, (tile + 1) * TILE)
                exponent = jnp.exp(score_ref[head, rows, :] - top)
                total = total + fold_rows(exponent)
                e_ref[head, rows, pl.ds(first, block)] = exponent.astype(jnp.bfloat16)
            inverse = 1.0 / jnp.sum(total, axis=0, keepdims=True)
            inv_ref[head, :, pl.ds(first, block)] = inverse
            context = jnp.dot(
                values_t[head * DH : (head + 1) * DH, :],
                e_ref[head, :, pl.ds(first, block)],
                preferred_element_type=jnp.float32,
            )
            outs.append(context * inverse)
        ctx_ref[pl.ds(first, block), :] = jnp.transpose(jnp.concatenate(outs, axis=0)).astype(
            jnp.bfloat16
        )

    for_blocks(length // block, block, one_block)


def for_blocks(count, block, body):
    if count == 1:
        body(0)
        return

    def step(index, carry):
        body(pl.multiple_of(index * block, block))
        return carry

    lax.fori_loop(0, count, step, 0)


def attention_forward(qkv, place, segment_row, segment_wide, bias_line, heads, token_rows):
    length = qkv.shape[0]
    block = query_block(length)
    pairs = heads // 2
    return pl.pallas_call(
        functools.partial(forward_kernel, block, token_rows),
        grid=(pairs,),
        in_specs=[
            pl.BlockSpec(memory_space=pltpu.SMEM),
            pl.BlockSpec((length, 3 * PAIR), lambda i: (0, i)),
            pl.BlockSpec((1, length), lambda i: (0, 0)),
            pl.BlockSpec((length, TILE), lambda i: (0, 0)),
            pl.BlockSpec((1, 2, 2 * length), lambda i: (i, 0, 0)),
        ],
        out_specs=[
            pl.BlockSpec((length, PAIR), lambda i: (0, i)),
            pl.BlockSpec((2, length, length), lambda i: (i, 0, 0)),
            pl.BlockSpec((2, 1, length), lambda i: (i, 0, 0)),
        ],
        out_shape=[
            jax.ShapeDtypeStruct((length, heads * DH), jnp.bfloat16),
            jax.ShapeDtypeStruct((heads, length, length), jnp.bfloat16),
            jax.ShapeDtypeStruct((heads, 1, length), jnp.float32),
        ],
        scratch_shapes=[
            pltpu.VMEM((2, TILE, 2 * length), jnp.float32),
            pltpu.VMEM((2, length, block), jnp.float32),
        ],
        compiler_params=pltpu.CompilerParams(vmem_limit_bytes=VMEM_BYTES),
        cost_estimate=NO_COST,
        name="attention_forward",
    )(place, qkv, segment_row, segment_wide, bias_line)


def backward_kernel(
    block,
    token_rows,
    place_ref,
    qkv_ref,
    d_ref,
    e_ref,
    inv_ref,
    grad_ref,
    line_ref,
    strip_ref,
    prob_ref,
    low_ref,
    key_sum,
    value_sum,
):
    length = qkv_ref.shape[0]
    q_ref = qkv_ref.at[:, :PAIR]
    k_ref = qkv_ref.at[:, PAIR : 2 * PAIR]
    v_ref = qkv_ref.at[:, 2 * PAIR :]
    tiles = length // TILE
    place = place_ref[0]
    keys_t = jnp.transpose(k_ref[...])
    strip_ref[...] = jnp.zeros_like(strip_ref)
    key_sum[...] = jnp.zeros_like(key_sum)
    value_sum[...] = jnp.zeros_like(value_sum)

    def one_block(first):
        q_block = q_ref[pl.ds(first, block), :]
        d_block = d_ref[pl.ds(first, block), :]
        outs = []
        for head in range(2):
            mask = half_lanes(q_block.shape, head)
            q_head = jnp.where(mask, q_block, jnp.zeros_like(q_block))
            inverse = inv_ref[head, :, pl.ds(first, block)]
            scale = jnp.transpose(jnp.broadcast_to(inverse, (PAIR, block)))
            d_head = jnp.where(mask, d_block.astype(jnp.float32) * scale, 0.0)
            d_head = d_head.astype(jnp.bfloat16)
            prob_ref[head] = cols_dot(v_ref[...], d_head)
            value_sum[...] += jnp.dot(
                e_ref[head, :, pl.ds(first, block)], d_head, preferred_element_type=jnp.float32
            )
            total = jnp.zeros((8, block), jnp.float32)
            for tile in range(tiles):
                rows = slice(tile * TILE, (tile + 1) * TILE)
                exponent = e_ref[head, rows, pl.ds(first, block)].astype(jnp.float32)
                total = total + fold_rows(exponent * prob_ref[head, rows, :])
            centre = jnp.sum(total, axis=0, keepdims=True) * inverse
            for tile in range(tiles):
                rows = slice(tile * TILE, (tile + 1) * TILE)
                exponent = e_ref[head, rows, pl.ds(first, block)].astype(jnp.float32)
                grad = exponent * (prob_ref[head, rows, :] - centre)
                offsets, group = bias_offsets(first, block, length, token_rows, place, tile)
                for part, offset in enumerate(offsets):
                    at = pl.ds(offset, group)
                    strip_ref[head, :, at] = (
                        strip_ref[head, :, at] + grad[:, part * group : (part + 1) * group]
                    )
                low_ref[head, rows, :] = grad.astype(jnp.bfloat16)
            key_sum[...] += jnp.dot(low_ref[head], q_head, preferred_element_type=jnp.float32)
            outs.append(
                jnp.dot(
                    keys_t[head * DH : (head + 1) * DH, :],
                    low_ref[head],
                    preferred_element_type=jnp.float32,
                )
            )
        grad_ref[pl.ds(first, block), :PAIR] = jnp.transpose(
            jnp.concatenate(outs, axis=0)
        ).astype(jnp.bfloat16)

    for_blocks(length // block, block, one_block)
    grad_ref[:, PAIR : 2 * PAIR] = key_sum[...].astype(jnp.bfloat16)
    grad_ref[:, 2 * PAIR :] = value_sum[...].astype(jnp.bfloat16)
    for head in range(2):
        turned = strip_ref[head]
        while turned.shape[0] > 1:
            half = turned.shape[0] // 2
            turned = pltpu.roll(turned[:half], half, 1) + turned[half:]
        line_ref[0, head : head + 1, :] = turned


def attention_backward(qkv, place, d, e, inv, heads, token_rows):
    length = qkv.shape[0]
    block = query_block(length)
    pairs = heads // 2
    triple = pl.BlockSpec((length, 3 * PAIR), lambda i: (0, i))
    return pl.pallas_call(
        functools.partial(backward_kernel, block, token_rows),
        grid=(pairs,),
        in_specs=[
            pl.BlockSpec(memory_space=pltpu.SMEM),
            triple,
            pl.BlockSpec((length, PAIR), lambda i: (0, i)),
            pl.BlockSpec((2, length, length), lambda i: (i, 0, 0)),
            pl.BlockSpec((2, 1, length), lambda i: (i, 0, 0)),
        ],
        out_specs=[triple, pl.BlockSpec((1, 2, 2 * length), lambda i: (i, 0, 0))],
        out_shape=[
            jax.ShapeDtypeStruct((length, 3 * heads * DH), jnp.bfloat16),
            jax.ShapeDtypeStruct((pairs, 2, 2 * length), jnp.float32),
        ],
        scratch_shapes=[
            pltpu.VMEM((2, TILE, 2 * length), jnp.float32),
            pltpu.VMEM((2, length, block), jnp.float32),
            pltpu.VMEM((2, length, block), jnp.bfloat16),
            pltpu.VMEM((length, PAIR), jnp.float32),
            pltpu.VMEM((length, PAIR), jnp.float32),
        ],
        compiler_params=pltpu.CompilerParams(vmem_limit_bytes=VMEM_BYTES),
        cost_estimate=NO_COST,
        name="attention_backward",
    )(place, qkv, d, e, inv)


def swap(piece, axis, step):
    return lax.ppermute(piece, axis, [(i, i ^ step) for i in range(lax.axis_size(axis))])


def gather_begin(piece, relay=True):
    count = lax.axis_size("seq")
    steps = (1, 2) if count == 4 and relay else range(1, count)
    return tuple(swap(piece, "seq", step) for step in steps)


def gather_end(piece, near):
    if len(near) != 2:
        return [[part] for part in (piece, *near)]
    first, second = near
    half = piece.shape[0] // 2
    upper = swap(second[:half], "seq", 1)
    lower = swap(first[half:], "seq", 2)
    return [[piece], [first], [second], [upper, lower]]


def joined(parts):
    return jnp.concatenate([part for pieces in parts for part in pieces], axis=0)


def gather_rows(piece):
    return joined(gather_end(piece, gather_begin(piece)))


def low_dot(rows, weights):
    return cols_dot(rows, weights).astype(jnp.bfloat16)


def split_terms(terms):
    count = lax.axis_size("seq")
    size = terms.shape[0] // (count - 1)
    return (terms[: 2 * size], terms[2 * size :]) if count == 4 else (terms, None)


def scatter_begin(far):
    if far is None:
        return ()
    half = far.shape[0] // 2
    return swap(far[:half], "seq", 1), swap(far[half:], "seq", 2)


def scatter_add(near, passing):
    if not passing:
        size = near.shape[0] // (lax.axis_size("seq") - 1)
        return tuple(near[start : start + size] for start in range(0, near.shape[0], size))
    size = near.shape[0] // 2
    upper, lower = (part.astype(jnp.float32) for part in passing)
    first = near[:size].astype(jnp.float32) + jnp.pad(lower, ((size // 2, 0), (0, 0)))
    second = near[size:].astype(jnp.float32) + jnp.pad(upper, ((0, size // 2), (0, 0)))
    return first.astype(jnp.bfloat16), second.astype(jnp.bfloat16)


def scatter_end(sums):
    return tuple(swap(part, "seq", k + 1) for k, part in enumerate(sums))


def add_parts(own, received):
    return own + sum(part.astype(jnp.float32) for part in received)


def scatter_sum(rows, weights):
    size = rows.shape[0] // lax.axis_size("seq")
    near, far = split_terms(low_dot(rows[size:], weights))
    received = scatter_end(scatter_add(near, scatter_begin(far)))
    return add_parts(cols_dot(rows[:size], weights), received)


def seq_sum(values):
    level = [values] + [swap(values, "seq", step) for step in range(1, lax.axis_size("seq"))]
    while len(level) > 1:
        level = [level[i] + level[i + 1] for i in range(0, len(level), 2)]
    return level[0]


def feed_forward_kernel(tile, x_ref, w_ref, act_ref, gelu_ref, slope_ref):
    rows = x_ref.shape[0]
    chunk = min(512, rows)
    for start in range(0, rows, chunk):
        at = slice(start, start + chunk)
        both = jnp.dot(x_ref[at, :], w_ref[...], preferred_element_type=jnp.float32)
        gate, up = both[:, :tile], both[:, tile:]
        square = gate * gate
        tanh = jnp.tanh(GELU_SCALE * gate * (1.0 + GELU_CUBE * square))
        half_up = 0.5 * (1.0 + tanh)
        gelu = gate * half_up
        bend = 0.5 * GELU_SCALE * gate * (1.0 - tanh * tanh) * (1.0 + 3.0 * GELU_CUBE * square)
        act_ref[at, :] = (gelu * up).astype(jnp.bfloat16)
        gelu_ref[at, :] = gelu.astype(jnp.bfloat16)
        slope_ref[at, :] = (up * (half_up + bend)).astype(jnp.bfloat16)


def feed_forward(rows, weights, tile):
    length, model_width = rows.shape
    units = weights.shape[1] // 2
    block = pl.BlockSpec((length, tile), lambda j: (0, j))
    return pl.pallas_call(
        functools.partial(feed_forward_kernel, tile),
        grid=(units // tile,),
        in_specs=[
            pl.BlockSpec((length, model_width), lambda j: (0, 0)),
            pl.BlockSpec((model_width, 2 * tile), lambda j: (0, j)),
        ],
        out_specs=[block, block, block],
        out_shape=[
            jax.ShapeDtypeStruct((length, units), jnp.bfloat16),
            jax.ShapeDtypeStruct((length, units), jnp.bfloat16),
            jax.ShapeDtypeStruct((length, units), jnp.bfloat16),
        ],
        compiler_params=pltpu.CompilerParams(vmem_limit_bytes=VMEM_BYTES),
        cost_estimate=NO_COST,
        name="feed_forward",
    )(rows, weights)


def feed_forward_back_kernel(tile, d_ref, w_ref, gelu_ref, slope_ref, grad_ref):
    rows = d_ref.shape[0]
    chunk = min(512, rows)
    for start in range(0, rows, chunk):
        at = slice(start, start + chunk)
        grad = jnp.dot(d_ref[at, :], w_ref[...], preferred_element_type=jnp.float32)
        grad_ref[at, :tile] = (grad * slope_ref[at, :].astype(jnp.float32)).astype(jnp.bfloat16)
        grad_ref[at, tile:] = (grad * gelu_ref[at, :].astype(jnp.float32)).astype(jnp.bfloat16)


def feed_forward_back(grad_rows, weights, gelu, slope, tile):
    length, model_width = grad_rows.shape
    units = weights.shape[1]
    block = pl.BlockSpec((length, tile), lambda j: (0, j))
    return pl.pallas_call(
        functools.partial(feed_forward_back_kernel, tile),
        grid=(units // tile,),
        in_specs=[
            pl.BlockSpec((length, model_width), lambda j: (0, 0)),
            pl.BlockSpec((model_width, tile), lambda j: (0, j)),
            block,
            block,
        ],
        out_specs=pl.BlockSpec((length, 2 * tile), lambda j: (0, j)),
        out_shape=jax.ShapeDtypeStruct((length, 2 * units), jnp.bfloat16),
        compiler_params=pltpu.CompilerParams(vmem_limit_bytes=VMEM_BYTES),
        cost_estimate=NO_COST,
        name="feed_forward_back",
    )(grad_rows, weights, gelu, slope)


def place_kernel(moves, lengths, block, widths, weighed, place_ref, *refs):
    count = sum(lengths)
    weights = refs[count : count + len(weighed)]
    outs = refs[count + len(weighed) : count + len(weighed) + len(widths)]
    total = jnp.zeros((block, TILE), jnp.float32)
    first = 0
    for step, length in enumerate(lengths):
        pieces = refs[first : first + length]
        first += length
        owner = jnp.bitwise_xor(place_ref[0], step)
        for out, source, target, size in moves:
            at = pl.ds(pl.multiple_of(owner * widths[out] + target, TILE), size)
            part = pieces[0][:, source : source + size]
            if length == 2:
                upper = pl.program_id(0) < pl.num_programs(0) // 2
                part = jnp.where(upper, part, pieces[1][:, source : source + size])
            part = part.astype(jnp.float32)
            outs[out][:, at] = part
            if out in weighed:
                part = part * weights[weighed.index(out)][:, at].astype(jnp.float32)
                for start in range(0, size, TILE):
                    total = total + part[:, start : start + TILE]
    if weighed:
        refs[-1][...] = total


def place_columns(parts, place, moves, widths, weights=()):
    lengths = tuple(len(pieces) for pieces in parts)
    count = lax.axis_size("seq")
    rows, width = parts[0][0].shape
    block = min(64, rows // 2)
    steps = rows // block

    def wide(size):
        return pl.BlockSpec((block, size), lambda i: (i, 0))

    def piece_specs(length):
        if length == 1:
            return [wide(width)]
        half = steps // 2
        return [
            pl.BlockSpec((block, width), lambda i: (jnp.minimum(i, half - 1), 0)),
            pl.BlockSpec((block, width), lambda i: (jnp.maximum(i - half, 0), 0)),
        ]

    whole = [wide(count * size) for size in widths]
    sums = [wide(TILE)] if weights else []
    shapes = [count * size for size in widths] + [TILE] * len(sums)
    weighed = tuple(range(len(weights)))
    return pl.pallas_call(
        functools.partial(place_kernel, moves, lengths, block, widths, weighed),
        grid=(steps,),
        in_specs=[pl.BlockSpec(memory_space=pltpu.SMEM)]
        + [spec for length in lengths for spec in piece_specs(length)]
        + whole[: len(weights)],
        out_specs=whole + sums,
        out_shape=[jax.ShapeDtypeStruct((rows, size), jnp.float32) for size in shapes],
        compiler_params=pltpu.CompilerParams(vmem_limit_bytes=VMEM_BYTES),
        cost_estimate=pl.CostEstimate(
            flops=0, bytes_accessed=8 * rows * sum(shapes), transcendentals=0
        ),
        name="place_columns",
    )(place, *[piece for pieces in parts for piece in pieces], *weights)


def place_far_kernel(moves, half, count, place_ref, upper_ref, lower_ref, *refs):
    weights, outs, sums_ref = refs[:count], refs[2 * count : 3 * count], refs[-1]
    for rows, piece in ((slice(0, half), upper_ref), (slice(half, 2 * half), lower_ref)):
        total = jnp.zeros((half, TILE), jnp.float32)
        for out, source, target, size in moves:
            at = slice(target, target + size)
            part = piece[:, source : source + size].astype(jnp.float32)
            outs[out][rows, at] = part
            part = part * weights[out][rows, at].astype(jnp.float32)
            for start in range(0, size, TILE):
                total = total + part[:, start : start + TILE]
        sums_ref[rows, :] = total


def place_far(halves, place, moves, widths, weights, outs):
    upper, lower = halves
    half, width = upper.shape
    count = len(widths)
    whole = pl.BlockSpec((half, width), lambda i, place_ref: (0, 0))
    column = [
        pl.BlockSpec((2 * half, size), lambda i, place_ref: (0, jnp.bitwise_xor(place_ref[0], 3)))
        for size in widths
    ]
    return pl.pallas_call(
        functools.partial(place_far_kernel, moves, half, count),
        grid_spec=pltpu.PrefetchScalarGridSpec(
            num_scalar_prefetch=1,
            grid=(1,),
            in_specs=[whole, whole] + column + [pl.BlockSpec(memory_space=pl.ANY)] * count,
            out_specs=column + [pl.BlockSpec((2 * half, TILE), lambda i, place_ref: (0, 0))],
        ),
        out_shape=[jax.ShapeDtypeStruct(out.shape, out.dtype) for out in outs]
        + [jax.ShapeDtypeStruct((2 * half, TILE), jnp.float32)],
        input_output_aliases={3 + count + k: k for k in range(count)},
        compiler_params=pltpu.CompilerParams(vmem_limit_bytes=VMEM_BYTES),
        cost_estimate=NO_COST,
        name="place_far",
    )(place, upper, lower, *weights, *outs)


def take_kernel(moves, count, place_ref, *refs):
    out_ref = refs[count]
    for which, source, target, size in moves:
        out_ref[:, source : source + size] = refs[which][:, target : target + size]


def take_columns(place, weights, moves, counts):
    rows = weights[0].shape[0]
    block = min(128, rows)
    width = sum(counts)

    def chosen(count):
        return pl.BlockSpec((block, count), lambda i, place_ref: (i, place_ref[0]))

    return pl.pallas_call(
        functools.partial(take_kernel, moves, len(weights)),
        grid_spec=pltpu.PrefetchScalarGridSpec(
            num_scalar_prefetch=1,
            grid=(rows // block,),
            in_specs=[chosen(count) for count in counts],
            out_specs=pl.BlockSpec((block, width), lambda i, place_ref: (i, 0)),
        ),
        out_shape=jax.ShapeDtypeStruct((rows, width), weights[0].dtype),
        compiler_params=pltpu.CompilerParams(vmem_limit_bytes=VMEM_BYTES),
        cost_estimate=NO_COST,
        name="take_columns",
    )(place, *weights)


def turn_kernel(core_ref, own_in, other_in, own_ref, other_ref):
    own_ref[...] = jnp.transpose(own_in[...])
    other_ref[...] = jnp.transpose(other_in[...])


def turn_halves(rows, core, groups):
    length, width = rows.shape
    size = width // groups

    def chosen(side):
        return pl.BlockSpec(
            (length, size), lambda i, core_ref: (0, 2 * i + jnp.bitwise_xor(core_ref[0], side))
        )

    half = jax.ShapeDtypeStruct((width // 2, length), rows.dtype)
    block = pl.BlockSpec((size, length), lambda i, core_ref: (i, 0))
    return pl.pallas_call(
        turn_kernel,
        grid_spec=pltpu.PrefetchScalarGridSpec(
            num_scalar_prefetch=1,
            grid=(groups // 2,),
            in_specs=[chosen(0), chosen(1)],
            out_specs=[block, block],
        ),
        out_shape=[half, half],
        compiler_params=pltpu.CompilerParams(vmem_limit_bytes=VMEM_BYTES),
        cost_estimate=NO_COST,
        name="turn_halves",
    )(core, rows, rows)


def added_dot_kernel(left_ref, right_ref, added_ref, out_ref):
    rows = left_ref.shape[0]
    chunk = min(512, rows)
    for start in range(0, rows, chunk):
        at = slice(start, start + chunk)
        product = jnp.dot(left_ref[at, :], right_ref[...], preferred_element_type=jnp.float32)
        out_ref[at, :] = (product + added_ref[at, :].astype(jnp.float32)).astype(jnp.bfloat16)


def added_dot(left, right, added):
    rows, depth = left.shape
    width = right.shape[1]
    tile = next(t for t in (512, 256, 128) if width % t == 0)
    column = pl.BlockSpec((rows, tile), lambda j: (0, j))
    return pl.pallas_call(
        added_dot_kernel,
        grid=(width // tile,),
        in_specs=[
            pl.BlockSpec((rows, depth), lambda j: (0, 0)),
            pl.BlockSpec((depth, tile), lambda j: (0, j)),
            column,
        ],
        out_specs=column,
        out_shape=jax.ShapeDtypeStruct((rows, width), jnp.bfloat16),
        compiler_params=pltpu.CompilerParams(vmem_limit_bytes=VMEM_BYTES),
        cost_estimate=NO_COST,
        name="added_dot",
    )(left, right, added)


def both(*values):
    return lax.optimization_barrier(values)


def on_device(
    tokens,
    segments,
    buckets,
    w_query,
    w_key,
    w_value,
    w_attn_out,
    gain_attn,
    rel_table,
    w_gate,
    w_up,
    w_down,
    gain_ffn,
    out_grad,
):
    token_rows = tokens.shape[1]
    model_width = tokens.shape[2]
    ffn_width = w_gate.shape[1]
    segment_row = segments[0]
    row_length = segment_row.shape[0]
    seq_count = lax.axis_size("seq")
    fsdp_count = lax.axis_size("fsdp")
    seq_place = lax.axis_index("seq")
    fsdp_place = lax.axis_index("fsdp")
    place = seq_place.astype(jnp.int32).reshape(1)
    head_count = model_width // seq_count // DH
    column_count = model_width // seq_count
    unit_count = ffn_width // seq_count

    tile = 256 if unit_count % 256 == 0 else 128
    pairs = head_count // 2

    def gather_weights(piece):
        return lax.all_gather(piece, "fsdp", axis=0, tiled=True)

    qkv_moves = [
        (which, (3 * pair + which) * PAIR, pair * PAIR, PAIR)
        for pair in range(pairs)
        for which in range(3)
    ] + [(3, 3 * column_count, 0, column_count)]
    unit_moves = [
        (which, (2 * block + which) * tile, block * tile, tile)
        for block in range(unit_count // tile)
        for which in range(2)
    ]
    attn_part = take_columns(
        place, (w_query, w_key, w_value, w_attn_out), qkv_moves, [column_count] * 4
    )
    attn_w = gather_weights(attn_part)
    gains = lax.all_gather(jnp.stack([gain_attn, gain_ffn]), "fsdp", axis=1, tiled=True)
    qkv_w = attn_w[:, : 3 * column_count]
    output_w = attn_w[:, 3 * column_count :]

    table_rows = jnp.pad(buckets[::-1], (0, 1), constant_values=-1)
    bucket_table = (
        table_rows[:, None] == jnp.arange(rel_table.shape[1], dtype=jnp.int32)[None, :]
    ).astype(jnp.float32)
    local_table = lax.dynamic_slice_in_dim(rel_table, seq_place * head_count, head_count, 0)
    bias_line = jnp.dot(local_table, jnp.transpose(bucket_table), precision=PRECISE)
    bias_line = bias_line.reshape(head_count // 2, 2, 2 * row_length)
    segment_wide = jnp.broadcast_to(segment_row[:, None], (row_length, TILE))

    stream = tokens[0].astype(jnp.float32)
    scale_attn = lax.rsqrt(jnp.mean(stream * stream, axis=-1, keepdims=True) + EPSILON)
    normed_attn = stream * scale_attn
    upstream = out_grad[0].astype(jnp.float32)

    stream_near = gather_begin(tokens[0])
    stream_near, gains = both(stream_near, gains)
    attn_gain = gains[0].astype(jnp.float32)
    ffn_gain = gains[1].astype(jnp.float32)
    stream_rows = joined(gather_end(tokens[0], stream_near))
    gate_up_part = take_columns(place, (w_gate, w_up), unit_moves, [unit_count] * 2)
    gate_up_part, stream_rows = both(gate_up_part, stream_rows)
    gate_up_w = gather_weights(gate_up_part)
    stream_rows = stream_rows.astype(jnp.float32)
    rows_scale = lax.rsqrt(jnp.mean(stream_rows * stream_rows, axis=-1, keepdims=True) + EPSILON)
    attn_rows = (stream_rows * rows_scale * attn_gain).astype(jnp.bfloat16)
    ff_grad_rows = gather_rows(out_grad[0])
    attn_rows, ff_grad_rows = both(attn_rows, ff_grad_rows)

    qkv = jnp.dot(attn_rows, qkv_w, preferred_element_type=jnp.float32).astype(jnp.bfloat16)
    down_part, qkv = both(
        lax.dynamic_slice_in_dim(w_down, seq_place * unit_count, unit_count, 1), qkv
    )
    down_w = gather_weights(down_part)
    context, exponents, inverse = attention_forward(
        qkv, place, segments, segment_wide, bias_line, head_count, token_rows
    )

    attn_out = scatter_sum(context, output_w)
    chips = fsdp_count // 2
    core = (fsdp_place % 2).astype(jnp.int32).reshape(1)
    groups = [[2 * chip + side for chip in range(chips)] for side in range(2)]

    def scatter_grads(grads, axis_index_groups=None):
        return lax.psum_scatter(
            grads,
            "fsdp",
            scatter_dimension=0,
            tiled=True,
            axis_index_groups=axis_index_groups,
        )

    resid = stream + attn_out
    scale_ffn = lax.rsqrt(jnp.mean(resid * resid, axis=-1, keepdims=True) + EPSILON)
    normed_ffn = resid * scale_ffn
    ffn_rows = gather_rows((normed_ffn * ffn_gain).astype(jnp.bfloat16))

    hidden, gelu, slope = feed_forward(ffn_rows, gate_up_w, tile)

    down_grad = rows_dot(ff_grad_rows, hidden).astype(jnp.bfloat16)
    ffn_own, ffn_other = turn_halves(ffn_rows, core, fsdp_count)
    down_owned = scatter_grads(down_grad)
    down_grad, hidden, gelu, ffn_own, ffn_other = both(down_grad, hidden, gelu, ffn_own, ffn_other)
    away = row_length // seq_count
    passed = 3 * away if seq_count == 4 else row_length
    ff_far = low_dot(hidden[passed:], down_w) if seq_count == 4 else None
    ff_far, hidden, gelu = both(ff_far, hidden, gelu)
    ff_passing = scatter_begin(ff_far)
    unit_grad = feed_forward_back(ff_grad_rows, down_w, gelu, slope, tile)
    unit_far = low_dot(unit_grad[passed:], gate_up_w) if seq_count == 4 else None
    unit_far, unit_grad, ff_passing = both(unit_far, unit_grad, ff_passing)
    unit_passing = scatter_begin(unit_far)
    unit_near = low_dot(unit_grad[away:passed], gate_up_w)
    gate_up_away = jnp.dot(
        ffn_other, unit_grad, preferred_element_type=jnp.float32
    ).astype(jnp.bfloat16)
    unit_near, unit_grad, unit_passing, gate_up_away, hidden = both(
        unit_near, unit_grad, unit_passing, gate_up_away, hidden
    )
    unit_sums = scatter_add(unit_near, unit_passing)
    unit_sums, unit_grad = both(unit_sums, unit_grad)
    unit_parts = scatter_end(unit_sums)
    gate_up_added = swap(gate_up_away, "fsdp", 1)
    gate_up_grad = added_dot(ffn_own, unit_grad, gate_up_added)
    ffn_in_own = cols_dot(unit_grad[:away], gate_up_w)
    ffn_in_own, gate_up_grad, unit_parts = both(ffn_in_own, gate_up_grad, unit_parts)
    gate_up_owned = scatter_grads(gate_up_grad, groups)
    ffn_in_grad = add_parts(ffn_in_own, unit_parts)

    resid_grad = upstream + norm_back(ffn_in_grad * ffn_gain, normed_ffn, scale_ffn)
    attn_grad = resid_grad.astype(jnp.bfloat16)
    attn_grad, hidden, down_owned = both(attn_grad, hidden, down_owned)
    attn_grad_rows = gather_rows(attn_grad)
    ff_near = low_dot(hidden[away:passed], down_w)
    ff_sums = scatter_add(ff_near, ff_passing)
    attn_grad_rows, ff_sums, down_owned = both(attn_grad_rows, ff_sums, down_owned)
    context_grad = jnp.dot(
        attn_grad_rows, output_w, preferred_element_type=jnp.float32
    ).astype(jnp.bfloat16)
    ff_parts = scatter_end(ff_sums)
    down_near = gather_begin(down_owned, relay=False)
    qkv_grad, line_grad = attention_backward(
        qkv, place, context_grad, exponents, inverse, head_count, token_rows
    )
    attn_grads = rows_dot(attn_rows, qkv_grad).astype(jnp.bfloat16)
    attn_grads, context, qkv_grad, ff_parts, down_near, attn_grad_rows, gate_up_owned = both(
        attn_grads, context, qkv_grad, ff_parts, down_near, attn_grad_rows, gate_up_owned
    )
    attn_owned = scatter_grads(attn_grads)
    gate_up_near = gather_begin(gate_up_owned)
    output_own, output_other = turn_halves(attn_grad_rows, core, fsdp_count)
    output_away = jnp.dot(
        output_other, context, preferred_element_type=jnp.float32
    ).astype(jnp.bfloat16)
    qkv_terms = low_dot(qkv_grad[away:], qkv_w)
    qkv_terms, qkv_grad, output_away, output_own, down_near, hidden = both(
        qkv_terms, qkv_grad, output_away, output_own, down_near, hidden
    )
    qkv_near, qkv_far = split_terms(qkv_terms)
    qkv_passing = scatter_begin(qkv_far)
    output_added = swap(output_away, "fsdp", 1)
    attn_in_own = cols_dot(qkv_grad[:away], qkv_w)
    output_grad = added_dot(output_own, context, output_added)
    attn_in_own, output_grad, qkv_passing, hidden, ffn_in_grad, gate_up_near, down_near = both(
        attn_in_own, output_grad, qkv_passing, hidden, ffn_in_grad, gate_up_near, down_near
    )
    output_owned = scatter_grads(output_grad, groups)
    qkv_sums = scatter_add(qkv_near, qkv_passing)
    qkv_sums, gate_up_near, down_near = both(qkv_sums, gate_up_near, down_near)
    attn_in_parts = scatter_end(qkv_sums)
    gate_up_pieces = gather_end(gate_up_owned, gate_up_near)
    down_pieces = gather_end(down_owned, down_near)
    ff_out = add_parts(cols_dot(hidden[:away], down_w), ff_parts)
    result = resid + ff_out
    (down_out,) = place_columns(down_pieces, place, [(0, 0, 0, unit_count)], [unit_count])
    own_segments = lax.dynamic_slice_in_dim(segment_row, seq_place * token_rows, token_rows, 0)
    valid = (own_segments >= 0).astype(jnp.float32)
    stat_terms = jnp.stack(
        [
            jnp.sum(valid * jnp.sum(result * result, axis=-1)),
            jnp.sum(valid * jnp.sum(attn_out * attn_out, axis=-1)),
            jnp.sum(valid * jnp.sum(ff_out * ff_out, axis=-1)),
            jnp.sum(valid),
        ]
    )
    table_part = jnp.dot(
        line_grad.reshape(head_count, 2 * row_length), bucket_table, precision=PRECISE
    )
    full_table = lax.dynamic_update_slice_in_dim(
        jnp.zeros(rel_table.shape, jnp.float32), table_part, seq_place * head_count, 0
    )
    packed = jnp.concatenate([full_table.reshape(-1), jnp.pad(stat_terms, (0, TILE - 4))])
    summed = jnp.sum(lax.all_gather(packed.reshape(-1, TILE), "fsdp"), axis=0)
    attn_owned, result, summed, down_out, gate_up_pieces, attn_in_parts = both(
        attn_owned, result, summed, down_out, gate_up_pieces, attn_in_parts
    )
    attn_near = gather_begin(attn_owned)
    attn_in_grad = add_parts(attn_in_own, attn_in_parts)
    stream_grad = resid_grad + norm_back(attn_in_grad * attn_gain, normed_attn, scale_attn)
    stream_grad = stream_grad.astype(jnp.bfloat16)
    gate_out, up_out, ffn_sums = place_columns(
        gate_up_pieces, place, unit_moves, [unit_count] * 2, (w_gate, w_up)
    )
    attn_near, stream_grad, gate_out, up_out, output_owned = both(
        attn_near, stream_grad, gate_out, up_out, output_owned
    )
    attn_pieces = gather_end(attn_owned, attn_near)
    output_near = gather_begin(output_owned, relay=False)
    attn_weights, attn_widths = (w_query, w_key, w_value), [column_count] * 3
    attn_outs = place_columns(
        attn_pieces[:3] if seq_count == 4 else attn_pieces,
        place,
        qkv_moves[:-1],
        attn_widths,
        attn_weights,
    )
    attn_pieces, output_near, summed, attn_outs = both(
        attn_pieces, output_near, summed, attn_outs
    )
    summed = seq_sum(summed).reshape(-1)
    *attn_outs, attn_sums = attn_outs
    if seq_count == 4:
        *attn_outs, far_sums = place_far(
            attn_pieces[3], place, qkv_moves[:-1], attn_widths, attn_weights, attn_outs
        )
        attn_sums = attn_sums + far_sums
    query_out, key_out, value_out = attn_outs
    (output_out,) = place_columns(
        gather_end(output_owned, output_near), place, [(0, 0, 0, column_count)], [column_count]
    )
    gain_attn_grad = jnp.sum(attn_sums, axis=1) / gain_attn.astype(jnp.float32)
    gain_ffn_grad = jnp.sum(ffn_sums, axis=1) / gain_ffn.astype(jnp.float32)
    stat_totals = summed[rel_table.size : rel_table.size + 4]
    rms_stats = jnp.sqrt(stat_totals[0:3] / (stat_totals[3] * model_width))
    table_share = rel_table.shape[0] // fsdp_count
    rel_table_grad = lax.dynamic_slice_in_dim(
        summed[: rel_table.size].reshape(rel_table.shape),
        fsdp_place * table_share,
        table_share,
        0,
    )
    return (
        result.astype(jnp.bfloat16)[None],
        stream_grad[None],
        query_out,
        key_out,
        value_out,
        output_out,
        gain_attn_grad,
        rel_table_grad,
        gate_out,
        up_out,
        down_out,
        gain_ffn_grad,
        rms_stats,
    )


def solution(mesh):
    in_specs = (
        P("fsdp", "seq", None),
        P("fsdp", None),
        P(),
        P("fsdp", None),
        P("fsdp", None),
        P("fsdp", None),
        P("fsdp", None),
        P("fsdp"),
        P(),
        P("fsdp", None),
        P("fsdp", None),
        P("fsdp", None),
        P("fsdp"),
        P("fsdp", "seq", None),
    )
    out_specs = (
        P("fsdp", "seq", None),
        P("fsdp", "seq", None),
        P("fsdp", None),
        P("fsdp", None),
        P("fsdp", None),
        P("fsdp", None),
        P("fsdp"),
        P("fsdp", None),
        P("fsdp", None),
        P("fsdp", None),
        P("fsdp", None),
        P("fsdp"),
        P(),
    )
    return jax.shard_map(
        on_device, mesh=mesh, in_specs=in_specs, out_specs=out_specs, check_vma=False
    )
```

```python
import functools

import jax
import jax.numpy as jnp
from jax import lax
from jax.experimental import pallas as pl
from jax.experimental.pallas import tpu as pltpu
from jax.sharding import PartitionSpec as P

DH = 64


EPSILON = 1e-06
PRECISE = lax.Precision.HIGHEST
MASKED_SCORE = -1e30
TILE = 128
PAIR = 2 * DH
GELU_SCALE = 0.7978845608
GELU_CUBE = 0.044715
NO_COST = pl.CostEstimate(flops=0, bytes_accessed=0, transcendentals=0)
VMEM_BYTES = 56 * 1024 * 1024


def rows_dot(left, right):
    return lax.dot_general(
        left, right, (((0,), (0,)), ((), ())), preferred_element_type=jnp.float32
    )


def cols_dot(left, right):
    return lax.dot_general(
        left, right, (((1,), (1,)), ((), ())), preferred_element_type=jnp.float32
    )


def norm_back(grad_hat, normed, scale):
    return scale * (grad_hat - normed * jnp.mean(grad_hat * normed, axis=-1, keepdims=True))


def half_lanes(shape, which):
    lane = lax.broadcasted_iota(jnp.int32, shape, 1)
    return (lane < DH) if which == 0 else (lane >= DH)


def fold_rows(tile):
    return jnp.sum(tile.reshape(tile.shape[0] // 8, 8, tile.shape[1]), axis=0)


def query_block(length):
    return min(length, max(256, 2**20 // length))


def whole_place(row, token_rows, place):
    return jnp.bitwise_xor(row // token_rows, place) * token_rows + row % token_rows


def bias_offsets(first, block, length, token_rows, place, tile):
    reach = length - TILE
    key_place = whole_place(tile * TILE, token_rows, place)
    group = min(block, token_rows)
    return [
        pl.multiple_of(
            whole_place(first + start, token_rows, place) + (reach - key_place), TILE
        )
        for start in range(0, block, group)
    ], group


def forward_kernel(
    block,
    token_rows,
    place_ref,
    qkv_ref,
    row_ref,
    col_ref,
    bias_ref,
    ctx_ref,
    e_ref,
    inv_ref,
    strip_ref,
    score_ref,
):
    length = qkv_ref.shape[0]
    q_ref = qkv_ref.at[:, :PAIR]
    k_ref = qkv_ref.at[:, PAIR : 2 * PAIR]
    v_ref = qkv_ref.at[:, 2 * PAIR :]
    tiles = length // TILE
    width = 2 * length
    place = place_ref[0]
    group = min(block, token_rows)
    values_t = jnp.transpose(v_ref[...])
    for head in range(2):
        wide = jnp.broadcast_to(bias_ref[0, head : head + 1, :], (TILE, width))
        strip_ref[head] = pltpu.roll(wide, width - (TILE - 1), 1, stride=1, stride_axis=0)

    def one_block(first):
        q_block = q_ref[pl.ds(first, block), :]
        segment_q = jnp.concatenate(
            [
                row_ref[
                    :,
                    pl.ds(
                        pl.multiple_of(whole_place(first + start, token_rows, place), TILE), group
                    ),
                ]
                for start in range(0, block, group)
            ],
            axis=1,
        )
        outs = []
        for head in range(2):
            q_head = jnp.where(half_lanes(q_block.shape, head), q_block, jnp.zeros_like(q_block))
            raw = cols_dot(k_ref[...], q_head)
            highest = jnp.full((8, block), -jnp.inf, jnp.float32)
            for tile in range(tiles):
                rows = slice(tile * TILE, (tile + 1) * TILE)
                offsets, _ = bias_offsets(first, block, length, token_rows, place, tile)
                bias = jnp.concatenate(
                    [strip_ref[head, :, pl.ds(offset, group)] for offset in offsets], axis=1
                )
                key_place = whole_place(tile * TILE, token_rows, place)
                segment_k = col_ref[pl.ds(pl.multiple_of(key_place, TILE), TILE), :]
                segment_k = jnp.concatenate([segment_k] * (block // TILE), axis=1)
                score = jnp.where(segment_k == segment_q, raw[rows, :] + bias, MASKED_SCORE)
                score_ref[head, rows, :] = score
                highest = jnp.maximum(
                    highest, jnp.max(score.reshape(TILE // 8, 8, block), axis=0)
                )
            top = jnp.max(highest, axis=0, keepdims=True)
            total = jnp.zeros((8, block), jnp.float32)
            for tile in range(tiles):
                rows = slice(tile * TILE, (tile + 1) * TILE)
                exponent = jnp.exp(score_ref[head, rows, :] - top)
                total = total + fold_rows(exponent)
                e_ref[head, rows, pl.ds(first, block)] = exponent.astype(jnp.bfloat16)
            inverse = 1.0 / jnp.sum(total, axis=0, keepdims=True)
            inv_ref[head, :, pl.ds(first, block)] = inverse
            context = jnp.dot(
                values_t[head * DH : (head + 1) * DH, :],
                e_ref[head, :, pl.ds(first, block)],
                preferred_element_type=jnp.float32,
            )
            outs.append(context * inverse)
        ctx_ref[pl.ds(first, block), :] = jnp.transpose(jnp.concatenate(outs, axis=0)).astype(
            jnp.bfloat16
        )

    for_blocks(length // block, block, one_block)


def for_blocks(count, block, body):
    if count == 1:
        body(0)
        return

    def step(index, carry):
        body(pl.multiple_of(index * block, block))
        return carry

    lax.fori_loop(0, count, step, 0)


def attention_forward(qkv, place, segment_row, segment_wide, bias_line, heads, token_rows):
    length = qkv.shape[0]
    block = query_block(length)
    pairs = heads // 2
    return pl.pallas_call(
        functools.partial(forward_kernel, block, token_rows),
        grid=(pairs,),
        in_specs=[
            pl.BlockSpec(memory_space=pltpu.SMEM),
            pl.BlockSpec((length, 3 * PAIR), lambda i: (0, i)),
            pl.BlockSpec((1, length), lambda i: (0, 0)),
            pl.BlockSpec((length, TILE), lambda i: (0, 0)),
            pl.BlockSpec((1, 2, 2 * length), lambda i: (i, 0, 0)),
        ],
        out_specs=[
            pl.BlockSpec((length, PAIR), lambda i: (0, i)),
            pl.BlockSpec((2, length, length), lambda i: (i, 0, 0)),
            pl.BlockSpec((2, 1, length), lambda i: (i, 0, 0)),
        ],
        out_shape=[
            jax.ShapeDtypeStruct((length, heads * DH), jnp.bfloat16),
            jax.ShapeDtypeStruct((heads, length, length), jnp.bfloat16),
            jax.ShapeDtypeStruct((heads, 1, length), jnp.float32),
        ],
        scratch_shapes=[
            pltpu.VMEM((2, TILE, 2 * length), jnp.float32),
            pltpu.VMEM((2, length, block), jnp.float32),
        ],
        compiler_params=pltpu.CompilerParams(vmem_limit_bytes=VMEM_BYTES),
        cost_estimate=NO_COST,
        name="attention_forward",
    )(place, qkv, segment_row, segment_wide, bias_line)


def backward_kernel(
    block,
    token_rows,
    place_ref,
    qkv_ref,
    d_ref,
    e_ref,
    inv_ref,
    grad_ref,
    line_ref,
    strip_ref,
    prob_ref,
    low_ref,
    key_sum,
    value_sum,
):
    length = qkv_ref.shape[0]
    q_ref = qkv_ref.at[:, :PAIR]
    k_ref = qkv_ref.at[:, PAIR : 2 * PAIR]
    v_ref = qkv_ref.at[:, 2 * PAIR :]
    tiles = length // TILE
    place = place_ref[0]
    keys_t = jnp.transpose(k_ref[...])
    strip_ref[...] = jnp.zeros_like(strip_ref)
    key_sum[...] = jnp.zeros_like(key_sum)
    value_sum[...] = jnp.zeros_like(value_sum)

    def one_block(first):
        q_block = q_ref[pl.ds(first, block), :]
        d_block = d_ref[pl.ds(first, block), :]
        outs = []
        for head in range(2):
            mask = half_lanes(q_block.shape, head)
            q_head = jnp.where(mask, q_block, jnp.zeros_like(q_block))
            inverse = inv_ref[head, :, pl.ds(first, block)]
            scale = jnp.transpose(jnp.broadcast_to(inverse, (PAIR, block)))
            d_head = jnp.where(mask, d_block.astype(jnp.float32) * scale, 0.0)
            d_head = d_head.astype(jnp.bfloat16)
            prob_ref[head] = cols_dot(v_ref[...], d_head)
            value_sum[...] += jnp.dot(
                e_ref[head, :, pl.ds(first, block)], d_head, preferred_element_type=jnp.float32
            )
            total = jnp.zeros((8, block), jnp.float32)
            for tile in range(tiles):
                rows = slice(tile * TILE, (tile + 1) * TILE)
                exponent = e_ref[head, rows, pl.ds(first, block)].astype(jnp.float32)
                total = total + fold_rows(exponent * prob_ref[head, rows, :])
            centre = jnp.sum(total, axis=0, keepdims=True) * inverse
            for tile in range(tiles):
                rows = slice(tile * TILE, (tile + 1) * TILE)
                exponent = e_ref[head, rows, pl.ds(first, block)].astype(jnp.float32)
                grad = exponent * (prob_ref[head, rows, :] - centre)
                offsets, group = bias_offsets(first, block, length, token_rows, place, tile)
                for part, offset in enumerate(offsets):
                    at = pl.ds(offset, group)
                    strip_ref[head, :, at] = (
                        strip_ref[head, :, at] + grad[:, part * group : (part + 1) * group]
                    )
                low_ref[head, rows, :] = grad.astype(jnp.bfloat16)
            key_sum[...] += jnp.dot(low_ref[head], q_head, preferred_element_type=jnp.float32)
            outs.append(
                jnp.dot(
                    keys_t[head * DH : (head + 1) * DH, :],
                    low_ref[head],
                    preferred_element_type=jnp.float32,
                )
            )
        grad_ref[pl.ds(first, block), :PAIR] = jnp.transpose(
            jnp.concatenate(outs, axis=0)
        ).astype(jnp.bfloat16)

    for_blocks(length // block, block, one_block)
    grad_ref[:, PAIR : 2 * PAIR] = key_sum[...].astype(jnp.bfloat16)
    grad_ref[:, 2 * PAIR :] = value_sum[...].astype(jnp.bfloat16)
    for head in range(2):
        turned = strip_ref[head]
        while turned.shape[0] > 1:
            half = turned.shape[0] // 2
            turned = pltpu.roll(turned[:half], half, 1) + turned[half:]
        line_ref[0, head : head + 1, :] = turned


def attention_backward(qkv, place, d, e, inv, heads, token_rows):
    length = qkv.shape[0]
    block = query_block(length)
    pairs = heads // 2
    triple = pl.BlockSpec((length, 3 * PAIR), lambda i: (0, i))
    return pl.pallas_call(
        functools.partial(backward_kernel, block, token_rows),
        grid=(pairs,),
        in_specs=[
            pl.BlockSpec(memory_space=pltpu.SMEM),
            triple,
            pl.BlockSpec((length, PAIR), lambda i: (0, i)),
            pl.BlockSpec((2, length, length), lambda i: (i, 0, 0)),
            pl.BlockSpec((2, 1, length), lambda i: (i, 0, 0)),
        ],
        out_specs=[triple, pl.BlockSpec((1, 2, 2 * length), lambda i: (i, 0, 0))],
        out_shape=[
            jax.ShapeDtypeStruct((length, 3 * heads * DH), jnp.bfloat16),
            jax.ShapeDtypeStruct((pairs, 2, 2 * length), jnp.float32),
        ],
        scratch_shapes=[
            pltpu.VMEM((2, TILE, 2 * length), jnp.float32),
            pltpu.VMEM((2, length, block), jnp.float32),
            pltpu.VMEM((2, length, block), jnp.bfloat16),
            pltpu.VMEM((length, PAIR), jnp.float32),
            pltpu.VMEM((length, PAIR), jnp.float32),
        ],
        compiler_params=pltpu.CompilerParams(vmem_limit_bytes=VMEM_BYTES),
        cost_estimate=NO_COST,
        name="attention_backward",
    )(place, qkv, d, e, inv)


def swap(piece, axis, step):
    return lax.ppermute(piece, axis, [(i, i ^ step) for i in range(lax.axis_size(axis))])


def gather_begin(piece, relay=True):
    count = lax.axis_size("seq")
    steps = (1, 2) if count == 4 and relay else range(1, count)
    return tuple(swap(piece, "seq", step) for step in steps)


def gather_end(piece, near):
    if len(near) != 2:
        return [[part] for part in (piece, *near)]
    first, second = near
    half = piece.shape[0] // 2
    upper = swap(second[:half], "seq", 1)
    lower = swap(first[half:], "seq", 2)
    return [[piece], [first], [second], [upper, lower]]


def joined(parts):
    return jnp.concatenate([part for pieces in parts for part in pieces], axis=0)


def gather_rows(piece):
    return joined(gather_end(piece, gather_begin(piece)))


def low_dot(rows, weights):
    return cols_dot(rows, weights).astype(jnp.bfloat16)


def split_terms(terms):
    count = lax.axis_size("seq")
    size = terms.shape[0] // (count - 1)
    return (terms[: 2 * size], terms[2 * size :]) if count == 4 else (terms, None)


def scatter_begin(far):
    if far is None:
        return ()
    half = far.shape[0] // 2
    return swap(far[:half], "seq", 1), swap(far[half:], "seq", 2)


def scatter_add(near, passing):
    if not passing:
        size = near.shape[0] // (lax.axis_size("seq") - 1)
        return tuple(near[start : start + size] for start in range(0, near.shape[0], size))
    size = near.shape[0] // 2
    upper, lower = (part.astype(jnp.float32) for part in passing)
    first = near[:size].astype(jnp.float32) + jnp.pad(lower, ((size // 2, 0), (0, 0)))
    second = near[size:].astype(jnp.float32) + jnp.pad(upper, ((0, size // 2), (0, 0)))
    return first.astype(jnp.bfloat16), second.astype(jnp.bfloat16)


def scatter_end(sums):
    return tuple(swap(part, "seq", k + 1) for k, part in enumerate(sums))


def add_parts(own, received):
    return own + sum(part.astype(jnp.float32) for part in received)


def scatter_sum(rows, weights):
    size = rows.shape[0] // lax.axis_size("seq")
    near, far = split_terms(low_dot(rows[size:], weights))
    received = scatter_end(scatter_add(near, scatter_begin(far)))
    return add_parts(cols_dot(rows[:size], weights), received)


def seq_sum(values):
    level = [values] + [swap(values, "seq", step) for step in range(1, lax.axis_size("seq"))]
    while len(level) > 1:
        level = [level[i] + level[i + 1] for i in range(0, len(level), 2)]
    return level[0]


def feed_forward_kernel(tile, x_ref, w_ref, act_ref, gelu_ref, slope_ref):
    rows = x_ref.shape[0]
    chunk = min(512, rows)
    for start in range(0, rows, chunk):
        at = slice(start, start + chunk)
        both = jnp.dot(x_ref[at, :], w_ref[...], preferred_element_type=jnp.float32)
        gate, up = both[:, :tile], both[:, tile:]
        square = gate * gate
        tanh = jnp.tanh(GELU_SCALE * gate * (1.0 + GELU_CUBE * square))
        half_up = 0.5 * (1.0 + tanh)
        gelu = gate * half_up
        bend = 0.5 * GELU_SCALE * gate * (1.0 - tanh * tanh) * (1.0 + 3.0 * GELU_CUBE * square)
        act_ref[at, :] = (gelu * up).astype(jnp.bfloat16)
        gelu_ref[at, :] = gelu.astype(jnp.bfloat16)
        slope_ref[at, :] = (up * (half_up + bend)).astype(jnp.bfloat16)


def feed_forward(rows, weights, tile):
    length, model_width = rows.shape
    units = weights.shape[1] // 2
    block = pl.BlockSpec((length, tile), lambda j: (0, j))
    return pl.pallas_call(
        functools.partial(feed_forward_kernel, tile),
        grid=(units // tile,),
        in_specs=[
            pl.BlockSpec((length, model_width), lambda j: (0, 0)),
            pl.BlockSpec((model_width, 2 * tile), lambda j: (0, j)),
        ],
        out_specs=[block, block, block],
        out_shape=[
            jax.ShapeDtypeStruct((length, units), jnp.bfloat16),
            jax.ShapeDtypeStruct((length, units), jnp.bfloat16),
            jax.ShapeDtypeStruct((length, units), jnp.bfloat16),
        ],
        compiler_params=pltpu.CompilerParams(vmem_limit_bytes=VMEM_BYTES),
        cost_estimate=NO_COST,
        name="feed_forward",
    )(rows, weights)


def feed_forward_back_kernel(tile, d_ref, w_ref, gelu_ref, slope_ref, grad_ref):
    rows = d_ref.shape[0]
    chunk = min(512, rows)
    for start in range(0, rows, chunk):
        at = slice(start, start + chunk)
        grad = jnp.dot(d_ref[at, :], w_ref[...], preferred_element_type=jnp.float32)
        grad_ref[at, :tile] = (grad * slope_ref[at, :].astype(jnp.float32)).astype(jnp.bfloat16)
        grad_ref[at, tile:] = (grad * gelu_ref[at, :].astype(jnp.float32)).astype(jnp.bfloat16)


def feed_forward_back(grad_rows, weights, gelu, slope, tile):
    length, model_width = grad_rows.shape
    units = weights.shape[1]
    block = pl.BlockSpec((length, tile), lambda j: (0, j))
    return pl.pallas_call(
        functools.partial(feed_forward_back_kernel, tile),
        grid=(units // tile,),
        in_specs=[
            pl.BlockSpec((length, model_width), lambda j: (0, 0)),
            pl.BlockSpec((model_width, tile), lambda j: (0, j)),
            block,
            block,
        ],
        out_specs=pl.BlockSpec((length, 2 * tile), lambda j: (0, j)),
        out_shape=jax.ShapeDtypeStruct((length, 2 * units), jnp.bfloat16),
        compiler_params=pltpu.CompilerParams(vmem_limit_bytes=VMEM_BYTES),
        cost_estimate=NO_COST,
        name="feed_forward_back",
    )(grad_rows, weights, gelu, slope)


def place_kernel(moves, lengths, block, widths, weighed, place_ref, *refs):
    count = sum(lengths)
    weights = refs[count : count + len(weighed)]
    outs = refs[count + len(weighed) : count + len(weighed) + len(widths)]
    total = jnp.zeros((block, TILE), jnp.float32)
    first = 0
    for step, length in enumerate(lengths):
        pieces = refs[first : first + length]
        first += length
        owner = jnp.bitwise_xor(place_ref[0], step)
        for out, source, target, size in moves:
            at = pl.ds(pl.multiple_of(owner * widths[out] + target, TILE), size)
            part = pieces[0][:, source : source + size]
            if length == 2:
                upper = pl.program_id(0) < pl.num_programs(0) // 2
                part = jnp.where(upper, part, pieces[1][:, source : source + size])
            part = part.astype(jnp.float32)
            outs[out][:, at] = part
            if out in weighed:
                part = part * weights[weighed.index(out)][:, at].astype(jnp.float32)
                for start in range(0, size, TILE):
                    total = total + part[:, start : start + TILE]
    if weighed:
        refs[-1][...] = total


def place_columns(parts, place, moves, widths, weights=()):
    lengths = tuple(len(pieces) for pieces in parts)
    count = lax.axis_size("seq")
    rows, width = parts[0][0].shape
    block = min(64, rows // 2)
    steps = rows // block

    def wide(size):
        return pl.BlockSpec((block, size), lambda i: (i, 0))

    def piece_specs(length):
        if length == 1:
            return [wide(width)]
        half = steps // 2
        return [
            pl.BlockSpec((block, width), lambda i: (jnp.minimum(i, half - 1), 0)),
            pl.BlockSpec((block, width), lambda i: (jnp.maximum(i - half, 0), 0)),
        ]

    whole = [wide(count * size) for size in widths]
    sums = [wide(TILE)] if weights else []
    shapes = [count * size for size in widths] + [TILE] * len(sums)
    weighed = tuple(range(len(weights)))
    return pl.pallas_call(
        functools.partial(place_kernel, moves, lengths, block, widths, weighed),
        grid=(steps,),
        in_specs=[pl.BlockSpec(memory_space=pltpu.SMEM)]
        + [spec for length in lengths for spec in piece_specs(length)]
        + whole[: len(weights)],
        out_specs=whole + sums,
        out_shape=[jax.ShapeDtypeStruct((rows, size), jnp.float32) for size in shapes],
        compiler_params=pltpu.CompilerParams(vmem_limit_bytes=VMEM_BYTES),
        cost_estimate=pl.CostEstimate(
            flops=0, bytes_accessed=8 * rows * sum(shapes), transcendentals=0
        ),
        name="place_columns",
    )(place, *[piece for pieces in parts for piece in pieces], *weights)


def take_kernel(moves, count, place_ref, *refs):
    out_ref = refs[count]
    for which, source, target, size in moves:
        out_ref[:, source : source + size] = refs[which][:, target : target + size]


def take_columns(place, weights, moves, counts):
    rows = weights[0].shape[0]
    block = min(128, rows)
    width = sum(counts)

    def chosen(count):
        return pl.BlockSpec((block, count), lambda i, place_ref: (i, place_ref[0]))

    return pl.pallas_call(
        functools.partial(take_kernel, moves, len(weights)),
        grid_spec=pltpu.PrefetchScalarGridSpec(
            num_scalar_prefetch=1,
            grid=(rows // block,),
            in_specs=[chosen(count) for count in counts],
            out_specs=pl.BlockSpec((block, width), lambda i, place_ref: (i, 0)),
        ),
        out_shape=jax.ShapeDtypeStruct((rows, width), weights[0].dtype),
        compiler_params=pltpu.CompilerParams(vmem_limit_bytes=VMEM_BYTES),
        cost_estimate=NO_COST,
        name="take_columns",
    )(place, *weights)


def turn_kernel(core_ref, own_in, other_in, own_ref, other_ref):
    own_ref[...] = jnp.transpose(own_in[...])
    other_ref[...] = jnp.transpose(other_in[...])


def turn_halves(rows, core, groups):
    length, width = rows.shape
    size = width // groups

    def chosen(side):
        return pl.BlockSpec(
            (length, size), lambda i, core_ref: (0, 2 * i + jnp.bitwise_xor(core_ref[0], side))
        )

    half = jax.ShapeDtypeStruct((width // 2, length), rows.dtype)
    block = pl.BlockSpec((size, length), lambda i, core_ref: (i, 0))
    return pl.pallas_call(
        turn_kernel,
        grid_spec=pltpu.PrefetchScalarGridSpec(
            num_scalar_prefetch=1,
            grid=(groups // 2,),
            in_specs=[chosen(0), chosen(1)],
            out_specs=[block, block],
        ),
        out_shape=[half, half],
        compiler_params=pltpu.CompilerParams(vmem_limit_bytes=VMEM_BYTES),
        cost_estimate=NO_COST,
        name="turn_halves",
    )(core, rows, rows)


def added_dot_kernel(left_ref, right_ref, added_ref, out_ref):
    rows = left_ref.shape[0]
    chunk = min(512, rows)
    for start in range(0, rows, chunk):
        at = slice(start, start + chunk)
        product = jnp.dot(left_ref[at, :], right_ref[...], preferred_element_type=jnp.float32)
        out_ref[at, :] = (product + added_ref[at, :].astype(jnp.float32)).astype(jnp.bfloat16)


def added_dot(left, right, added):
    rows, depth = left.shape
    width = right.shape[1]
    tile = next(t for t in (512, 256, 128) if width % t == 0)
    column = pl.BlockSpec((rows, tile), lambda j: (0, j))
    return pl.pallas_call(
        added_dot_kernel,
        grid=(width // tile,),
        in_specs=[
            pl.BlockSpec((rows, depth), lambda j: (0, 0)),
            pl.BlockSpec((depth, tile), lambda j: (0, j)),
            column,
        ],
        out_specs=column,
        out_shape=jax.ShapeDtypeStruct((rows, width), jnp.bfloat16),
        compiler_params=pltpu.CompilerParams(vmem_limit_bytes=VMEM_BYTES),
        cost_estimate=NO_COST,
        name="added_dot",
    )(left, right, added)


def both(*values):
    return lax.optimization_barrier(values)


def on_device(
    tokens,
    segments,
    buckets,
    w_query,
    w_key,
    w_value,
    w_attn_out,
    gain_attn,
    rel_table,
    w_gate,
    w_up,
    w_down,
    gain_ffn,
    out_grad,
):
    token_rows = tokens.shape[1]
    model_width = tokens.shape[2]
    ffn_width = w_gate.shape[1]
    segment_row = segments[0]
    row_length = segment_row.shape[0]
    seq_count = lax.axis_size("seq")
    fsdp_count = lax.axis_size("fsdp")
    seq_place = lax.axis_index("seq")
    fsdp_place = lax.axis_index("fsdp")
    place = seq_place.astype(jnp.int32).reshape(1)
    head_count = model_width // seq_count // DH
    column_count = model_width // seq_count
    unit_count = ffn_width // seq_count

    tile = 256 if unit_count % 256 == 0 else 128
    pairs = head_count // 2

    def gather_weights(piece):
        return lax.all_gather(piece, "fsdp", axis=0, tiled=True)

    qkv_moves = [
        (which, (3 * pair + which) * PAIR, pair * PAIR, PAIR)
        for pair in range(pairs)
        for which in range(3)
    ] + [(3, 3 * column_count, 0, column_count)]
    unit_moves = [
        (which, (2 * block + which) * tile, block * tile, tile)
        for block in range(unit_count // tile)
        for which in range(2)
    ]
    attn_part = take_columns(
        place, (w_query, w_key, w_value, w_attn_out), qkv_moves, [column_count] * 4
    )
    attn_w = gather_weights(attn_part)
    gains = lax.all_gather(jnp.stack([gain_attn, gain_ffn]), "fsdp", axis=1, tiled=True)
    qkv_w = attn_w[:, : 3 * column_count]
    output_w = attn_w[:, 3 * column_count :]

    table_rows = jnp.pad(buckets[::-1], (0, 1), constant_values=-1)
    bucket_table = (
        table_rows[:, None] == jnp.arange(rel_table.shape[1], dtype=jnp.int32)[None, :]
    ).astype(jnp.float32)
    local_table = lax.dynamic_slice_in_dim(rel_table, seq_place * head_count, head_count, 0)
    bias_line = jnp.dot(local_table, jnp.transpose(bucket_table), precision=PRECISE)
    bias_line = bias_line.reshape(head_count // 2, 2, 2 * row_length)
    segment_wide = jnp.broadcast_to(segment_row[:, None], (row_length, TILE))

    stream = tokens[0].astype(jnp.float32)
    scale_attn = lax.rsqrt(jnp.mean(stream * stream, axis=-1, keepdims=True) + EPSILON)
    normed_attn = stream * scale_attn
    upstream = out_grad[0].astype(jnp.float32)

    stream_near = gather_begin(tokens[0])
    stream_near, gains = both(stream_near, gains)
    attn_gain = gains[0].astype(jnp.float32)
    ffn_gain = gains[1].astype(jnp.float32)
    stream_rows = joined(gather_end(tokens[0], stream_near))
    gate_up_part = take_columns(place, (w_gate, w_up), unit_moves, [unit_count] * 2)
    gate_up_part, stream_rows = both(gate_up_part, stream_rows)
    gate_up_w = gather_weights(gate_up_part)
    stream_rows = stream_rows.astype(jnp.float32)
    rows_scale = lax.rsqrt(jnp.mean(stream_rows * stream_rows, axis=-1, keepdims=True) + EPSILON)
    attn_rows = (stream_rows * rows_scale * attn_gain).astype(jnp.bfloat16)
    ff_grad_rows = gather_rows(out_grad[0])
    attn_rows, ff_grad_rows = both(attn_rows, ff_grad_rows)

    qkv = jnp.dot(attn_rows, qkv_w, preferred_element_type=jnp.float32).astype(jnp.bfloat16)
    down_part, qkv = both(
        lax.dynamic_slice_in_dim(w_down, seq_place * unit_count, unit_count, 1), qkv
    )
    down_w = gather_weights(down_part)
    context, exponents, inverse = attention_forward(
        qkv, place, segments, segment_wide, bias_line, head_count, token_rows
    )

    attn_out = scatter_sum(context, output_w)
    chips = fsdp_count // 2
    core = (fsdp_place % 2).astype(jnp.int32).reshape(1)
    groups = [[2 * chip + side for chip in range(chips)] for side in range(2)]

    def scatter_grads(grads, axis_index_groups=None):
        return lax.psum_scatter(
            grads,
            "fsdp",
            scatter_dimension=0,
            tiled=True,
            axis_index_groups=axis_index_groups,
        )

    resid = stream + attn_out
    scale_ffn = lax.rsqrt(jnp.mean(resid * resid, axis=-1, keepdims=True) + EPSILON)
    normed_ffn = resid * scale_ffn
    ffn_rows = gather_rows((normed_ffn * ffn_gain).astype(jnp.bfloat16))

    hidden, gelu, slope = feed_forward(ffn_rows, gate_up_w, tile)

    down_grad = rows_dot(ff_grad_rows, hidden).astype(jnp.bfloat16)
    down_owned = scatter_grads(down_grad)
    down_grad, hidden, gelu = both(down_grad, hidden, gelu)
    away = row_length // seq_count
    passed = 3 * away if seq_count == 4 else row_length
    ff_far = low_dot(hidden[passed:], down_w) if seq_count == 4 else None
    ff_far, hidden, gelu = both(ff_far, hidden, gelu)
    ff_passing = scatter_begin(ff_far)
    unit_grad = feed_forward_back(ff_grad_rows, down_w, gelu, slope, tile)
    unit_far = low_dot(unit_grad[passed:], gate_up_w) if seq_count == 4 else None
    unit_far, unit_grad, ff_passing = both(unit_far, unit_grad, ff_passing)
    unit_passing = scatter_begin(unit_far)
    unit_near = low_dot(unit_grad[away:passed], gate_up_w)
    unit_near, unit_grad, unit_passing = both(unit_near, unit_grad, unit_passing)
    unit_sums = scatter_add(unit_near, unit_passing)
    unit_sums, unit_grad = both(unit_sums, unit_grad)
    unit_parts = scatter_end(unit_sums)
    gate_up_grad = rows_dot(ffn_rows, unit_grad).astype(jnp.bfloat16)
    ffn_in_own = cols_dot(unit_grad[:away], gate_up_w)
    ffn_in_own, gate_up_grad, unit_parts = both(ffn_in_own, gate_up_grad, unit_parts)
    gate_up_owned = scatter_grads(gate_up_grad)
    ffn_in_grad = add_parts(ffn_in_own, unit_parts)

    resid_grad = upstream + norm_back(ffn_in_grad * ffn_gain, normed_ffn, scale_ffn)
    attn_grad = resid_grad.astype(jnp.bfloat16)
    attn_grad, hidden, down_owned = both(attn_grad, hidden, down_owned)
    attn_grad_rows = gather_rows(attn_grad)
    ff_near = low_dot(hidden[away:passed], down_w)
    ff_sums = scatter_add(ff_near, ff_passing)
    attn_grad_rows, ff_sums, down_owned = both(attn_grad_rows, ff_sums, down_owned)
    context_grad = jnp.dot(
        attn_grad_rows, output_w, preferred_element_type=jnp.float32
    ).astype(jnp.bfloat16)
    ff_parts = scatter_end(ff_sums)
    down_near = gather_begin(down_owned, relay=False)
    qkv_grad, line_grad = attention_backward(
        qkv, place, context_grad, exponents, inverse, head_count, token_rows
    )
    qkv_terms = low_dot(qkv_grad[away:], qkv_w)
    qkv_terms, qkv_grad = both(qkv_terms, qkv_grad)
    attn_grads = rows_dot(attn_rows, qkv_grad).astype(jnp.bfloat16)
    attn_grads, context, qkv_grad, ff_parts, down_near, attn_grad_rows, qkv_terms = both(
        attn_grads, context, qkv_grad, ff_parts, down_near, attn_grad_rows, qkv_terms
    )
    attn_owned = scatter_grads(attn_grads)
    qkv_near, qkv_far = split_terms(qkv_terms)
    qkv_passing = scatter_begin(qkv_far)
    output_own, output_other = turn_halves(attn_grad_rows, core, fsdp_count)
    output_away = jnp.dot(
        output_other, context, preferred_element_type=jnp.float32
    ).astype(jnp.bfloat16)
    qkv_passing, gate_up_owned, output_away, output_own, hidden, down_near, qkv_grad = both(
        qkv_passing, gate_up_owned, output_away, output_own, hidden, down_near, qkv_grad
    )
    attn_in_own = cols_dot(qkv_grad[:away], qkv_w)
    gate_up_near = gather_begin(gate_up_owned)
    output_added = swap(output_away, "fsdp", 1)
    output_grad = added_dot(output_own, context, output_added)
    output_owned = scatter_grads(output_grad, groups)
    attn_in_parts = scatter_end(scatter_add(qkv_near, qkv_passing))
    gate_up_pieces = gather_end(gate_up_owned, gate_up_near)
    down_pieces = gather_end(down_owned, down_near)
    ff_out = add_parts(cols_dot(hidden[:away], down_w), ff_parts)
    result = resid + ff_out
    (down_out,) = place_columns(down_pieces, place, [(0, 0, 0, unit_count)], [unit_count])
    own_segments = lax.dynamic_slice_in_dim(segment_row, seq_place * token_rows, token_rows, 0)
    valid = (own_segments >= 0).astype(jnp.float32)
    stat_terms = jnp.stack(
        [
            jnp.sum(valid * jnp.sum(result * result, axis=-1)),
            jnp.sum(valid * jnp.sum(attn_out * attn_out, axis=-1)),
            jnp.sum(valid * jnp.sum(ff_out * ff_out, axis=-1)),
            jnp.sum(valid),
        ]
    )
    table_part = jnp.dot(
        line_grad.reshape(head_count, 2 * row_length), bucket_table, precision=PRECISE
    )
    full_table = lax.dynamic_update_slice_in_dim(
        jnp.zeros(rel_table.shape, jnp.float32), table_part, seq_place * head_count, 0
    )
    packed = jnp.concatenate([full_table.reshape(-1), jnp.pad(stat_terms, (0, TILE - 4))])
    summed = jnp.sum(lax.all_gather(packed.reshape(-1, TILE), "fsdp"), axis=0)
    attn_owned, result, summed, down_out, gate_up_pieces, attn_in_parts = both(
        attn_owned, result, summed, down_out, gate_up_pieces, attn_in_parts
    )
    attn_near = gather_begin(attn_owned)
    attn_in_grad = add_parts(attn_in_own, attn_in_parts)
    stream_grad = resid_grad + norm_back(attn_in_grad * attn_gain, normed_attn, scale_attn)
    stream_grad = stream_grad.astype(jnp.bfloat16)
    gate_out, up_out, ffn_sums = place_columns(
        gate_up_pieces, place, unit_moves, [unit_count] * 2, (w_gate, w_up)
    )
    attn_near, stream_grad, gate_out, up_out = both(attn_near, stream_grad, gate_out, up_out)
    attn_pieces = gather_end(attn_owned, attn_near)
    summed = seq_sum(summed).reshape(-1)
    attn_pieces, output_owned, summed = both(attn_pieces, output_owned, summed)
    output_near = gather_begin(output_owned, relay=False)
    attn_outs = place_columns(
        attn_pieces,
        place,
        qkv_moves[:-1],
        [column_count] * 3,
        (w_query, w_key, w_value),
    )
    output_near, attn_outs = both(output_near, attn_outs)
    query_out, key_out, value_out, attn_sums = attn_outs
    (output_out,) = place_columns(
        gather_end(output_owned, output_near), place, [(0, 0, 0, column_count)], [column_count]
    )
    gain_attn_grad = jnp.sum(attn_sums, axis=1) / gain_attn.astype(jnp.float32)
    gain_ffn_grad = jnp.sum(ffn_sums, axis=1) / gain_ffn.astype(jnp.float32)
    stat_totals = summed[rel_table.size : rel_table.size + 4]
    rms_stats = jnp.sqrt(stat_totals[0:3] / (stat_totals[3] * model_width))
    table_share = rel_table.shape[0] // fsdp_count
    rel_table_grad = lax.dynamic_slice_in_dim(
        summed[: rel_table.size].reshape(rel_table.shape),
        fsdp_place * table_share,
        table_share,
        0,
    )
    return (
        result.astype(jnp.bfloat16)[None],
        stream_grad[None],
        query_out,
        key_out,
        value_out,
        output_out,
        gain_attn_grad,
        rel_table_grad,
        gate_out,
        up_out,
        down_out,
        gain_ffn_grad,
        rms_stats,
    )


def solution(mesh):
    in_specs = (
        P("fsdp", "seq", None),
        P("fsdp", None),
        P(),
        P("fsdp", None),
        P("fsdp", None),
        P("fsdp", None),
        P("fsdp", None),
        P("fsdp"),
        P(),
        P("fsdp", None),
        P("fsdp", None),
        P("fsdp", None),
        P("fsdp"),
        P("fsdp", "seq", None),
    )
    out_specs = (
        P("fsdp", "seq", None),
        P("fsdp", "seq", None),
        P("fsdp", None),
        P("fsdp", None),
        P("fsdp", None),
        P("fsdp", None),
        P("fsdp"),
        P("fsdp", None),
        P("fsdp", None),
        P("fsdp", None),
        P("fsdp", None),
        P("fsdp"),
        P(),
    )
    return jax.shard_map(
        on_device, mesh=mesh, in_specs=in_specs, out_specs=out_specs, check_vma=False
    )
```

```python
import functools

import jax
import jax.numpy as jnp
from jax import lax
from jax.experimental import pallas as pl
from jax.experimental.pallas import tpu as pltpu
from jax.sharding import PartitionSpec as P

DH = 64


EPSILON = 1e-06
PRECISE = lax.Precision.HIGHEST
MASKED_SCORE = -1e30
TILE = 128
PAIR = 2 * DH
GELU_SCALE = 0.7978845608
GELU_CUBE = 0.044715
NO_COST = pl.CostEstimate(flops=0, bytes_accessed=0, transcendentals=0)
VMEM_BYTES = 56 * 1024 * 1024


def rows_dot(left, right):
    return lax.dot_general(
        left, right, (((0,), (0,)), ((), ())), preferred_element_type=jnp.float32
    )


def cols_dot(left, right):
    return lax.dot_general(
        left, right, (((1,), (1,)), ((), ())), preferred_element_type=jnp.float32
    )


def norm_back(grad_hat, normed, scale):
    return scale * (grad_hat - normed * jnp.mean(grad_hat * normed, axis=-1, keepdims=True))


def half_lanes(shape, which):
    lane = lax.broadcasted_iota(jnp.int32, shape, 1)
    return (lane < DH) if which == 0 else (lane >= DH)


def fold_rows(tile):
    return jnp.sum(tile.reshape(tile.shape[0] // 8, 8, tile.shape[1]), axis=0)


def query_block(length):
    return min(length, max(256, 2**20 // length))


def whole_place(row, token_rows, place):
    return jnp.bitwise_xor(row // token_rows, place) * token_rows + row % token_rows


def bias_offsets(first, block, length, token_rows, place, tile):
    reach = length - TILE
    key_place = whole_place(tile * TILE, token_rows, place)
    group = min(block, token_rows)
    return [
        pl.multiple_of(
            whole_place(first + start, token_rows, place) + (reach - key_place), TILE
        )
        for start in range(0, block, group)
    ], group


def forward_kernel(
    block,
    token_rows,
    place_ref,
    qkv_ref,
    row_ref,
    col_ref,
    bias_ref,
    ctx_ref,
    e_ref,
    inv_ref,
    strip_ref,
    score_ref,
):
    length = qkv_ref.shape[0]
    q_ref = qkv_ref.at[:, :PAIR]
    k_ref = qkv_ref.at[:, PAIR : 2 * PAIR]
    v_ref = qkv_ref.at[:, 2 * PAIR :]
    tiles = length // TILE
    width = 2 * length
    place = place_ref[0]
    group = min(block, token_rows)
    values_t = jnp.transpose(v_ref[...])
    for head in range(2):
        wide = jnp.broadcast_to(bias_ref[0, head : head + 1, :], (TILE, width))
        strip_ref[head] = pltpu.roll(wide, width - (TILE - 1), 1, stride=1, stride_axis=0)

    def one_block(first):
        q_block = q_ref[pl.ds(first, block), :]
        segment_q = jnp.concatenate(
            [
                row_ref[
                    :,
                    pl.ds(
                        pl.multiple_of(whole_place(first + start, token_rows, place), TILE), group
                    ),
                ]
                for start in range(0, block, group)
            ],
            axis=1,
        )
        outs = []
        for head in range(2):
            q_head = jnp.where(half_lanes(q_block.shape, head), q_block, jnp.zeros_like(q_block))
            raw = cols_dot(k_ref[...], q_head)
            highest = jnp.full((8, block), -jnp.inf, jnp.float32)
            for tile in range(tiles):
                rows = slice(tile * TILE, (tile + 1) * TILE)
                offsets, _ = bias_offsets(first, block, length, token_rows, place, tile)
                bias = jnp.concatenate(
                    [strip_ref[head, :, pl.ds(offset, group)] for offset in offsets], axis=1
                )
                key_place = whole_place(tile * TILE, token_rows, place)
                segment_k = col_ref[pl.ds(pl.multiple_of(key_place, TILE), TILE), :]
                segment_k = jnp.concatenate([segment_k] * (block // TILE), axis=1)
                score = jnp.where(segment_k == segment_q, raw[rows, :] + bias, MASKED_SCORE)
                score_ref[head, rows, :] = score
                highest = jnp.maximum(
                    highest, jnp.max(score.reshape(TILE // 8, 8, block), axis=0)
                )
            top = jnp.max(highest, axis=0, keepdims=True)
            total = jnp.zeros((8, block), jnp.float32)
            for tile in range(tiles):
                rows = slice(tile * TILE, (tile + 1) * TILE)
                exponent = jnp.exp(score_ref[head, rows, :] - top)
                total = total + fold_rows(exponent)
                e_ref[head, rows, pl.ds(first, block)] = exponent.astype(jnp.bfloat16)
            inverse = 1.0 / jnp.sum(total, axis=0, keepdims=True)
            inv_ref[head, :, pl.ds(first, block)] = inverse
            context = jnp.dot(
                values_t[head * DH : (head + 1) * DH, :],
                e_ref[head, :, pl.ds(first, block)],
                preferred_element_type=jnp.float32,
            )
            outs.append(context * inverse)
        ctx_ref[pl.ds(first, block), :] = jnp.transpose(jnp.concatenate(outs, axis=0)).astype(
            jnp.bfloat16
        )

    for_blocks(length // block, block, one_block)


def for_blocks(count, block, body):
    if count == 1:
        body(0)
        return

    def step(index, carry):
        body(pl.multiple_of(index * block, block))
        return carry

    lax.fori_loop(0, count, step, 0)


def attention_forward(qkv, place, segment_row, segment_wide, bias_line, heads, token_rows):
    length = qkv.shape[0]
    block = query_block(length)
    pairs = heads // 2
    return pl.pallas_call(
        functools.partial(forward_kernel, block, token_rows),
        grid=(pairs,),
        in_specs=[
            pl.BlockSpec(memory_space=pltpu.SMEM),
            pl.BlockSpec((length, 3 * PAIR), lambda i: (0, i)),
            pl.BlockSpec((1, length), lambda i: (0, 0)),
            pl.BlockSpec((length, TILE), lambda i: (0, 0)),
            pl.BlockSpec((1, 2, 2 * length), lambda i: (i, 0, 0)),
        ],
        out_specs=[
            pl.BlockSpec((length, PAIR), lambda i: (0, i)),
            pl.BlockSpec((2, length, length), lambda i: (i, 0, 0)),
            pl.BlockSpec((2, 1, length), lambda i: (i, 0, 0)),
        ],
        out_shape=[
            jax.ShapeDtypeStruct((length, heads * DH), jnp.bfloat16),
            jax.ShapeDtypeStruct((heads, length, length), jnp.bfloat16),
            jax.ShapeDtypeStruct((heads, 1, length), jnp.float32),
        ],
        scratch_shapes=[
            pltpu.VMEM((2, TILE, 2 * length), jnp.float32),
            pltpu.VMEM((2, length, block), jnp.float32),
        ],
        compiler_params=pltpu.CompilerParams(vmem_limit_bytes=VMEM_BYTES),
        cost_estimate=NO_COST,
        name="attention_forward",
    )(place, qkv, segment_row, segment_wide, bias_line)


def backward_kernel(
    block,
    token_rows,
    place_ref,
    qkv_ref,
    d_ref,
    e_ref,
    inv_ref,
    grad_ref,
    line_ref,
    strip_ref,
    prob_ref,
    low_ref,
    key_sum,
    value_sum,
):
    length = qkv_ref.shape[0]
    q_ref = qkv_ref.at[:, :PAIR]
    k_ref = qkv_ref.at[:, PAIR : 2 * PAIR]
    v_ref = qkv_ref.at[:, 2 * PAIR :]
    tiles = length // TILE
    place = place_ref[0]
    keys_t = jnp.transpose(k_ref[...])
    strip_ref[...] = jnp.zeros_like(strip_ref)
    key_sum[...] = jnp.zeros_like(key_sum)
    value_sum[...] = jnp.zeros_like(value_sum)

    def one_block(first):
        q_block = q_ref[pl.ds(first, block), :]
        d_block = d_ref[pl.ds(first, block), :]
        outs = []
        for head in range(2):
            mask = half_lanes(q_block.shape, head)
            q_head = jnp.where(mask, q_block, jnp.zeros_like(q_block))
            inverse = inv_ref[head, :, pl.ds(first, block)]
            scale = jnp.transpose(jnp.broadcast_to(inverse, (PAIR, block)))
            d_head = jnp.where(mask, d_block.astype(jnp.float32) * scale, 0.0)
            d_head = d_head.astype(jnp.bfloat16)
            prob_ref[head] = cols_dot(v_ref[...], d_head)
            value_sum[...] += jnp.dot(
                e_ref[head, :, pl.ds(first, block)], d_head, preferred_element_type=jnp.float32
            )
            total = jnp.zeros((8, block), jnp.float32)
            for tile in range(tiles):
                rows = slice(tile * TILE, (tile + 1) * TILE)
                exponent = e_ref[head, rows, pl.ds(first, block)].astype(jnp.float32)
                total = total + fold_rows(exponent * prob_ref[head, rows, :])
            centre = jnp.sum(total, axis=0, keepdims=True) * inverse
            for tile in range(tiles):
                rows = slice(tile * TILE, (tile + 1) * TILE)
                exponent = e_ref[head, rows, pl.ds(first, block)].astype(jnp.float32)
                grad = exponent * (prob_ref[head, rows, :] - centre)
                offsets, group = bias_offsets(first, block, length, token_rows, place, tile)
                for part, offset in enumerate(offsets):
                    at = pl.ds(offset, group)
                    strip_ref[head, :, at] = (
                        strip_ref[head, :, at] + grad[:, part * group : (part + 1) * group]
                    )
                low_ref[head, rows, :] = grad.astype(jnp.bfloat16)
            key_sum[...] += jnp.dot(low_ref[head], q_head, preferred_element_type=jnp.float32)
            outs.append(
                jnp.dot(
                    keys_t[head * DH : (head + 1) * DH, :],
                    low_ref[head],
                    preferred_element_type=jnp.float32,
                )
            )
        grad_ref[pl.ds(first, block), :PAIR] = jnp.transpose(
            jnp.concatenate(outs, axis=0)
        ).astype(jnp.bfloat16)

    for_blocks(length // block, block, one_block)
    grad_ref[:, PAIR : 2 * PAIR] = key_sum[...].astype(jnp.bfloat16)
    grad_ref[:, 2 * PAIR :] = value_sum[...].astype(jnp.bfloat16)
    for head in range(2):
        turned = strip_ref[head]
        while turned.shape[0] > 1:
            half = turned.shape[0] // 2
            turned = pltpu.roll(turned[:half], half, 1) + turned[half:]
        line_ref[0, head : head + 1, :] = turned


def attention_backward(qkv, place, d, e, inv, heads, token_rows):
    length = qkv.shape[0]
    block = query_block(length)
    pairs = heads // 2
    triple = pl.BlockSpec((length, 3 * PAIR), lambda i: (0, i))
    return pl.pallas_call(
        functools.partial(backward_kernel, block, token_rows),
        grid=(pairs,),
        in_specs=[
            pl.BlockSpec(memory_space=pltpu.SMEM),
            triple,
            pl.BlockSpec((length, PAIR), lambda i: (0, i)),
            pl.BlockSpec((2, length, length), lambda i: (i, 0, 0)),
            pl.BlockSpec((2, 1, length), lambda i: (i, 0, 0)),
        ],
        out_specs=[triple, pl.BlockSpec((1, 2, 2 * length), lambda i: (i, 0, 0))],
        out_shape=[
            jax.ShapeDtypeStruct((length, 3 * heads * DH), jnp.bfloat16),
            jax.ShapeDtypeStruct((pairs, 2, 2 * length), jnp.float32),
        ],
        scratch_shapes=[
            pltpu.VMEM((2, TILE, 2 * length), jnp.float32),
            pltpu.VMEM((2, length, block), jnp.float32),
            pltpu.VMEM((2, length, block), jnp.bfloat16),
            pltpu.VMEM((length, PAIR), jnp.float32),
            pltpu.VMEM((length, PAIR), jnp.float32),
        ],
        compiler_params=pltpu.CompilerParams(vmem_limit_bytes=VMEM_BYTES),
        cost_estimate=NO_COST,
        name="attention_backward",
    )(place, qkv, d, e, inv)


def swap(piece, axis, step):
    return lax.ppermute(piece, axis, [(i, i ^ step) for i in range(lax.axis_size(axis))])


def gather_begin(piece, relay=True):
    count = lax.axis_size("seq")
    steps = (1, 2) if count == 4 and relay else range(1, count)
    return tuple(swap(piece, "seq", step) for step in steps)


def gather_end(piece, near):
    if len(near) != 2:
        return [[part] for part in (piece, *near)]
    first, second = near
    half = piece.shape[0] // 2
    upper = swap(second[:half], "seq", 1)
    lower = swap(first[half:], "seq", 2)
    return [[piece], [first], [second], [upper, lower]]


def joined(parts):
    return jnp.concatenate([part for pieces in parts for part in pieces], axis=0)


def gather_rows(piece):
    return joined(gather_end(piece, gather_begin(piece)))


def low_dot(rows, weights):
    return cols_dot(rows, weights).astype(jnp.bfloat16)


def split_terms(terms):
    count = lax.axis_size("seq")
    size = terms.shape[0] // (count - 1)
    return (terms[: 2 * size], terms[2 * size :]) if count == 4 else (terms, None)


def scatter_begin(far):
    if far is None:
        return ()
    half = far.shape[0] // 2
    return swap(far[:half], "seq", 1), swap(far[half:], "seq", 2)


def scatter_add(near, passing):
    if not passing:
        size = near.shape[0] // (lax.axis_size("seq") - 1)
        return tuple(near[start : start + size] for start in range(0, near.shape[0], size))
    size = near.shape[0] // 2
    upper, lower = (part.astype(jnp.float32) for part in passing)
    first = near[:size].astype(jnp.float32) + jnp.pad(lower, ((size // 2, 0), (0, 0)))
    second = near[size:].astype(jnp.float32) + jnp.pad(upper, ((0, size // 2), (0, 0)))
    return first.astype(jnp.bfloat16), second.astype(jnp.bfloat16)


def scatter_end(sums):
    return tuple(swap(part, "seq", k + 1) for k, part in enumerate(sums))


def add_parts(own, received):
    return own + sum(part.astype(jnp.float32) for part in received)


def scatter_sum(rows, weights):
    size = rows.shape[0] // lax.axis_size("seq")
    near, far = split_terms(low_dot(rows[size:], weights))
    received = scatter_end(scatter_add(near, scatter_begin(far)))
    return add_parts(cols_dot(rows[:size], weights), received)


def seq_sum(values):
    level = [values] + [swap(values, "seq", step) for step in range(1, lax.axis_size("seq"))]
    while len(level) > 1:
        level = [level[i] + level[i + 1] for i in range(0, len(level), 2)]
    return level[0]


def feed_forward_kernel(tile, x_ref, w_ref, act_ref, gelu_ref, slope_ref):
    rows = x_ref.shape[0]
    chunk = min(512, rows)
    for start in range(0, rows, chunk):
        at = slice(start, start + chunk)
        both = jnp.dot(x_ref[at, :], w_ref[...], preferred_element_type=jnp.float32)
        gate, up = both[:, :tile], both[:, tile:]
        square = gate * gate
        tanh = jnp.tanh(GELU_SCALE * gate * (1.0 + GELU_CUBE * square))
        half_up = 0.5 * (1.0 + tanh)
        gelu = gate * half_up
        bend = 0.5 * GELU_SCALE * gate * (1.0 - tanh * tanh) * (1.0 + 3.0 * GELU_CUBE * square)
        act_ref[at, :] = (gelu * up).astype(jnp.bfloat16)
        gelu_ref[at, :] = gelu.astype(jnp.bfloat16)
        slope_ref[at, :] = (up * (half_up + bend)).astype(jnp.bfloat16)


def feed_forward(rows, weights, tile):
    length, model_width = rows.shape
    units = weights.shape[1] // 2
    block = pl.BlockSpec((length, tile), lambda j: (0, j))
    return pl.pallas_call(
        functools.partial(feed_forward_kernel, tile),
        grid=(units // tile,),
        in_specs=[
            pl.BlockSpec((length, model_width), lambda j: (0, 0)),
            pl.BlockSpec((model_width, 2 * tile), lambda j: (0, j)),
        ],
        out_specs=[block, block, block],
        out_shape=[
            jax.ShapeDtypeStruct((length, units), jnp.bfloat16),
            jax.ShapeDtypeStruct((length, units), jnp.bfloat16),
            jax.ShapeDtypeStruct((length, units), jnp.bfloat16),
        ],
        compiler_params=pltpu.CompilerParams(vmem_limit_bytes=VMEM_BYTES),
        cost_estimate=NO_COST,
        name="feed_forward",
    )(rows, weights)


def feed_forward_back_kernel(tile, d_ref, w_ref, gelu_ref, slope_ref, grad_ref):
    rows = d_ref.shape[0]
    chunk = min(512, rows)
    for start in range(0, rows, chunk):
        at = slice(start, start + chunk)
        grad = jnp.dot(d_ref[at, :], w_ref[...], preferred_element_type=jnp.float32)
        grad_ref[at, :tile] = (grad * slope_ref[at, :].astype(jnp.float32)).astype(jnp.bfloat16)
        grad_ref[at, tile:] = (grad * gelu_ref[at, :].astype(jnp.float32)).astype(jnp.bfloat16)


def feed_forward_back(grad_rows, weights, gelu, slope, tile):
    length, model_width = grad_rows.shape
    units = weights.shape[1]
    block = pl.BlockSpec((length, tile), lambda j: (0, j))
    return pl.pallas_call(
        functools.partial(feed_forward_back_kernel, tile),
        grid=(units // tile,),
        in_specs=[
            pl.BlockSpec((length, model_width), lambda j: (0, 0)),
            pl.BlockSpec((model_width, tile), lambda j: (0, j)),
            block,
            block,
        ],
        out_specs=pl.BlockSpec((length, 2 * tile), lambda j: (0, j)),
        out_shape=jax.ShapeDtypeStruct((length, 2 * units), jnp.bfloat16),
        compiler_params=pltpu.CompilerParams(vmem_limit_bytes=VMEM_BYTES),
        cost_estimate=NO_COST,
        name="feed_forward_back",
    )(grad_rows, weights, gelu, slope)


def place_kernel(moves, lengths, block, widths, weighed, place_ref, *refs):
    count = sum(lengths)
    weights = refs[count : count + len(weighed)]
    outs = refs[count + len(weighed) : count + len(weighed) + len(widths)]
    total = jnp.zeros((block, TILE), jnp.float32)
    first = 0
    for step, length in enumerate(lengths):
        pieces = refs[first : first + length]
        first += length
        owner = jnp.bitwise_xor(place_ref[0], step)
        for out, source, target, size in moves:
            at = pl.ds(pl.multiple_of(owner * widths[out] + target, TILE), size)
            part = pieces[0][:, source : source + size]
            if length == 2:
                upper = pl.program_id(0) < pl.num_programs(0) // 2
                part = jnp.where(upper, part, pieces[1][:, source : source + size])
            part = part.astype(jnp.float32)
            outs[out][:, at] = part
            if out in weighed:
                part = part * weights[weighed.index(out)][:, at].astype(jnp.float32)
                for start in range(0, size, TILE):
                    total = total + part[:, start : start + TILE]
    if weighed:
        refs[-1][...] = total


def place_columns(parts, place, moves, widths, weights=()):
    lengths = tuple(len(pieces) for pieces in parts)
    count = lax.axis_size("seq")
    rows, width = parts[0][0].shape
    block = min(64, rows // 2)
    steps = rows // block

    def wide(size):
        return pl.BlockSpec((block, size), lambda i: (i, 0))

    def piece_specs(length):
        if length == 1:
            return [wide(width)]
        half = steps // 2
        return [
            pl.BlockSpec((block, width), lambda i: (jnp.minimum(i, half - 1), 0)),
            pl.BlockSpec((block, width), lambda i: (jnp.maximum(i - half, 0), 0)),
        ]

    whole = [wide(count * size) for size in widths]
    sums = [wide(TILE)] if weights else []
    shapes = [count * size for size in widths] + [TILE] * len(sums)
    weighed = tuple(range(len(weights)))
    return pl.pallas_call(
        functools.partial(place_kernel, moves, lengths, block, widths, weighed),
        grid=(steps,),
        in_specs=[pl.BlockSpec(memory_space=pltpu.SMEM)]
        + [spec for length in lengths for spec in piece_specs(length)]
        + whole[: len(weights)],
        out_specs=whole + sums,
        out_shape=[jax.ShapeDtypeStruct((rows, size), jnp.float32) for size in shapes],
        compiler_params=pltpu.CompilerParams(vmem_limit_bytes=VMEM_BYTES),
        cost_estimate=pl.CostEstimate(
            flops=0, bytes_accessed=8 * rows * sum(shapes), transcendentals=0
        ),
        name="place_columns",
    )(place, *[piece for pieces in parts for piece in pieces], *weights)


def take_kernel(moves, count, place_ref, *refs):
    out_ref = refs[count]
    for which, source, target, size in moves:
        out_ref[:, source : source + size] = refs[which][:, target : target + size]


def take_columns(place, weights, moves, counts):
    rows = weights[0].shape[0]
    block = min(128, rows)
    width = sum(counts)

    def chosen(count):
        return pl.BlockSpec((block, count), lambda i, place_ref: (i, place_ref[0]))

    return pl.pallas_call(
        functools.partial(take_kernel, moves, len(weights)),
        grid_spec=pltpu.PrefetchScalarGridSpec(
            num_scalar_prefetch=1,
            grid=(rows // block,),
            in_specs=[chosen(count) for count in counts],
            out_specs=pl.BlockSpec((block, width), lambda i, place_ref: (i, 0)),
        ),
        out_shape=jax.ShapeDtypeStruct((rows, width), weights[0].dtype),
        compiler_params=pltpu.CompilerParams(vmem_limit_bytes=VMEM_BYTES),
        cost_estimate=NO_COST,
        name="take_columns",
    )(place, *weights)


def turn_kernel(core_ref, own_in, other_in, own_ref, other_ref):
    own_ref[...] = jnp.transpose(own_in[...])
    other_ref[...] = jnp.transpose(other_in[...])


def turn_halves(rows, core, groups):
    length, width = rows.shape
    size = width // groups

    def chosen(side):
        return pl.BlockSpec(
            (length, size), lambda i, core_ref: (0, 2 * i + jnp.bitwise_xor(core_ref[0], side))
        )

    half = jax.ShapeDtypeStruct((width // 2, length), rows.dtype)
    block = pl.BlockSpec((size, length), lambda i, core_ref: (i, 0))
    return pl.pallas_call(
        turn_kernel,
        grid_spec=pltpu.PrefetchScalarGridSpec(
            num_scalar_prefetch=1,
            grid=(groups // 2,),
            in_specs=[chosen(0), chosen(1)],
            out_specs=[block, block],
        ),
        out_shape=[half, half],
        compiler_params=pltpu.CompilerParams(vmem_limit_bytes=VMEM_BYTES),
        cost_estimate=NO_COST,
        name="turn_halves",
    )(core, rows, rows)


def added_dot_kernel(left_ref, right_ref, added_ref, out_ref):
    rows = left_ref.shape[0]
    chunk = min(512, rows)
    for start in range(0, rows, chunk):
        at = slice(start, start + chunk)
        product = jnp.dot(left_ref[at, :], right_ref[...], preferred_element_type=jnp.float32)
        out_ref[at, :] = (product + added_ref[at, :].astype(jnp.float32)).astype(jnp.bfloat16)


def added_dot(left, right, added):
    rows, depth = left.shape
    width = right.shape[1]
    tile = next(t for t in (512, 256, 128) if width % t == 0)
    column = pl.BlockSpec((rows, tile), lambda j: (0, j))
    return pl.pallas_call(
        added_dot_kernel,
        grid=(width // tile,),
        in_specs=[
            pl.BlockSpec((rows, depth), lambda j: (0, 0)),
            pl.BlockSpec((depth, tile), lambda j: (0, j)),
            column,
        ],
        out_specs=column,
        out_shape=jax.ShapeDtypeStruct((rows, width), jnp.bfloat16),
        compiler_params=pltpu.CompilerParams(vmem_limit_bytes=VMEM_BYTES),
        cost_estimate=NO_COST,
        name="added_dot",
    )(left, right, added)


def both(*values):
    return lax.optimization_barrier(values)


def on_device(
    tokens,
    segments,
    buckets,
    w_query,
    w_key,
    w_value,
    w_attn_out,
    gain_attn,
    rel_table,
    w_gate,
    w_up,
    w_down,
    gain_ffn,
    out_grad,
):
    token_rows = tokens.shape[1]
    model_width = tokens.shape[2]
    ffn_width = w_gate.shape[1]
    segment_row = segments[0]
    row_length = segment_row.shape[0]
    seq_count = lax.axis_size("seq")
    fsdp_count = lax.axis_size("fsdp")
    seq_place = lax.axis_index("seq")
    fsdp_place = lax.axis_index("fsdp")
    place = seq_place.astype(jnp.int32).reshape(1)
    head_count = model_width // seq_count // DH
    column_count = model_width // seq_count
    unit_count = ffn_width // seq_count

    tile = 256 if unit_count % 256 == 0 else 128
    pairs = head_count // 2

    def gather_weights(piece):
        return lax.all_gather(piece, "fsdp", axis=0, tiled=True)

    qkv_moves = [
        (which, (3 * pair + which) * PAIR, pair * PAIR, PAIR)
        for pair in range(pairs)
        for which in range(3)
    ] + [(3, 3 * column_count, 0, column_count)]
    unit_moves = [
        (which, (2 * block + which) * tile, block * tile, tile)
        for block in range(unit_count // tile)
        for which in range(2)
    ]
    attn_part = take_columns(
        place, (w_query, w_key, w_value, w_attn_out), qkv_moves, [column_count] * 4
    )
    attn_w = gather_weights(attn_part)
    gains = lax.all_gather(jnp.stack([gain_attn, gain_ffn]), "fsdp", axis=1, tiled=True)
    qkv_w = attn_w[:, : 3 * column_count]
    output_w = attn_w[:, 3 * column_count :]

    table_rows = jnp.pad(buckets[::-1], (0, 1), constant_values=-1)
    bucket_table = (
        table_rows[:, None] == jnp.arange(rel_table.shape[1], dtype=jnp.int32)[None, :]
    ).astype(jnp.float32)
    local_table = lax.dynamic_slice_in_dim(rel_table, seq_place * head_count, head_count, 0)
    bias_line = jnp.dot(local_table, jnp.transpose(bucket_table), precision=PRECISE)
    bias_line = bias_line.reshape(head_count // 2, 2, 2 * row_length)
    segment_wide = jnp.broadcast_to(segment_row[:, None], (row_length, TILE))

    stream = tokens[0].astype(jnp.float32)
    scale_attn = lax.rsqrt(jnp.mean(stream * stream, axis=-1, keepdims=True) + EPSILON)
    normed_attn = stream * scale_attn
    upstream = out_grad[0].astype(jnp.float32)

    stream_near = gather_begin(tokens[0])
    stream_near, gains = both(stream_near, gains)
    attn_gain = gains[0].astype(jnp.float32)
    ffn_gain = gains[1].astype(jnp.float32)
    stream_rows = joined(gather_end(tokens[0], stream_near))
    gate_up_part = take_columns(place, (w_gate, w_up), unit_moves, [unit_count] * 2)
    gate_up_part, stream_rows = both(gate_up_part, stream_rows)
    gate_up_w = gather_weights(gate_up_part)
    stream_rows = stream_rows.astype(jnp.float32)
    rows_scale = lax.rsqrt(jnp.mean(stream_rows * stream_rows, axis=-1, keepdims=True) + EPSILON)
    attn_rows = (stream_rows * rows_scale * attn_gain).astype(jnp.bfloat16)
    ff_grad_rows = gather_rows(out_grad[0])
    attn_rows, ff_grad_rows = both(attn_rows, ff_grad_rows)

    qkv = jnp.dot(attn_rows, qkv_w, preferred_element_type=jnp.float32).astype(jnp.bfloat16)
    down_part, qkv = both(
        lax.dynamic_slice_in_dim(w_down, seq_place * unit_count, unit_count, 1), qkv
    )
    down_w = gather_weights(down_part)
    context, exponents, inverse = attention_forward(
        qkv, place, segments, segment_wide, bias_line, head_count, token_rows
    )

    attn_out = scatter_sum(context, output_w)
    chips = fsdp_count // 2
    core = (fsdp_place % 2).astype(jnp.int32).reshape(1)
    groups = [[2 * chip + side for chip in range(chips)] for side in range(2)]

    def scatter_grads(grads, axis_index_groups=None):
        return lax.psum_scatter(
            grads,
            "fsdp",
            scatter_dimension=0,
            tiled=True,
            axis_index_groups=axis_index_groups,
        )

    resid = stream + attn_out
    scale_ffn = lax.rsqrt(jnp.mean(resid * resid, axis=-1, keepdims=True) + EPSILON)
    normed_ffn = resid * scale_ffn
    ffn_rows = gather_rows((normed_ffn * ffn_gain).astype(jnp.bfloat16))

    hidden, gelu, slope = feed_forward(ffn_rows, gate_up_w, tile)

    down_grad = rows_dot(ff_grad_rows, hidden).astype(jnp.bfloat16)
    down_owned = scatter_grads(down_grad)
    down_grad, hidden, gelu = both(down_grad, hidden, gelu)
    away = row_length // seq_count
    passed = 3 * away if seq_count == 4 else row_length
    ff_far = low_dot(hidden[passed:], down_w) if seq_count == 4 else None
    ff_far, hidden, gelu = both(ff_far, hidden, gelu)
    ff_passing = scatter_begin(ff_far)
    unit_grad = feed_forward_back(ff_grad_rows, down_w, gelu, slope, tile)
    unit_far = low_dot(unit_grad[passed:], gate_up_w) if seq_count == 4 else None
    unit_far, unit_grad, ff_passing = both(unit_far, unit_grad, ff_passing)
    unit_passing = scatter_begin(unit_far)
    unit_near = low_dot(unit_grad[away:passed], gate_up_w)
    unit_near, unit_grad, unit_passing = both(unit_near, unit_grad, unit_passing)
    unit_sums = scatter_add(unit_near, unit_passing)
    unit_sums, unit_grad = both(unit_sums, unit_grad)
    unit_parts = scatter_end(unit_sums)
    gate_up_grad = rows_dot(ffn_rows, unit_grad).astype(jnp.bfloat16)
    ffn_in_own = cols_dot(unit_grad[:away], gate_up_w)
    ffn_in_own, gate_up_grad, unit_parts = both(ffn_in_own, gate_up_grad, unit_parts)
    gate_up_owned = scatter_grads(gate_up_grad)
    ffn_in_grad = add_parts(ffn_in_own, unit_parts)

    resid_grad = upstream + norm_back(ffn_in_grad * ffn_gain, normed_ffn, scale_ffn)
    attn_grad = resid_grad.astype(jnp.bfloat16)
    attn_grad, hidden, down_owned = both(attn_grad, hidden, down_owned)
    attn_grad_rows = gather_rows(attn_grad)
    ff_near = low_dot(hidden[away:passed], down_w)
    ff_sums = scatter_add(ff_near, ff_passing)
    attn_grad_rows, ff_sums, down_owned = both(attn_grad_rows, ff_sums, down_owned)
    context_grad = jnp.dot(
        attn_grad_rows, output_w, preferred_element_type=jnp.float32
    ).astype(jnp.bfloat16)
    ff_parts = scatter_end(ff_sums)
    down_near = gather_begin(down_owned, relay=False)
    qkv_grad, line_grad = attention_backward(
        qkv, place, context_grad, exponents, inverse, head_count, token_rows
    )
    qkv_terms = low_dot(qkv_grad[away:], qkv_w)
    qkv_terms, qkv_grad, ff_parts, down_near = both(qkv_terms, qkv_grad, ff_parts, down_near)
    qkv_near, qkv_far = split_terms(qkv_terms)
    qkv_passing = scatter_begin(qkv_far)
    attn_grads = rows_dot(attn_rows, qkv_grad).astype(jnp.bfloat16)
    attn_grads, context, qkv_grad, attn_grad_rows, qkv_passing, gate_up_owned, hidden = both(
        attn_grads, context, qkv_grad, attn_grad_rows, qkv_passing, gate_up_owned, hidden
    )
    attn_owned = scatter_grads(attn_grads)
    gate_up_near = gather_begin(gate_up_owned)
    attn_in_parts = scatter_end(scatter_add(qkv_near, qkv_passing))
    output_own, output_other = turn_halves(attn_grad_rows, core, fsdp_count)
    output_away = jnp.dot(
        output_other, context, preferred_element_type=jnp.float32
    ).astype(jnp.bfloat16)
    output_added = swap(output_away, "fsdp", 1)
    attn_in_own = cols_dot(qkv_grad[:away], qkv_w)
    output_grad = added_dot(output_own, context, output_added)
    ff_out = add_parts(cols_dot(hidden[:away], down_w), ff_parts)
    result = resid + ff_out
    own_segments = lax.dynamic_slice_in_dim(segment_row, seq_place * token_rows, token_rows, 0)
    valid = (own_segments >= 0).astype(jnp.float32)
    stat_terms = jnp.stack(
        [
            jnp.sum(valid * jnp.sum(result * result, axis=-1)),
            jnp.sum(valid * jnp.sum(attn_out * attn_out, axis=-1)),
            jnp.sum(valid * jnp.sum(ff_out * ff_out, axis=-1)),
            jnp.sum(valid),
        ]
    )
    table_part = jnp.dot(
        line_grad.reshape(head_count, 2 * row_length), bucket_table, precision=PRECISE
    )
    full_table = lax.dynamic_update_slice_in_dim(
        jnp.zeros(rel_table.shape, jnp.float32), table_part, seq_place * head_count, 0
    )
    packed = jnp.concatenate([full_table.reshape(-1), jnp.pad(stat_terms, (0, TILE - 4))])
    gate_up_near, packed, output_grad, attn_in_own, result = both(
        gate_up_near, packed, output_grad, attn_in_own, result
    )
    output_owned = scatter_grads(output_grad, groups)
    gate_up_pieces = gather_end(gate_up_owned, gate_up_near)
    down_pieces = gather_end(down_owned, down_near)
    (down_out,) = place_columns(down_pieces, place, [(0, 0, 0, unit_count)], [unit_count])
    summed = jnp.sum(lax.all_gather(packed.reshape(-1, TILE), "fsdp"), axis=0)
    summed, attn_in_parts = both(summed, attn_in_parts)
    summed = seq_sum(summed)
    attn_owned, summed, down_out, gate_up_pieces, attn_in_parts = both(
        attn_owned, summed, down_out, gate_up_pieces, attn_in_parts
    )
    attn_near = gather_begin(attn_owned)
    attn_in_grad = add_parts(attn_in_own, attn_in_parts)
    stream_grad = resid_grad + norm_back(attn_in_grad * attn_gain, normed_attn, scale_attn)
    stream_grad = stream_grad.astype(jnp.bfloat16)
    gate_out, up_out, ffn_sums = place_columns(
        gate_up_pieces, place, unit_moves, [unit_count] * 2, (w_gate, w_up)
    )
    attn_near, stream_grad, gate_out, up_out = both(attn_near, stream_grad, gate_out, up_out)
    attn_pieces = gather_end(attn_owned, attn_near)
    attn_pieces[-1][0], output_owned = both(attn_pieces[-1][0], output_owned)
    summed = summed.reshape(-1)
    output_near = gather_begin(output_owned, relay=False)
    attn_outs = place_columns(
        attn_pieces,
        place,
        qkv_moves[:-1],
        [column_count] * 3,
        (w_query, w_key, w_value),
    )
    output_near, attn_outs = both(output_near, attn_outs)
    query_out, key_out, value_out, attn_sums = attn_outs
    (output_out,) = place_columns(
        gather_end(output_owned, output_near), place, [(0, 0, 0, column_count)], [column_count]
    )
    gain_attn_grad = jnp.sum(attn_sums, axis=1) / gain_attn.astype(jnp.float32)
    gain_ffn_grad = jnp.sum(ffn_sums, axis=1) / gain_ffn.astype(jnp.float32)
    stat_totals = summed[rel_table.size : rel_table.size + 4]
    rms_stats = jnp.sqrt(stat_totals[0:3] / (stat_totals[3] * model_width))
    table_share = rel_table.shape[0] // fsdp_count
    rel_table_grad = lax.dynamic_slice_in_dim(
        summed[: rel_table.size].reshape(rel_table.shape),
        fsdp_place * table_share,
        table_share,
        0,
    )
    return (
        result.astype(jnp.bfloat16)[None],
        stream_grad[None],
        query_out,
        key_out,
        value_out,
        output_out,
        gain_attn_grad,
        rel_table_grad,
        gate_out,
        up_out,
        down_out,
        gain_ffn_grad,
        rms_stats,
    )


def solution(mesh):
    in_specs = (
        P("fsdp", "seq", None),
        P("fsdp", None),
        P(),
        P("fsdp", None),
        P("fsdp", None),
        P("fsdp", None),
        P("fsdp", None),
        P("fsdp"),
        P(),
        P("fsdp", None),
        P("fsdp", None),
        P("fsdp", None),
        P("fsdp"),
        P("fsdp", "seq", None),
    )
    out_specs = (
        P("fsdp", "seq", None),
        P("fsdp", "seq", None),
        P("fsdp", None),
        P("fsdp", None),
        P("fsdp", None),
        P("fsdp", None),
        P("fsdp"),
        P("fsdp", None),
        P("fsdp", None),
        P("fsdp", None),
        P("fsdp", None),
        P("fsdp"),
        P(),
    )
    return jax.shard_map(
        on_device, mesh=mesh, in_specs=in_specs, out_specs=out_specs, check_vma=False
    )
```

```python
import functools

import jax
import jax.numpy as jnp
from jax import lax
from jax.experimental import pallas as pl
from jax.experimental.pallas import tpu as pltpu
from jax.sharding import PartitionSpec as P

DH = 64


EPSILON = 1e-06
PRECISE = lax.Precision.HIGHEST
MASKED_SCORE = -1e30
TILE = 128
PAIR = 2 * DH
GELU_SCALE = 0.7978845608
GELU_CUBE = 0.044715
NO_COST = pl.CostEstimate(flops=0, bytes_accessed=0, transcendentals=0)
VMEM_BYTES = 56 * 1024 * 1024


def rows_dot(left, right):
    return lax.dot_general(
        left, right, (((0,), (0,)), ((), ())), preferred_element_type=jnp.float32
    )


def cols_dot(left, right):
    return lax.dot_general(
        left, right, (((1,), (1,)), ((), ())), preferred_element_type=jnp.float32
    )


def norm_back(grad_hat, normed, scale):
    return scale * (grad_hat - normed * jnp.mean(grad_hat * normed, axis=-1, keepdims=True))


def norm_backward_kernel(lengths, own_ref, up_ref, resid_ref, gain_ref, *refs):
    *parts, out_ref, low_ref = refs
    resid = resid_ref[...]
    scale = lax.rsqrt(jnp.mean(resid * resid, axis=-1, keepdims=True) + EPSILON)
    grad = own_ref[...].astype(jnp.float32)
    first = 0
    for length in lengths:
        part = parts[first][...]
        if length == 2:
            upper = pl.program_id(0) < pl.num_programs(0) // 2
            part = jnp.where(upper, part, parts[first + 1][...])
        grad = grad + part.astype(jnp.float32)
        first += length
    out = up_ref[...].astype(jnp.float32)
    out = out + norm_back(grad * gain_ref[...], resid * scale, scale)
    out_ref[...] = out
    low_ref[...] = out.astype(jnp.bfloat16)


def norm_backward(own, parts, upstream, resid, gain):
    rows, width = resid.shape
    block = min(64, rows // 2)
    steps = rows // block
    rowwise = pl.BlockSpec((block, width), lambda i: (i, 0))
    halves = [
        pl.BlockSpec((block, width), lambda i: (jnp.minimum(i, steps // 2 - 1), 0)),
        pl.BlockSpec((block, width), lambda i: (jnp.maximum(i - steps // 2, 0), 0)),
    ]
    lengths = tuple(len(part) for part in parts)
    part_specs = [spec for length in lengths for spec in (halves if length == 2 else [rowwise])]
    return pl.pallas_call(
        functools.partial(norm_backward_kernel, lengths),
        grid=(steps,),
        in_specs=[rowwise] * 3 + [pl.BlockSpec((1, width), lambda i: (0, 0))] + part_specs,
        out_specs=[rowwise, rowwise],
        out_shape=[
            jax.ShapeDtypeStruct((rows, width), jnp.float32),
            jax.ShapeDtypeStruct((rows, width), jnp.bfloat16),
        ],
        compiler_params=pltpu.CompilerParams(vmem_limit_bytes=VMEM_BYTES),
        cost_estimate=NO_COST,
        name="norm_backward",
    )(own, upstream, resid, gain[None, :], *[piece for part in parts for piece in part])


def half_lanes(shape, which):
    lane = lax.broadcasted_iota(jnp.int32, shape, 1)
    return (lane < DH) if which == 0 else (lane >= DH)


def fold_rows(tile):
    return jnp.sum(tile.reshape(tile.shape[0] // 8, 8, tile.shape[1]), axis=0)


def query_block(length):
    return min(length, max(256, 2**20 // length))


def whole_place(row, token_rows, place):
    return jnp.bitwise_xor(row // token_rows, place) * token_rows + row % token_rows


def bias_offsets(first, block, length, token_rows, place, tile):
    reach = length - TILE
    key_place = whole_place(tile * TILE, token_rows, place)
    group = min(block, token_rows)
    return [
        pl.multiple_of(
            whole_place(first + start, token_rows, place) + (reach - key_place), TILE
        )
        for start in range(0, block, group)
    ], group


def forward_kernel(
    block,
    token_rows,
    place_ref,
    qkv_ref,
    row_ref,
    col_ref,
    bias_ref,
    ctx_ref,
    e_ref,
    inv_ref,
    strip_ref,
    score_ref,
):
    length = qkv_ref.shape[0]
    q_ref = qkv_ref.at[:, :PAIR]
    k_ref = qkv_ref.at[:, PAIR : 2 * PAIR]
    v_ref = qkv_ref.at[:, 2 * PAIR :]
    tiles = length // TILE
    width = 2 * length
    place = place_ref[0]
    group = min(block, token_rows)
    values_t = jnp.transpose(v_ref[...])
    for head in range(2):
        wide = jnp.broadcast_to(bias_ref[0, head : head + 1, :], (TILE, width))
        strip_ref[head] = pltpu.roll(wide, width - (TILE - 1), 1, stride=1, stride_axis=0)

    def one_block(first):
        q_block = q_ref[pl.ds(first, block), :]
        segment_q = jnp.concatenate(
            [
                row_ref[
                    :,
                    pl.ds(
                        pl.multiple_of(whole_place(first + start, token_rows, place), TILE), group
                    ),
                ]
                for start in range(0, block, group)
            ],
            axis=1,
        )
        outs = []
        for head in range(2):
            q_head = jnp.where(half_lanes(q_block.shape, head), q_block, jnp.zeros_like(q_block))
            raw = cols_dot(k_ref[...], q_head)
            highest = jnp.full((8, block), -jnp.inf, jnp.float32)
            for tile in range(tiles):
                rows = slice(tile * TILE, (tile + 1) * TILE)
                offsets, _ = bias_offsets(first, block, length, token_rows, place, tile)
                bias = jnp.concatenate(
                    [strip_ref[head, :, pl.ds(offset, group)] for offset in offsets], axis=1
                )
                key_place = whole_place(tile * TILE, token_rows, place)
                segment_k = col_ref[pl.ds(pl.multiple_of(key_place, TILE), TILE), :]
                segment_k = jnp.concatenate([segment_k] * (block // TILE), axis=1)
                score = jnp.where(segment_k == segment_q, raw[rows, :] + bias, MASKED_SCORE)
                score_ref[head, rows, :] = score
                highest = jnp.maximum(
                    highest, jnp.max(score.reshape(TILE // 8, 8, block), axis=0)
                )
            top = jnp.max(highest, axis=0, keepdims=True)
            total = jnp.zeros((8, block), jnp.float32)
            for tile in range(tiles):
                rows = slice(tile * TILE, (tile + 1) * TILE)
                exponent = jnp.exp(score_ref[head, rows, :] - top)
                total = total + fold_rows(exponent)
                e_ref[head, rows, pl.ds(first, block)] = exponent.astype(jnp.bfloat16)
            inverse = 1.0 / jnp.sum(total, axis=0, keepdims=True)
            inv_ref[head, :, pl.ds(first, block)] = inverse
            context = jnp.dot(
                values_t[head * DH : (head + 1) * DH, :],
                e_ref[head, :, pl.ds(first, block)],
                preferred_element_type=jnp.float32,
            )
            outs.append(context * inverse)
        ctx_ref[pl.ds(first, block), :] = jnp.transpose(jnp.concatenate(outs, axis=0)).astype(
            jnp.bfloat16
        )

    for_blocks(length // block, block, one_block)


def for_blocks(count, block, body):
    if count == 1:
        body(0)
        return

    def step(index, carry):
        body(pl.multiple_of(index * block, block))
        return carry

    lax.fori_loop(0, count, step, 0)


def attention_forward(qkv, place, segment_row, segment_wide, bias_line, heads, token_rows):
    length = qkv.shape[0]
    block = query_block(length)
    pairs = heads // 2
    return pl.pallas_call(
        functools.partial(forward_kernel, block, token_rows),
        grid=(pairs,),
        in_specs=[
            pl.BlockSpec(memory_space=pltpu.SMEM),
            pl.BlockSpec((length, 3 * PAIR), lambda i: (0, i)),
            pl.BlockSpec((1, length), lambda i: (0, 0)),
            pl.BlockSpec((length, TILE), lambda i: (0, 0)),
            pl.BlockSpec((1, 2, 2 * length), lambda i: (i, 0, 0)),
        ],
        out_specs=[
            pl.BlockSpec((length, PAIR), lambda i: (0, i)),
            pl.BlockSpec((2, length, length), lambda i: (i, 0, 0)),
            pl.BlockSpec((2, 1, length), lambda i: (i, 0, 0)),
        ],
        out_shape=[
            jax.ShapeDtypeStruct((length, heads * DH), jnp.bfloat16),
            jax.ShapeDtypeStruct((heads, length, length), jnp.bfloat16),
            jax.ShapeDtypeStruct((heads, 1, length), jnp.float32),
        ],
        scratch_shapes=[
            pltpu.VMEM((2, TILE, 2 * length), jnp.float32),
            pltpu.VMEM((2, length, block), jnp.float32),
        ],
        compiler_params=pltpu.CompilerParams(vmem_limit_bytes=VMEM_BYTES),
        cost_estimate=NO_COST,
        name="attention_forward",
    )(place, qkv, segment_row, segment_wide, bias_line)


def backward_kernel(
    block,
    token_rows,
    place_ref,
    qkv_ref,
    d_ref,
    e_ref,
    inv_ref,
    grad_ref,
    line_ref,
    strip_ref,
    prob_ref,
    low_ref,
    key_sum,
    value_sum,
):
    length = qkv_ref.shape[0]
    q_ref = qkv_ref.at[:, :PAIR]
    k_ref = qkv_ref.at[:, PAIR : 2 * PAIR]
    v_ref = qkv_ref.at[:, 2 * PAIR :]
    tiles = length // TILE
    place = place_ref[0]
    keys_t = jnp.transpose(k_ref[...])
    strip_ref[...] = jnp.zeros_like(strip_ref)
    key_sum[...] = jnp.zeros_like(key_sum)
    value_sum[...] = jnp.zeros_like(value_sum)

    def one_block(first):
        q_block = q_ref[pl.ds(first, block), :]
        d_block = d_ref[pl.ds(first, block), :]
        outs = []
        for head in range(2):
            mask = half_lanes(q_block.shape, head)
            q_head = jnp.where(mask, q_block, jnp.zeros_like(q_block))
            inverse = inv_ref[head, :, pl.ds(first, block)]
            scale = jnp.transpose(jnp.broadcast_to(inverse, (PAIR, block)))
            d_head = jnp.where(mask, d_block.astype(jnp.float32) * scale, 0.0)
            d_head = d_head.astype(jnp.bfloat16)
            prob_ref[head] = cols_dot(v_ref[...], d_head)
            value_sum[...] += jnp.dot(
                e_ref[head, :, pl.ds(first, block)], d_head, preferred_element_type=jnp.float32
            )
            total = jnp.zeros((8, block), jnp.float32)
            for tile in range(tiles):
                rows = slice(tile * TILE, (tile + 1) * TILE)
                exponent = e_ref[head, rows, pl.ds(first, block)].astype(jnp.float32)
                total = total + fold_rows(exponent * prob_ref[head, rows, :])
            centre = jnp.sum(total, axis=0, keepdims=True) * inverse
            for tile in range(tiles):
                rows = slice(tile * TILE, (tile + 1) * TILE)
                exponent = e_ref[head, rows, pl.ds(first, block)].astype(jnp.float32)
                grad = exponent * (prob_ref[head, rows, :] - centre)
                offsets, group = bias_offsets(first, block, length, token_rows, place, tile)
                for part, offset in enumerate(offsets):
                    at = pl.ds(offset, group)
                    strip_ref[head, :, at] = (
                        strip_ref[head, :, at] + grad[:, part * group : (part + 1) * group]
                    )
                low_ref[head, rows, :] = grad.astype(jnp.bfloat16)
            key_sum[...] += jnp.dot(low_ref[head], q_head, preferred_element_type=jnp.float32)
            outs.append(
                jnp.dot(
                    keys_t[head * DH : (head + 1) * DH, :],
                    low_ref[head],
                    preferred_element_type=jnp.float32,
                )
            )
        grad_ref[pl.ds(first, block), :PAIR] = jnp.transpose(
            jnp.concatenate(outs, axis=0)
        ).astype(jnp.bfloat16)

    for_blocks(length // block, block, one_block)
    grad_ref[:, PAIR : 2 * PAIR] = key_sum[...].astype(jnp.bfloat16)
    grad_ref[:, 2 * PAIR :] = value_sum[...].astype(jnp.bfloat16)
    for head in range(2):
        turned = strip_ref[head]
        while turned.shape[0] > 1:
            half = turned.shape[0] // 2
            turned = pltpu.roll(turned[:half], half, 1) + turned[half:]
        line_ref[0, head : head + 1, :] = turned


def attention_backward(qkv, place, d, e, inv, heads, token_rows):
    length = qkv.shape[0]
    block = query_block(length)
    pairs = heads // 2
    triple = pl.BlockSpec((length, 3 * PAIR), lambda i: (0, i))
    return pl.pallas_call(
        functools.partial(backward_kernel, block, token_rows),
        grid=(pairs,),
        in_specs=[
            pl.BlockSpec(memory_space=pltpu.SMEM),
            triple,
            pl.BlockSpec((length, PAIR), lambda i: (0, i)),
            pl.BlockSpec((2, length, length), lambda i: (i, 0, 0)),
            pl.BlockSpec((2, 1, length), lambda i: (i, 0, 0)),
        ],
        out_specs=[triple, pl.BlockSpec((1, 2, 2 * length), lambda i: (i, 0, 0))],
        out_shape=[
            jax.ShapeDtypeStruct((length, 3 * heads * DH), jnp.bfloat16),
            jax.ShapeDtypeStruct((pairs, 2, 2 * length), jnp.float32),
        ],
        scratch_shapes=[
            pltpu.VMEM((2, TILE, 2 * length), jnp.float32),
            pltpu.VMEM((2, length, block), jnp.float32),
            pltpu.VMEM((2, length, block), jnp.bfloat16),
            pltpu.VMEM((length, PAIR), jnp.float32),
            pltpu.VMEM((length, PAIR), jnp.float32),
        ],
        compiler_params=pltpu.CompilerParams(vmem_limit_bytes=VMEM_BYTES),
        cost_estimate=NO_COST,
        name="attention_backward",
    )(place, qkv, d, e, inv)


def swap(piece, axis, step):
    return lax.ppermute(piece, axis, [(i, i ^ step) for i in range(lax.axis_size(axis))])


def gather_begin(piece, relay=True):
    count = lax.axis_size("seq")
    steps = (1, 2) if count == 4 and relay else range(1, count)
    return tuple(swap(piece, "seq", step) for step in steps)


def gather_end(piece, near):
    if len(near) != 2:
        return [[part] for part in (piece, *near)]
    first, second = near
    half = piece.shape[0] // 2
    upper = swap(second[:half], "seq", 1)
    lower = swap(first[half:], "seq", 2)
    return [[piece], [first], [second], [upper, lower]]


def joined(parts):
    return jnp.concatenate([part for pieces in parts for part in pieces], axis=0)


def gather_rows(piece):
    return joined(gather_end(piece, gather_begin(piece)))


def low_dot(rows, weights):
    return cols_dot(rows, weights).astype(jnp.bfloat16)


def split_terms(terms):
    count = lax.axis_size("seq")
    size = terms.shape[0] // (count - 1)
    return (terms[: 2 * size], terms[2 * size :]) if count == 4 else (terms, None)


def scatter_begin(far):
    if far is None:
        return ()
    half = far.shape[0] // 2
    return swap(far[:half], "seq", 1), swap(far[half:], "seq", 2)


def scatter_add(near, passing):
    if not passing:
        size = near.shape[0] // (lax.axis_size("seq") - 1)
        return tuple(near[start : start + size] for start in range(0, near.shape[0], size))
    size = near.shape[0] // 2
    upper, lower = (part.astype(jnp.float32) for part in passing)
    first = near[:size].astype(jnp.float32) + jnp.pad(lower, ((size // 2, 0), (0, 0)))
    second = near[size:].astype(jnp.float32) + jnp.pad(upper, ((0, size // 2), (0, 0)))
    return first.astype(jnp.bfloat16), second.astype(jnp.bfloat16)


def scatter_end(sums):
    return tuple(swap(part, "seq", k + 1) for k, part in enumerate(sums))


def scatter_early(near):
    if lax.axis_size("seq") != 4:
        return ()
    size = near.shape[0] // 2
    half = size // 2
    return swap(near[:half], "seq", 1), swap(near[size + half :], "seq", 2)


def scatter_late(near, passing, early):
    if not passing:
        return [(part,) for part in scatter_end(scatter_add(near, passing))]
    size = near.shape[0] // 2
    half = size // 2
    upper, lower = (part.astype(jnp.float32) for part in passing)
    first = near[half:size].astype(jnp.float32) + lower
    second = near[size : size + half].astype(jnp.float32) + upper
    first_lower = swap(first.astype(jnp.bfloat16), "seq", 1)
    second_upper = swap(second.astype(jnp.bfloat16), "seq", 2)
    first_upper, second_lower = early
    return [(first_upper, first_lower), (second_upper, second_lower)]


def add_parts(own, received):
    return own + sum(part.astype(jnp.float32) for part in received)


def scatter_sum(rows, weights):
    size = rows.shape[0] // lax.axis_size("seq")
    near, far = split_terms(low_dot(rows[size:], weights))
    received = scatter_end(scatter_add(near, scatter_begin(far)))
    return add_parts(cols_dot(rows[:size], weights), received)


def seq_sum(values):
    level = [values] + [swap(values, "seq", step) for step in range(1, lax.axis_size("seq"))]
    while len(level) > 1:
        level = [level[i] + level[i + 1] for i in range(0, len(level), 2)]
    return level[0]


def feed_forward_kernel(tile, x_ref, w_ref, act_ref, gelu_ref, slope_ref):
    rows = x_ref.shape[0]
    chunk = min(512, rows)
    for start in range(0, rows, chunk):
        at = slice(start, start + chunk)
        both = jnp.dot(x_ref[at, :], w_ref[...], preferred_element_type=jnp.float32)
        gate, up = both[:, :tile], both[:, tile:]
        square = gate * gate
        tanh = jnp.tanh(GELU_SCALE * gate * (1.0 + GELU_CUBE * square))
        half_up = 0.5 * (1.0 + tanh)
        gelu = gate * half_up
        bend = 0.5 * GELU_SCALE * gate * (1.0 - tanh * tanh) * (1.0 + 3.0 * GELU_CUBE * square)
        act_ref[at, :] = (gelu * up).astype(jnp.bfloat16)
        gelu_ref[at, :] = gelu.astype(jnp.bfloat16)
        slope_ref[at, :] = (up * (half_up + bend)).astype(jnp.bfloat16)


def feed_forward(rows, weights, tile):
    length, model_width = rows.shape
    units = weights.shape[1] // 2
    block = pl.BlockSpec((length, tile), lambda j: (0, j))
    return pl.pallas_call(
        functools.partial(feed_forward_kernel, tile),
        grid=(units // tile,),
        in_specs=[
            pl.BlockSpec((length, model_width), lambda j: (0, 0)),
            pl.BlockSpec((model_width, 2 * tile), lambda j: (0, j)),
        ],
        out_specs=[block, block, block],
        out_shape=[
            jax.ShapeDtypeStruct((length, units), jnp.bfloat16),
            jax.ShapeDtypeStruct((length, units), jnp.bfloat16),
            jax.ShapeDtypeStruct((length, units), jnp.bfloat16),
        ],
        compiler_params=pltpu.CompilerParams(vmem_limit_bytes=VMEM_BYTES),
        cost_estimate=NO_COST,
        name="feed_forward",
    )(rows, weights)


def feed_forward_back_kernel(tile, d_ref, w_ref, gelu_ref, slope_ref, grad_ref):
    rows = d_ref.shape[0]
    chunk = min(512, rows)
    for start in range(0, rows, chunk):
        at = slice(start, start + chunk)
        grad = jnp.dot(d_ref[at, :], w_ref[...], preferred_element_type=jnp.float32)
        grad_ref[at, :tile] = (grad * slope_ref[at, :].astype(jnp.float32)).astype(jnp.bfloat16)
        grad_ref[at, tile:] = (grad * gelu_ref[at, :].astype(jnp.float32)).astype(jnp.bfloat16)


def feed_forward_back(grad_rows, weights, gelu, slope, tile):
    length, model_width = grad_rows.shape
    units = weights.shape[1]
    block = pl.BlockSpec((length, tile), lambda j: (0, j))
    return pl.pallas_call(
        functools.partial(feed_forward_back_kernel, tile),
        grid=(units // tile,),
        in_specs=[
            pl.BlockSpec((length, model_width), lambda j: (0, 0)),
            pl.BlockSpec((model_width, tile), lambda j: (0, j)),
            block,
            block,
        ],
        out_specs=pl.BlockSpec((length, 2 * tile), lambda j: (0, j)),
        out_shape=jax.ShapeDtypeStruct((length, 2 * units), jnp.bfloat16),
        compiler_params=pltpu.CompilerParams(vmem_limit_bytes=VMEM_BYTES),
        cost_estimate=NO_COST,
        name="feed_forward_back",
    )(grad_rows, weights, gelu, slope)


def place_kernel(moves, lengths, block, widths, weighed, place_ref, *refs):
    count = sum(lengths)
    weights = refs[count : count + len(weighed)]
    outs = refs[count + len(weighed) : count + len(weighed) + len(widths)]
    total = jnp.zeros((block, TILE), jnp.float32)
    first = 0
    for step, length in enumerate(lengths):
        pieces = refs[first : first + length]
        first += length
        owner = jnp.bitwise_xor(place_ref[0], step)
        for out, source, target, size in moves:
            at = pl.ds(pl.multiple_of(owner * widths[out] + target, TILE), size)
            part = pieces[0][:, source : source + size]
            if length == 2:
                upper = pl.program_id(0) < pl.num_programs(0) // 2
                part = jnp.where(upper, part, pieces[1][:, source : source + size])
            part = part.astype(jnp.float32)
            outs[out][:, at] = part
            if out in weighed:
                part = part * weights[weighed.index(out)][:, at].astype(jnp.float32)
                for start in range(0, size, TILE):
                    total = total + part[:, start : start + TILE]
    if weighed:
        refs[-1][...] = total


def place_columns(parts, place, moves, widths, weights=()):
    lengths = tuple(len(pieces) for pieces in parts)
    count = lax.axis_size("seq")
    rows, width = parts[0][0].shape
    block = min(64, rows // 2)
    steps = rows // block

    def wide(size):
        return pl.BlockSpec((block, size), lambda i: (i, 0))

    def piece_specs(length):
        if length == 1:
            return [wide(width)]
        half = steps // 2
        return [
            pl.BlockSpec((block, width), lambda i: (jnp.minimum(i, half - 1), 0)),
            pl.BlockSpec((block, width), lambda i: (jnp.maximum(i - half, 0), 0)),
        ]

    whole = [wide(count * size) for size in widths]
    sums = [wide(TILE)] if weights else []
    shapes = [count * size for size in widths] + [TILE] * len(sums)
    weighed = tuple(range(len(weights)))
    return pl.pallas_call(
        functools.partial(place_kernel, moves, lengths, block, widths, weighed),
        grid=(steps,),
        in_specs=[pl.BlockSpec(memory_space=pltpu.SMEM)]
        + [spec for length in lengths for spec in piece_specs(length)]
        + whole[: len(weights)],
        out_specs=whole + sums,
        out_shape=[jax.ShapeDtypeStruct((rows, size), jnp.float32) for size in shapes],
        compiler_params=pltpu.CompilerParams(vmem_limit_bytes=VMEM_BYTES),
        cost_estimate=pl.CostEstimate(
            flops=0, bytes_accessed=8 * rows * sum(shapes), transcendentals=0
        ),
        name="place_columns",
    )(place, *[piece for pieces in parts for piece in pieces], *weights)


def take_kernel(moves, count, place_ref, *refs):
    out_ref = refs[count]
    for which, source, target, size in moves:
        out_ref[:, source : source + size] = refs[which][:, target : target + size]


def take_columns(place, weights, moves, counts):
    rows = weights[0].shape[0]
    block = min(128, rows)
    width = sum(counts)

    def chosen(count):
        return pl.BlockSpec((block, count), lambda i, place_ref: (i, place_ref[0]))

    return pl.pallas_call(
        functools.partial(take_kernel, moves, len(weights)),
        grid_spec=pltpu.PrefetchScalarGridSpec(
            num_scalar_prefetch=1,
            grid=(rows // block,),
            in_specs=[chosen(count) for count in counts],
            out_specs=pl.BlockSpec((block, width), lambda i, place_ref: (i, 0)),
        ),
        out_shape=jax.ShapeDtypeStruct((rows, width), weights[0].dtype),
        compiler_params=pltpu.CompilerParams(vmem_limit_bytes=VMEM_BYTES),
        cost_estimate=NO_COST,
        name="take_columns",
    )(place, *weights)


def turn_kernel(core_ref, own_in, other_in, own_ref, other_ref):
    own_ref[...] = jnp.transpose(own_in[...])
    other_ref[...] = jnp.transpose(other_in[...])


def turn_halves(rows, core, groups):
    length, width = rows.shape
    size = width // groups

    def chosen(side):
        return pl.BlockSpec(
            (length, size), lambda i, core_ref: (0, 2 * i + jnp.bitwise_xor(core_ref[0], side))
        )

    half = jax.ShapeDtypeStruct((width // 2, length), rows.dtype)
    block = pl.BlockSpec((size, length), lambda i, core_ref: (i, 0))
    return pl.pallas_call(
        turn_kernel,
        grid_spec=pltpu.PrefetchScalarGridSpec(
            num_scalar_prefetch=1,
            grid=(groups // 2,),
            in_specs=[chosen(0), chosen(1)],
            out_specs=[block, block],
        ),
        out_shape=[half, half],
        compiler_params=pltpu.CompilerParams(vmem_limit_bytes=VMEM_BYTES),
        cost_estimate=NO_COST,
        name="turn_halves",
    )(core, rows, rows)


def added_dot_kernel(left_ref, right_ref, added_ref, out_ref):
    rows = left_ref.shape[0]
    chunk = min(512, rows)
    for start in range(0, rows, chunk):
        at = slice(start, start + chunk)
        product = jnp.dot(left_ref[at, :], right_ref[...], preferred_element_type=jnp.float32)
        out_ref[at, :] = (product + added_ref[at, :].astype(jnp.float32)).astype(jnp.bfloat16)


def added_dot(left, right, added):
    rows, depth = left.shape
    width = right.shape[1]
    tile = next(t for t in (512, 256, 128) if width % t == 0)
    column = pl.BlockSpec((rows, tile), lambda j: (0, j))
    return pl.pallas_call(
        added_dot_kernel,
        grid=(width // tile,),
        in_specs=[
            pl.BlockSpec((rows, depth), lambda j: (0, 0)),
            pl.BlockSpec((depth, tile), lambda j: (0, j)),
            column,
        ],
        out_specs=column,
        out_shape=jax.ShapeDtypeStruct((rows, width), jnp.bfloat16),
        compiler_params=pltpu.CompilerParams(vmem_limit_bytes=VMEM_BYTES),
        cost_estimate=NO_COST,
        name="added_dot",
    )(left, right, added)


def both(*values):
    return lax.optimization_barrier(values)


def on_device(
    tokens,
    segments,
    buckets,
    w_query,
    w_key,
    w_value,
    w_attn_out,
    gain_attn,
    rel_table,
    w_gate,
    w_up,
    w_down,
    gain_ffn,
    out_grad,
):
    token_rows = tokens.shape[1]
    model_width = tokens.shape[2]
    ffn_width = w_gate.shape[1]
    segment_row = segments[0]
    row_length = segment_row.shape[0]
    seq_count = lax.axis_size("seq")
    fsdp_count = lax.axis_size("fsdp")
    seq_place = lax.axis_index("seq")
    fsdp_place = lax.axis_index("fsdp")
    place = seq_place.astype(jnp.int32).reshape(1)
    head_count = model_width // seq_count // DH
    column_count = model_width // seq_count
    unit_count = ffn_width // seq_count

    tile = 256 if unit_count % 256 == 0 else 128
    pairs = head_count // 2

    def gather_weights(piece):
        return lax.all_gather(piece, "fsdp", axis=0, tiled=True)

    qkv_moves = [
        (which, (3 * pair + which) * PAIR, pair * PAIR, PAIR)
        for pair in range(pairs)
        for which in range(3)
    ] + [(3, 3 * column_count, 0, column_count)]
    unit_moves = [
        (which, (2 * block + which) * tile, block * tile, tile)
        for block in range(unit_count // tile)
        for which in range(2)
    ]
    attn_part = take_columns(
        place, (w_query, w_key, w_value, w_attn_out), qkv_moves, [column_count] * 4
    )
    attn_w = gather_weights(attn_part)
    gains = lax.all_gather(jnp.stack([gain_attn, gain_ffn]), "fsdp", axis=1, tiled=True)
    qkv_w = attn_w[:, : 3 * column_count]
    output_w = attn_w[:, 3 * column_count :]

    table_rows = jnp.pad(buckets[::-1], (0, 1), constant_values=-1)
    bucket_table = (
        table_rows[:, None] == jnp.arange(rel_table.shape[1], dtype=jnp.int32)[None, :]
    ).astype(jnp.float32)
    local_table = lax.dynamic_slice_in_dim(rel_table, seq_place * head_count, head_count, 0)
    bias_line = jnp.dot(local_table, jnp.transpose(bucket_table), precision=PRECISE)
    bias_line = bias_line.reshape(head_count // 2, 2, 2 * row_length)
    segment_wide = jnp.broadcast_to(segment_row[:, None], (row_length, TILE))

    stream = tokens[0].astype(jnp.float32)
    scale_attn = lax.rsqrt(jnp.mean(stream * stream, axis=-1, keepdims=True) + EPSILON)
    normed_attn = stream * scale_attn

    stream_near = gather_begin(tokens[0])
    stream_near, gains = both(stream_near, gains)
    attn_gain = gains[0].astype(jnp.float32)
    ffn_gain = gains[1].astype(jnp.float32)
    stream_rows = joined(gather_end(tokens[0], stream_near))
    gate_up_part = take_columns(place, (w_gate, w_up), unit_moves, [unit_count] * 2)
    gate_up_part, stream_rows = both(gate_up_part, stream_rows)
    gate_up_w = gather_weights(gate_up_part)
    stream_rows = stream_rows.astype(jnp.float32)
    rows_scale = lax.rsqrt(jnp.mean(stream_rows * stream_rows, axis=-1, keepdims=True) + EPSILON)
    attn_rows = (stream_rows * rows_scale * attn_gain).astype(jnp.bfloat16)
    ff_grad_rows = gather_rows(out_grad[0])
    attn_rows, ff_grad_rows = both(attn_rows, ff_grad_rows)

    qkv = jnp.dot(attn_rows, qkv_w, preferred_element_type=jnp.float32).astype(jnp.bfloat16)
    down_part, qkv = both(
        lax.dynamic_slice_in_dim(w_down, seq_place * unit_count, unit_count, 1), qkv
    )
    down_w = gather_weights(down_part)
    context, exponents, inverse = attention_forward(
        qkv, place, segments, segment_wide, bias_line, head_count, token_rows
    )

    attn_out = scatter_sum(context, output_w)
    chips = fsdp_count // 2
    core = (fsdp_place % 2).astype(jnp.int32).reshape(1)
    groups = [[2 * chip + side for chip in range(chips)] for side in range(2)]

    def scatter_grads(grads, axis_index_groups=None):
        return lax.psum_scatter(
            grads,
            "fsdp",
            scatter_dimension=0,
            tiled=True,
            axis_index_groups=axis_index_groups,
        )

    resid = stream + attn_out
    scale_ffn = lax.rsqrt(jnp.mean(resid * resid, axis=-1, keepdims=True) + EPSILON)
    normed_ffn = resid * scale_ffn
    ffn_rows = gather_rows((normed_ffn * ffn_gain).astype(jnp.bfloat16))

    hidden, gelu, slope = feed_forward(ffn_rows, gate_up_w, tile)

    down_grad = rows_dot(ff_grad_rows, hidden).astype(jnp.bfloat16)
    down_owned = scatter_grads(down_grad)
    down_grad, hidden, gelu = both(down_grad, hidden, gelu)
    away = row_length // seq_count
    passed = 3 * away if seq_count == 4 else row_length
    ff_far = low_dot(hidden[passed:], down_w) if seq_count == 4 else None
    ff_far, hidden, gelu = both(ff_far, hidden, gelu)
    ff_passing = scatter_begin(ff_far)
    unit_grad = feed_forward_back(ff_grad_rows, down_w, gelu, slope, tile)
    unit_far = low_dot(unit_grad[passed:], gate_up_w) if seq_count == 4 else None
    unit_far, unit_grad, ff_passing = both(unit_far, unit_grad, ff_passing)
    unit_passing = scatter_begin(unit_far)
    unit_terms = low_dot(unit_grad[:passed], gate_up_w)
    unit_early = scatter_early(unit_terms[away:])
    unit_terms, unit_grad, unit_passing = both(unit_terms, unit_grad, unit_passing)
    unit_parts = scatter_late(unit_terms[away:], unit_passing, unit_early)
    gate_up_grad = rows_dot(ffn_rows, unit_grad).astype(jnp.bfloat16)
    gate_up_grad, unit_parts = both(gate_up_grad, unit_parts)
    gate_up_owned = scatter_grads(gate_up_grad)
    resid_grad, attn_grad = norm_backward(unit_terms, unit_parts, out_grad[0], resid, ffn_gain)
    attn_grad, hidden, down_owned = both(attn_grad, hidden, down_owned)
    attn_grad_rows = gather_rows(attn_grad)
    ff_near = low_dot(hidden[away:passed], down_w)
    ff_sums = scatter_add(ff_near, ff_passing)
    attn_grad_rows, ff_sums, down_owned = both(attn_grad_rows, ff_sums, down_owned)
    context_grad = jnp.dot(
        attn_grad_rows, output_w, preferred_element_type=jnp.float32
    ).astype(jnp.bfloat16)
    ff_parts = scatter_end(ff_sums)
    down_near = gather_begin(down_owned, relay=False)
    qkv_grad, line_grad = attention_backward(
        qkv, place, context_grad, exponents, inverse, head_count, token_rows
    )
    qkv_terms = low_dot(qkv_grad[away:], qkv_w)
    qkv_terms, qkv_grad, ff_parts, down_near = both(qkv_terms, qkv_grad, ff_parts, down_near)
    qkv_near, qkv_far = split_terms(qkv_terms)
    qkv_passing = scatter_begin(qkv_far)
    attn_grads = rows_dot(attn_rows, qkv_grad).astype(jnp.bfloat16)
    attn_grads, context, qkv_grad, attn_grad_rows, qkv_passing, gate_up_owned, hidden = both(
        attn_grads, context, qkv_grad, attn_grad_rows, qkv_passing, gate_up_owned, hidden
    )
    attn_owned = scatter_grads(attn_grads)
    gate_up_near = gather_begin(gate_up_owned)
    attn_in_parts = scatter_end(scatter_add(qkv_near, qkv_passing))
    output_own, output_other = turn_halves(attn_grad_rows, core, fsdp_count)
    output_away = jnp.dot(
        output_other, context, preferred_element_type=jnp.float32
    ).astype(jnp.bfloat16)
    output_added = swap(output_away, "fsdp", 1)
    attn_in_own = cols_dot(qkv_grad[:away], qkv_w)
    output_grad = added_dot(output_own, context, output_added)
    ff_out = add_parts(cols_dot(hidden[:away], down_w), ff_parts)
    result = resid + ff_out
    own_segments = lax.dynamic_slice_in_dim(segment_row, seq_place * token_rows, token_rows, 0)
    valid = (own_segments >= 0).astype(jnp.float32)
    stat_terms = jnp.stack(
        [
            jnp.sum(valid * jnp.sum(result * result, axis=-1)),
            jnp.sum(valid * jnp.sum(attn_out * attn_out, axis=-1)),
            jnp.sum(valid * jnp.sum(ff_out * ff_out, axis=-1)),
            jnp.sum(valid),
        ]
    )
    table_part = jnp.dot(
        line_grad.reshape(head_count, 2 * row_length), bucket_table, precision=PRECISE
    )
    full_table = lax.dynamic_update_slice_in_dim(
        jnp.zeros(rel_table.shape, jnp.float32), table_part, seq_place * head_count, 0
    )
    packed = jnp.concatenate([full_table.reshape(-1), jnp.pad(stat_terms, (0, TILE - 4))])
    gate_up_near, packed, output_grad, attn_in_own, result = both(
        gate_up_near, packed, output_grad, attn_in_own, result
    )
    output_owned = scatter_grads(output_grad, groups)
    gate_up_pieces = gather_end(gate_up_owned, gate_up_near)
    down_pieces = gather_end(down_owned, down_near)
    (down_out,) = place_columns(down_pieces, place, [(0, 0, 0, unit_count)], [unit_count])
    summed = jnp.sum(lax.all_gather(packed.reshape(-1, TILE), "fsdp"), axis=0)
    summed, attn_in_parts = both(summed, attn_in_parts)
    summed = seq_sum(summed)
    attn_owned, summed, down_out, gate_up_pieces, attn_in_parts = both(
        attn_owned, summed, down_out, gate_up_pieces, attn_in_parts
    )
    attn_near = gather_begin(attn_owned)
    attn_in_grad = add_parts(attn_in_own, attn_in_parts)
    stream_grad = resid_grad + norm_back(attn_in_grad * attn_gain, normed_attn, scale_attn)
    stream_grad = stream_grad.astype(jnp.bfloat16)
    gate_out, up_out, ffn_sums = place_columns(
        gate_up_pieces, place, unit_moves, [unit_count] * 2, (w_gate, w_up)
    )
    attn_near, stream_grad, gate_out, up_out = both(attn_near, stream_grad, gate_out, up_out)
    attn_pieces = gather_end(attn_owned, attn_near)
    attn_pieces[-1][0], output_owned = both(attn_pieces[-1][0], output_owned)
    summed = summed.reshape(-1)
    output_near = gather_begin(output_owned, relay=False)
    attn_outs = place_columns(
        attn_pieces,
        place,
        qkv_moves[:-1],
        [column_count] * 3,
        (w_query, w_key, w_value),
    )
    output_near, attn_outs = both(output_near, attn_outs)
    query_out, key_out, value_out, attn_sums = attn_outs
    (output_out,) = place_columns(
        gather_end(output_owned, output_near), place, [(0, 0, 0, column_count)], [column_count]
    )
    gain_attn_grad = jnp.sum(attn_sums, axis=1) / gain_attn.astype(jnp.float32)
    gain_ffn_grad = jnp.sum(ffn_sums, axis=1) / gain_ffn.astype(jnp.float32)
    stat_totals = summed[rel_table.size : rel_table.size + 4]
    rms_stats = jnp.sqrt(stat_totals[0:3] / (stat_totals[3] * model_width))
    table_share = rel_table.shape[0] // fsdp_count
    rel_table_grad = lax.dynamic_slice_in_dim(
        summed[: rel_table.size].reshape(rel_table.shape),
        fsdp_place * table_share,
        table_share,
        0,
    )
    return (
        result.astype(jnp.bfloat16)[None],
        stream_grad[None],
        query_out,
        key_out,
        value_out,
        output_out,
        gain_attn_grad,
        rel_table_grad,
        gate_out,
        up_out,
        down_out,
        gain_ffn_grad,
        rms_stats,
    )


def solution(mesh):
    in_specs = (
        P("fsdp", "seq", None),
        P("fsdp", None),
        P(),
        P("fsdp", None),
        P("fsdp", None),
        P("fsdp", None),
        P("fsdp", None),
        P("fsdp"),
        P(),
        P("fsdp", None),
        P("fsdp", None),
        P("fsdp", None),
        P("fsdp"),
        P("fsdp", "seq", None),
    )
    out_specs = (
        P("fsdp", "seq", None),
        P("fsdp", "seq", None),
        P("fsdp", None),
        P("fsdp", None),
        P("fsdp", None),
        P("fsdp", None),
        P("fsdp"),
        P("fsdp", None),
        P("fsdp", None),
        P("fsdp", None),
        P("fsdp", None),
        P("fsdp"),
        P(),
    )
    return jax.shard_map(
        on_device, mesh=mesh, in_specs=in_specs, out_specs=out_specs, check_vma=False
    )
```

```python
import functools

import jax
import jax.numpy as jnp
from jax import lax
from jax.experimental import pallas as pl
from jax.experimental.pallas import tpu as pltpu
from jax.sharding import PartitionSpec as P

DH = 64


EPSILON = 1e-06
PRECISE = lax.Precision.HIGHEST
MASKED_SCORE = -1e30
TILE = 128
PAIR = 2 * DH
GELU_SCALE = 0.7978845608
GELU_CUBE = 0.044715
NO_COST = pl.CostEstimate(flops=0, bytes_accessed=0, transcendentals=0)
VMEM_BYTES = 56 * 1024 * 1024


def rows_dot(left, right):
    return lax.dot_general(
        left, right, (((0,), (0,)), ((), ())), preferred_element_type=jnp.float32
    )


def cols_dot(left, right):
    return lax.dot_general(
        left, right, (((1,), (1,)), ((), ())), preferred_element_type=jnp.float32
    )


def norm_back(grad_hat, normed, scale):
    return scale * (grad_hat - normed * jnp.mean(grad_hat * normed, axis=-1, keepdims=True))


def norm_backward_kernel(lengths, own_ref, up_ref, resid_ref, gain_ref, *refs):
    *parts, out_ref, low_ref = refs
    resid = resid_ref[...]
    scale = lax.rsqrt(jnp.mean(resid * resid, axis=-1, keepdims=True) + EPSILON)
    grad = own_ref[...].astype(jnp.float32)
    first = 0
    for length in lengths:
        part = parts[first][...]
        if length == 2:
            upper = pl.program_id(0) < pl.num_programs(0) // 2
            part = jnp.where(upper, part, parts[first + 1][...])
        grad = grad + part.astype(jnp.float32)
        first += length
    out = up_ref[...].astype(jnp.float32)
    out = out + norm_back(grad * gain_ref[...], resid * scale, scale)
    out_ref[...] = out
    low_ref[...] = out.astype(jnp.bfloat16)


def norm_backward(own, parts, upstream, resid, gain):
    rows, width = resid.shape
    block = min(64, rows // 2)
    steps = rows // block
    rowwise = pl.BlockSpec((block, width), lambda i: (i, 0))
    halves = [
        pl.BlockSpec((block, width), lambda i: (jnp.minimum(i, steps // 2 - 1), 0)),
        pl.BlockSpec((block, width), lambda i: (jnp.maximum(i - steps // 2, 0), 0)),
    ]
    lengths = tuple(len(part) for part in parts)
    part_specs = [spec for length in lengths for spec in (halves if length == 2 else [rowwise])]
    return pl.pallas_call(
        functools.partial(norm_backward_kernel, lengths),
        grid=(steps,),
        in_specs=[rowwise] * 3 + [pl.BlockSpec((1, width), lambda i: (0, 0))] + part_specs,
        out_specs=[rowwise, rowwise],
        out_shape=[
            jax.ShapeDtypeStruct((rows, width), jnp.float32),
            jax.ShapeDtypeStruct((rows, width), jnp.bfloat16),
        ],
        compiler_params=pltpu.CompilerParams(vmem_limit_bytes=VMEM_BYTES),
        cost_estimate=NO_COST,
        name="norm_backward",
    )(own, upstream, resid, gain[None, :], *[piece for part in parts for piece in part])


def half_lanes(shape, which):
    lane = lax.broadcasted_iota(jnp.int32, shape, 1)
    return (lane < DH) if which == 0 else (lane >= DH)


def fold_rows(tile):
    return jnp.sum(tile.reshape(tile.shape[0] // 8, 8, tile.shape[1]), axis=0)


def query_block(length):
    return min(length, max(256, 2**20 // length))


def whole_place(row, token_rows, place):
    return jnp.bitwise_xor(row // token_rows, place) * token_rows + row % token_rows


def bias_offsets(first, block, length, token_rows, place, tile):
    reach = length - TILE
    key_place = whole_place(tile * TILE, token_rows, place)
    group = min(block, token_rows)
    return [
        pl.multiple_of(
            whole_place(first + start, token_rows, place) + (reach - key_place), TILE
        )
        for start in range(0, block, group)
    ], group


def forward_kernel(
    block,
    token_rows,
    place_ref,
    qkv_ref,
    row_ref,
    col_ref,
    bias_ref,
    ctx_ref,
    e_ref,
    inv_ref,
    strip_ref,
    score_ref,
):
    length = qkv_ref.shape[0]
    q_ref = qkv_ref.at[:, :PAIR]
    k_ref = qkv_ref.at[:, PAIR : 2 * PAIR]
    v_ref = qkv_ref.at[:, 2 * PAIR :]
    tiles = length // TILE
    width = 2 * length
    place = place_ref[0]
    group = min(block, token_rows)
    values_t = jnp.transpose(v_ref[...])
    for head in range(2):
        wide = jnp.broadcast_to(bias_ref[0, head : head + 1, :], (TILE, width))
        strip_ref[head] = pltpu.roll(wide, width - (TILE - 1), 1, stride=1, stride_axis=0)

    def one_block(first):
        q_block = q_ref[pl.ds(first, block), :]
        segment_q = jnp.concatenate(
            [
                row_ref[
                    :,
                    pl.ds(
                        pl.multiple_of(whole_place(first + start, token_rows, place), TILE), group
                    ),
                ]
                for start in range(0, block, group)
            ],
            axis=1,
        )
        outs = []
        for head in range(2):
            q_head = jnp.where(half_lanes(q_block.shape, head), q_block, jnp.zeros_like(q_block))
            raw = cols_dot(k_ref[...], q_head)
            highest = jnp.full((8, block), -jnp.inf, jnp.float32)
            for tile in range(tiles):
                rows = slice(tile * TILE, (tile + 1) * TILE)
                offsets, _ = bias_offsets(first, block, length, token_rows, place, tile)
                bias = jnp.concatenate(
                    [strip_ref[head, :, pl.ds(offset, group)] for offset in offsets], axis=1
                )
                key_place = whole_place(tile * TILE, token_rows, place)
                segment_k = col_ref[pl.ds(pl.multiple_of(key_place, TILE), TILE), :]
                segment_k = jnp.concatenate([segment_k] * (block // TILE), axis=1)
                score = jnp.where(segment_k == segment_q, raw[rows, :] + bias, MASKED_SCORE)
                score_ref[head, rows, :] = score
                highest = jnp.maximum(
                    highest, jnp.max(score.reshape(TILE // 8, 8, block), axis=0)
                )
            top = jnp.max(highest, axis=0, keepdims=True)
            total = jnp.zeros((8, block), jnp.float32)
            for tile in range(tiles):
                rows = slice(tile * TILE, (tile + 1) * TILE)
                exponent = jnp.exp(score_ref[head, rows, :] - top)
                total = total + fold_rows(exponent)
                e_ref[head, rows, pl.ds(first, block)] = exponent.astype(jnp.bfloat16)
            inverse = 1.0 / jnp.sum(total, axis=0, keepdims=True)
            inv_ref[head, :, pl.ds(first, block)] = inverse
            context = jnp.dot(
                values_t[head * DH : (head + 1) * DH, :],
                e_ref[head, :, pl.ds(first, block)],
                preferred_element_type=jnp.float32,
            )
            outs.append(context * inverse)
        ctx_ref[pl.ds(first, block), :] = jnp.transpose(jnp.concatenate(outs, axis=0)).astype(
            jnp.bfloat16
        )

    for_blocks(length // block, block, one_block)


def for_blocks(count, block, body):
    if count == 1:
        body(0)
        return

    def step(index, carry):
        body(pl.multiple_of(index * block, block))
        return carry

    lax.fori_loop(0, count, step, 0)


def attention_forward(qkv, place, segment_row, segment_wide, bias_line, heads, token_rows):
    length = qkv.shape[0]
    block = query_block(length)
    pairs = heads // 2
    return pl.pallas_call(
        functools.partial(forward_kernel, block, token_rows),
        grid=(pairs,),
        in_specs=[
            pl.BlockSpec(memory_space=pltpu.SMEM),
            pl.BlockSpec((length, 3 * PAIR), lambda i: (0, i)),
            pl.BlockSpec((1, length), lambda i: (0, 0)),
            pl.BlockSpec((length, TILE), lambda i: (0, 0)),
            pl.BlockSpec((1, 2, 2 * length), lambda i: (i, 0, 0)),
        ],
        out_specs=[
            pl.BlockSpec((length, PAIR), lambda i: (0, i)),
            pl.BlockSpec((2, length, length), lambda i: (i, 0, 0)),
            pl.BlockSpec((2, 1, length), lambda i: (i, 0, 0)),
        ],
        out_shape=[
            jax.ShapeDtypeStruct((length, heads * DH), jnp.bfloat16),
            jax.ShapeDtypeStruct((heads, length, length), jnp.bfloat16),
            jax.ShapeDtypeStruct((heads, 1, length), jnp.float32),
        ],
        scratch_shapes=[
            pltpu.VMEM((2, TILE, 2 * length), jnp.float32),
            pltpu.VMEM((2, length, block), jnp.float32),
        ],
        compiler_params=pltpu.CompilerParams(vmem_limit_bytes=VMEM_BYTES),
        cost_estimate=NO_COST,
        name="attention_forward",
    )(place, qkv, segment_row, segment_wide, bias_line)


def backward_kernel(
    block,
    token_rows,
    place_ref,
    qkv_ref,
    d_ref,
    e_ref,
    inv_ref,
    grad_ref,
    line_ref,
    strip_ref,
    prob_ref,
    low_ref,
    key_sum,
    value_sum,
):
    length = qkv_ref.shape[0]
    q_ref = qkv_ref.at[:, :PAIR]
    k_ref = qkv_ref.at[:, PAIR : 2 * PAIR]
    v_ref = qkv_ref.at[:, 2 * PAIR :]
    tiles = length // TILE
    place = place_ref[0]
    keys_t = jnp.transpose(k_ref[...])
    strip_ref[...] = jnp.zeros_like(strip_ref)
    key_sum[...] = jnp.zeros_like(key_sum)
    value_sum[...] = jnp.zeros_like(value_sum)

    def one_block(first):
        q_block = q_ref[pl.ds(first, block), :]
        d_block = d_ref[pl.ds(first, block), :]
        outs = []
        for head in range(2):
            mask = half_lanes(q_block.shape, head)
            q_head = jnp.where(mask, q_block, jnp.zeros_like(q_block))
            inverse = inv_ref[head, :, pl.ds(first, block)]
            scale = jnp.transpose(jnp.broadcast_to(inverse, (PAIR, block)))
            d_head = jnp.where(mask, d_block.astype(jnp.float32) * scale, 0.0)
            d_head = d_head.astype(jnp.bfloat16)
            prob_ref[head] = cols_dot(v_ref[...], d_head)
            value_sum[...] += jnp.dot(
                e_ref[head, :, pl.ds(first, block)], d_head, preferred_element_type=jnp.float32
            )
            total = jnp.zeros((8, block), jnp.float32)
            for tile in range(tiles):
                rows = slice(tile * TILE, (tile + 1) * TILE)
                exponent = e_ref[head, rows, pl.ds(first, block)].astype(jnp.float32)
                total = total + fold_rows(exponent * prob_ref[head, rows, :])
            centre = jnp.sum(total, axis=0, keepdims=True) * inverse
            for tile in range(tiles):
                rows = slice(tile * TILE, (tile + 1) * TILE)
                exponent = e_ref[head, rows, pl.ds(first, block)].astype(jnp.float32)
                grad = exponent * (prob_ref[head, rows, :] - centre)
                offsets, group = bias_offsets(first, block, length, token_rows, place, tile)
                for part, offset in enumerate(offsets):
                    at = pl.ds(offset, group)
                    strip_ref[head, :, at] = (
                        strip_ref[head, :, at] + grad[:, part * group : (part + 1) * group]
                    )
                low_ref[head, rows, :] = grad.astype(jnp.bfloat16)
            key_sum[...] += jnp.dot(low_ref[head], q_head, preferred_element_type=jnp.float32)
            outs.append(
                jnp.dot(
                    keys_t[head * DH : (head + 1) * DH, :],
                    low_ref[head],
                    preferred_element_type=jnp.float32,
                )
            )
        grad_ref[pl.ds(first, block), :PAIR] = jnp.transpose(
            jnp.concatenate(outs, axis=0)
        ).astype(jnp.bfloat16)

    for_blocks(length // block, block, one_block)
    grad_ref[:, PAIR : 2 * PAIR] = key_sum[...].astype(jnp.bfloat16)
    grad_ref[:, 2 * PAIR :] = value_sum[...].astype(jnp.bfloat16)
    for head in range(2):
        turned = strip_ref[head]
        while turned.shape[0] > 1:
            half = turned.shape[0] // 2
            turned = pltpu.roll(turned[:half], half, 1) + turned[half:]
        line_ref[0, head : head + 1, :] = turned


def attention_backward(qkv, place, d, e, inv, heads, token_rows):
    length = qkv.shape[0]
    block = query_block(length)
    pairs = heads // 2
    triple = pl.BlockSpec((length, 3 * PAIR), lambda i: (0, i))
    return pl.pallas_call(
        functools.partial(backward_kernel, block, token_rows),
        grid=(pairs,),
        in_specs=[
            pl.BlockSpec(memory_space=pltpu.SMEM),
            triple,
            pl.BlockSpec((length, PAIR), lambda i: (0, i)),
            pl.BlockSpec((2, length, length), lambda i: (i, 0, 0)),
            pl.BlockSpec((2, 1, length), lambda i: (i, 0, 0)),
        ],
        out_specs=[triple, pl.BlockSpec((1, 2, 2 * length), lambda i: (i, 0, 0))],
        out_shape=[
            jax.ShapeDtypeStruct((length, 3 * heads * DH), jnp.bfloat16),
            jax.ShapeDtypeStruct((pairs, 2, 2 * length), jnp.float32),
        ],
        scratch_shapes=[
            pltpu.VMEM((2, TILE, 2 * length), jnp.float32),
            pltpu.VMEM((2, length, block), jnp.float32),
            pltpu.VMEM((2, length, block), jnp.bfloat16),
            pltpu.VMEM((length, PAIR), jnp.float32),
            pltpu.VMEM((length, PAIR), jnp.float32),
        ],
        compiler_params=pltpu.CompilerParams(vmem_limit_bytes=VMEM_BYTES),
        cost_estimate=NO_COST,
        name="attention_backward",
    )(place, qkv, d, e, inv)


def swap(piece, axis, step):
    return lax.ppermute(piece, axis, [(i, i ^ step) for i in range(lax.axis_size(axis))])


def gather_begin(piece, relay=True):
    count = lax.axis_size("seq")
    steps = (1, 2) if count == 4 and relay else range(1, count)
    return tuple(swap(piece, "seq", step) for step in steps)


def gather_end(piece, near):
    if len(near) != 2:
        return [[part] for part in (piece, *near)]
    first, second = near
    half = piece.shape[0] // 2
    upper = swap(second[:half], "seq", 1)
    lower = swap(first[half:], "seq", 2)
    return [[piece], [first], [second], [upper, lower]]


def joined(parts):
    return jnp.concatenate([part for pieces in parts for part in pieces], axis=0)


def gather_rows(piece):
    return joined(gather_end(piece, gather_begin(piece)))


def low_dot(rows, weights):
    return cols_dot(rows, weights).astype(jnp.bfloat16)


def split_terms(terms):
    count = lax.axis_size("seq")
    size = terms.shape[0] // (count - 1)
    return (terms[: 2 * size], terms[2 * size :]) if count == 4 else (terms, None)


def scatter_begin(far):
    if far is None:
        return ()
    half = far.shape[0] // 2
    return swap(far[:half], "seq", 1), swap(far[half:], "seq", 2)


def scatter_add(near, passing):
    if not passing:
        size = near.shape[0] // (lax.axis_size("seq") - 1)
        return tuple(near[start : start + size] for start in range(0, near.shape[0], size))
    size = near.shape[0] // 2
    upper, lower = (part.astype(jnp.float32) for part in passing)
    first = near[:size].astype(jnp.float32) + jnp.pad(lower, ((size // 2, 0), (0, 0)))
    second = near[size:].astype(jnp.float32) + jnp.pad(upper, ((0, size // 2), (0, 0)))
    return first.astype(jnp.bfloat16), second.astype(jnp.bfloat16)


def scatter_end(sums):
    return tuple(swap(part, "seq", k + 1) for k, part in enumerate(sums))


def scatter_early(near):
    if lax.axis_size("seq") != 4:
        return ()
    size = near.shape[0] // 2
    half = size // 2
    return swap(near[:half], "seq", 1), swap(near[size + half :], "seq", 2)


def scatter_late(near, passing, early):
    if not passing:
        return [(part,) for part in scatter_end(scatter_add(near, passing))]
    size = near.shape[0] // 2
    half = size // 2
    upper, lower = (part.astype(jnp.float32) for part in passing)
    first = near[half:size].astype(jnp.float32) + lower
    second = near[size : size + half].astype(jnp.float32) + upper
    first_lower = swap(first.astype(jnp.bfloat16), "seq", 1)
    second_upper = swap(second.astype(jnp.bfloat16), "seq", 2)
    first_upper, second_lower = early
    return [(first_upper, first_lower), (second_upper, second_lower)]


def add_parts(own, received):
    return own + sum(part.astype(jnp.float32) for part in received)


def scatter_sum(rows, weights):
    size = rows.shape[0] // lax.axis_size("seq")
    near, far = split_terms(low_dot(rows[size:], weights))
    received = scatter_end(scatter_add(near, scatter_begin(far)))
    return add_parts(cols_dot(rows[:size], weights), received)


def seq_sum(values):
    level = [values] + [swap(values, "seq", step) for step in range(1, lax.axis_size("seq"))]
    while len(level) > 1:
        level = [level[i] + level[i + 1] for i in range(0, len(level), 2)]
    return level[0]


def feed_forward_kernel(tile, x_ref, w_ref, act_ref, gelu_ref, slope_ref):
    rows = x_ref.shape[0]
    chunk = min(512, rows)
    for start in range(0, rows, chunk):
        at = slice(start, start + chunk)
        both = jnp.dot(x_ref[at, :], w_ref[...], preferred_element_type=jnp.float32)
        gate, up = both[:, :tile], both[:, tile:]
        square = gate * gate
        tanh = jnp.tanh(GELU_SCALE * gate * (1.0 + GELU_CUBE * square))
        half_up = 0.5 * (1.0 + tanh)
        gelu = gate * half_up
        bend = 0.5 * GELU_SCALE * gate * (1.0 - tanh * tanh) * (1.0 + 3.0 * GELU_CUBE * square)
        act_ref[at, :] = (gelu * up).astype(jnp.bfloat16)
        gelu_ref[at, :] = gelu.astype(jnp.bfloat16)
        slope_ref[at, :] = (up * (half_up + bend)).astype(jnp.bfloat16)


def feed_forward(rows, weights, tile):
    length, model_width = rows.shape
    units = weights.shape[1] // 2
    block = pl.BlockSpec((length, tile), lambda j: (0, j))
    return pl.pallas_call(
        functools.partial(feed_forward_kernel, tile),
        grid=(units // tile,),
        in_specs=[
            pl.BlockSpec((length, model_width), lambda j: (0, 0)),
            pl.BlockSpec((model_width, 2 * tile), lambda j: (0, j)),
        ],
        out_specs=[block, block, block],
        out_shape=[
            jax.ShapeDtypeStruct((length, units), jnp.bfloat16),
            jax.ShapeDtypeStruct((length, units), jnp.bfloat16),
            jax.ShapeDtypeStruct((length, units), jnp.bfloat16),
        ],
        compiler_params=pltpu.CompilerParams(vmem_limit_bytes=VMEM_BYTES),
        cost_estimate=NO_COST,
        name="feed_forward",
    )(rows, weights)


def feed_forward_back_kernel(tile, d_ref, w_ref, gelu_ref, slope_ref, grad_ref):
    rows = d_ref.shape[0]
    chunk = min(512, rows)
    for start in range(0, rows, chunk):
        at = slice(start, start + chunk)
        grad = jnp.dot(d_ref[at, :], w_ref[...], preferred_element_type=jnp.float32)
        grad_ref[at, :tile] = (grad * slope_ref[at, :].astype(jnp.float32)).astype(jnp.bfloat16)
        grad_ref[at, tile:] = (grad * gelu_ref[at, :].astype(jnp.float32)).astype(jnp.bfloat16)


def feed_forward_back(grad_rows, weights, gelu, slope, tile):
    length, model_width = grad_rows.shape
    units = weights.shape[1]
    block = pl.BlockSpec((length, tile), lambda j: (0, j))
    return pl.pallas_call(
        functools.partial(feed_forward_back_kernel, tile),
        grid=(units // tile,),
        in_specs=[
            pl.BlockSpec((length, model_width), lambda j: (0, 0)),
            pl.BlockSpec((model_width, tile), lambda j: (0, j)),
            block,
            block,
        ],
        out_specs=pl.BlockSpec((length, 2 * tile), lambda j: (0, j)),
        out_shape=jax.ShapeDtypeStruct((length, 2 * units), jnp.bfloat16),
        compiler_params=pltpu.CompilerParams(vmem_limit_bytes=VMEM_BYTES),
        cost_estimate=NO_COST,
        name="feed_forward_back",
    )(grad_rows, weights, gelu, slope)


def place_kernel(moves, lengths, block, widths, weighed, place_ref, *refs):
    count = sum(lengths)
    weights = refs[count : count + len(weighed)]
    outs = refs[count + len(weighed) : count + len(weighed) + len(widths)]
    total = jnp.zeros((block, TILE), jnp.float32)
    first = 0
    for step, length in enumerate(lengths):
        pieces = refs[first : first + length]
        first += length
        owner = jnp.bitwise_xor(place_ref[0], step)
        for out, source, target, size in moves:
            at = pl.ds(pl.multiple_of(owner * widths[out] + target, TILE), size)
            part = pieces[0][:, source : source + size]
            if length == 2:
                upper = pl.program_id(0) < pl.num_programs(0) // 2
                part = jnp.where(upper, part, pieces[1][:, source : source + size])
            part = part.astype(jnp.float32)
            outs[out][:, at] = part
            if out in weighed:
                part = part * weights[weighed.index(out)][:, at].astype(jnp.float32)
                for start in range(0, size, TILE):
                    total = total + part[:, start : start + TILE]
    if weighed:
        refs[-1][...] = total


def place_columns(parts, place, moves, widths, weights=()):
    lengths = tuple(len(pieces) for pieces in parts)
    count = lax.axis_size("seq")
    rows, width = parts[0][0].shape
    block = min(64, rows // 2)
    steps = rows // block

    def wide(size):
        return pl.BlockSpec((block, size), lambda i: (i, 0))

    def piece_specs(length):
        if length == 1:
            return [wide(width)]
        half = steps // 2
        return [
            pl.BlockSpec((block, width), lambda i: (jnp.minimum(i, half - 1), 0)),
            pl.BlockSpec((block, width), lambda i: (jnp.maximum(i - half, 0), 0)),
        ]

    whole = [wide(count * size) for size in widths]
    sums = [wide(TILE)] if weights else []
    shapes = [count * size for size in widths] + [TILE] * len(sums)
    weighed = tuple(range(len(weights)))
    return pl.pallas_call(
        functools.partial(place_kernel, moves, lengths, block, widths, weighed),
        grid=(steps,),
        in_specs=[pl.BlockSpec(memory_space=pltpu.SMEM)]
        + [spec for length in lengths for spec in piece_specs(length)]
        + whole[: len(weights)],
        out_specs=whole + sums,
        out_shape=[jax.ShapeDtypeStruct((rows, size), jnp.float32) for size in shapes],
        compiler_params=pltpu.CompilerParams(vmem_limit_bytes=VMEM_BYTES),
        cost_estimate=pl.CostEstimate(
            flops=0, bytes_accessed=8 * rows * sum(shapes), transcendentals=0
        ),
        name="place_columns",
    )(place, *[piece for pieces in parts for piece in pieces], *weights)


def take_kernel(moves, count, place_ref, *refs):
    out_ref = refs[count]
    for which, source, target, size in moves:
        out_ref[:, source : source + size] = refs[which][:, target : target + size]


def take_columns(place, weights, moves, counts):
    rows = weights[0].shape[0]
    block = min(128, rows)
    width = sum(counts)

    def chosen(count):
        return pl.BlockSpec((block, count), lambda i, place_ref: (i, place_ref[0]))

    return pl.pallas_call(
        functools.partial(take_kernel, moves, len(weights)),
        grid_spec=pltpu.PrefetchScalarGridSpec(
            num_scalar_prefetch=1,
            grid=(rows // block,),
            in_specs=[chosen(count) for count in counts],
            out_specs=pl.BlockSpec((block, width), lambda i, place_ref: (i, 0)),
        ),
        out_shape=jax.ShapeDtypeStruct((rows, width), weights[0].dtype),
        compiler_params=pltpu.CompilerParams(vmem_limit_bytes=VMEM_BYTES),
        cost_estimate=NO_COST,
        name="take_columns",
    )(place, *weights)


def turn_kernel(core_ref, own_in, other_in, own_ref, other_ref):
    own_ref[...] = jnp.transpose(own_in[...])
    other_ref[...] = jnp.transpose(other_in[...])


def turn_halves(rows, core, groups):
    length, width = rows.shape
    size = width // groups

    def chosen(side):
        return pl.BlockSpec(
            (length, size), lambda i, core_ref: (0, 2 * i + jnp.bitwise_xor(core_ref[0], side))
        )

    half = jax.ShapeDtypeStruct((width // 2, length), rows.dtype)
    block = pl.BlockSpec((size, length), lambda i, core_ref: (i, 0))
    return pl.pallas_call(
        turn_kernel,
        grid_spec=pltpu.PrefetchScalarGridSpec(
            num_scalar_prefetch=1,
            grid=(groups // 2,),
            in_specs=[chosen(0), chosen(1)],
            out_specs=[block, block],
        ),
        out_shape=[half, half],
        compiler_params=pltpu.CompilerParams(vmem_limit_bytes=VMEM_BYTES),
        cost_estimate=NO_COST,
        name="turn_halves",
    )(core, rows, rows)


def added_dot_kernel(left_ref, right_ref, added_ref, out_ref):
    rows = left_ref.shape[0]
    chunk = min(512, rows)
    for start in range(0, rows, chunk):
        at = slice(start, start + chunk)
        product = jnp.dot(left_ref[at, :], right_ref[...], preferred_element_type=jnp.float32)
        out_ref[at, :] = (product + added_ref[at, :].astype(jnp.float32)).astype(jnp.bfloat16)


def added_dot(left, right, added):
    rows, depth = left.shape
    width = right.shape[1]
    tile = next(t for t in (512, 256, 128) if width % t == 0)
    column = pl.BlockSpec((rows, tile), lambda j: (0, j))
    return pl.pallas_call(
        added_dot_kernel,
        grid=(width // tile,),
        in_specs=[
            pl.BlockSpec((rows, depth), lambda j: (0, 0)),
            pl.BlockSpec((depth, tile), lambda j: (0, j)),
            column,
        ],
        out_specs=column,
        out_shape=jax.ShapeDtypeStruct((rows, width), jnp.bfloat16),
        compiler_params=pltpu.CompilerParams(vmem_limit_bytes=VMEM_BYTES),
        cost_estimate=NO_COST,
        name="added_dot",
    )(left, right, added)


def both(*values):
    return lax.optimization_barrier(values)


def on_device(
    tokens,
    segments,
    buckets,
    w_query,
    w_key,
    w_value,
    w_attn_out,
    gain_attn,
    rel_table,
    w_gate,
    w_up,
    w_down,
    gain_ffn,
    out_grad,
):
    token_rows = tokens.shape[1]
    model_width = tokens.shape[2]
    ffn_width = w_gate.shape[1]
    segment_row = segments[0]
    row_length = segment_row.shape[0]
    seq_count = lax.axis_size("seq")
    fsdp_count = lax.axis_size("fsdp")
    seq_place = lax.axis_index("seq")
    fsdp_place = lax.axis_index("fsdp")
    place = seq_place.astype(jnp.int32).reshape(1)
    head_count = model_width // seq_count // DH
    column_count = model_width // seq_count
    unit_count = ffn_width // seq_count

    tile = 256 if unit_count % 256 == 0 else 128
    pairs = head_count // 2

    def gather_weights(piece):
        return lax.all_gather(piece, "fsdp", axis=0, tiled=True)

    qkv_moves = [
        (which, (3 * pair + which) * PAIR, pair * PAIR, PAIR)
        for pair in range(pairs)
        for which in range(3)
    ] + [(3, 3 * column_count, 0, column_count)]
    unit_moves = [
        (which, (2 * block + which) * tile, block * tile, tile)
        for block in range(unit_count // tile)
        for which in range(2)
    ]
    attn_part = take_columns(
        place, (w_query, w_key, w_value, w_attn_out), qkv_moves, [column_count] * 4
    )
    attn_w = gather_weights(attn_part)
    gains = lax.all_gather(jnp.stack([gain_attn, gain_ffn]), "fsdp", axis=1, tiled=True)
    qkv_w = attn_w[:, : 3 * column_count]
    output_w = attn_w[:, 3 * column_count :]

    table_rows = jnp.pad(buckets[::-1], (0, 1), constant_values=-1)
    bucket_table = (
        table_rows[:, None] == jnp.arange(rel_table.shape[1], dtype=jnp.int32)[None, :]
    ).astype(jnp.float32)
    local_table = lax.dynamic_slice_in_dim(rel_table, seq_place * head_count, head_count, 0)
    bias_line = jnp.dot(local_table, jnp.transpose(bucket_table), precision=PRECISE)
    bias_line = bias_line.reshape(head_count // 2, 2, 2 * row_length)
    segment_wide = jnp.broadcast_to(segment_row[:, None], (row_length, TILE))

    stream = tokens[0].astype(jnp.float32)
    scale_attn = lax.rsqrt(jnp.mean(stream * stream, axis=-1, keepdims=True) + EPSILON)
    normed_attn = stream * scale_attn

    stream_near = gather_begin(tokens[0])
    stream_near, gains = both(stream_near, gains)
    attn_gain = gains[0].astype(jnp.float32)
    ffn_gain = gains[1].astype(jnp.float32)
    stream_rows = joined(gather_end(tokens[0], stream_near))
    gate_up_part = take_columns(place, (w_gate, w_up), unit_moves, [unit_count] * 2)
    gate_up_part, stream_rows = both(gate_up_part, stream_rows)
    gate_up_w = gather_weights(gate_up_part)
    stream_rows = stream_rows.astype(jnp.float32)
    rows_scale = lax.rsqrt(jnp.mean(stream_rows * stream_rows, axis=-1, keepdims=True) + EPSILON)
    attn_rows = (stream_rows * rows_scale * attn_gain).astype(jnp.bfloat16)
    ff_grad_rows = gather_rows(out_grad[0])
    attn_rows, ff_grad_rows = both(attn_rows, ff_grad_rows)

    qkv = jnp.dot(attn_rows, qkv_w, preferred_element_type=jnp.float32).astype(jnp.bfloat16)
    down_part, qkv = both(
        lax.dynamic_slice_in_dim(w_down, seq_place * unit_count, unit_count, 1), qkv
    )
    down_w = gather_weights(down_part)
    context, exponents, inverse = attention_forward(
        qkv, place, segments, segment_wide, bias_line, head_count, token_rows
    )

    attn_out = scatter_sum(context, output_w)
    chips = fsdp_count // 2
    core = (fsdp_place % 2).astype(jnp.int32).reshape(1)
    groups = [[2 * chip + side for chip in range(chips)] for side in range(2)]

    def scatter_grads(grads, axis_index_groups=None):
        return lax.psum_scatter(
            grads,
            "fsdp",
            scatter_dimension=0,
            tiled=True,
            axis_index_groups=axis_index_groups,
        )

    resid = stream + attn_out
    scale_ffn = lax.rsqrt(jnp.mean(resid * resid, axis=-1, keepdims=True) + EPSILON)
    normed_ffn = resid * scale_ffn
    ffn_rows = gather_rows((normed_ffn * ffn_gain).astype(jnp.bfloat16))

    hidden, gelu, slope = feed_forward(ffn_rows, gate_up_w, tile)

    down_grad = rows_dot(ff_grad_rows, hidden).astype(jnp.bfloat16)
    down_owned = scatter_grads(down_grad)
    down_grad, hidden, gelu = both(down_grad, hidden, gelu)
    away = row_length // seq_count
    passed = 3 * away if seq_count == 4 else row_length
    ff_far = low_dot(hidden[passed:], down_w) if seq_count == 4 else None
    ff_far, hidden, gelu = both(ff_far, hidden, gelu)
    ff_passing = scatter_begin(ff_far)
    unit_grad = feed_forward_back(ff_grad_rows, down_w, gelu, slope, tile)
    unit_far = low_dot(unit_grad[passed:], gate_up_w) if seq_count == 4 else None
    unit_far, unit_grad, ff_passing = both(unit_far, unit_grad, ff_passing)
    unit_passing = scatter_begin(unit_far)
    unit_terms = low_dot(unit_grad[:passed], gate_up_w)
    unit_early = scatter_early(unit_terms[away:])
    unit_terms, unit_grad, unit_passing = both(unit_terms, unit_grad, unit_passing)
    unit_parts = scatter_late(unit_terms[away:], unit_passing, unit_early)
    gate_up_grad = rows_dot(ffn_rows, unit_grad).astype(jnp.bfloat16)
    gate_up_grad, unit_parts = both(gate_up_grad, unit_parts)
    gate_up_owned = scatter_grads(gate_up_grad)
    resid_grad, attn_grad = norm_backward(unit_terms, unit_parts, out_grad[0], resid, ffn_gain)
    attn_grad, hidden, down_owned = both(attn_grad, hidden, down_owned)
    attn_grad_rows = gather_rows(attn_grad)
    ff_near = low_dot(hidden[away:passed], down_w)
    ff_sums = scatter_add(ff_near, ff_passing)
    attn_grad_rows, ff_sums, down_owned = both(attn_grad_rows, ff_sums, down_owned)
    context_grad = jnp.dot(
        attn_grad_rows, output_w, preferred_element_type=jnp.float32
    ).astype(jnp.bfloat16)
    ff_parts = scatter_end(ff_sums)
    down_near = gather_begin(down_owned, relay=False)
    qkv_grad, line_grad = attention_backward(
        qkv, place, context_grad, exponents, inverse, head_count, token_rows
    )
    qkv_terms = low_dot(qkv_grad[away:], qkv_w)
    qkv_terms, qkv_grad, ff_parts, down_near = both(qkv_terms, qkv_grad, ff_parts, down_near)
    qkv_near, qkv_far = split_terms(qkv_terms)
    qkv_passing = scatter_begin(qkv_far)
    attn_grads = rows_dot(attn_rows, qkv_grad).astype(jnp.bfloat16)
    attn_grads, context, qkv_grad, attn_grad_rows, qkv_passing, gate_up_owned, hidden = both(
        attn_grads, context, qkv_grad, attn_grad_rows, qkv_passing, gate_up_owned, hidden
    )
    attn_owned = scatter_grads(attn_grads)
    gate_up_near = gather_begin(gate_up_owned)
    attn_in_parts = scatter_end(scatter_add(qkv_near, qkv_passing))
    output_own, output_other = turn_halves(attn_grad_rows, core, fsdp_count)
    output_away = jnp.dot(
        output_other, context, preferred_element_type=jnp.float32
    ).astype(jnp.bfloat16)
    output_added = swap(output_away, "fsdp", 1)
    attn_in_own = cols_dot(qkv_grad[:away], qkv_w)
    output_grad = added_dot(output_own, context, output_added)
    ff_out = add_parts(cols_dot(hidden[:away], down_w), ff_parts)
    result = resid + ff_out
    own_segments = lax.dynamic_slice_in_dim(segment_row, seq_place * token_rows, token_rows, 0)
    valid = (own_segments >= 0).astype(jnp.float32)
    stat_terms = jnp.stack(
        [
            jnp.sum(valid * jnp.sum(result * result, axis=-1)),
            jnp.sum(valid * jnp.sum(attn_out * attn_out, axis=-1)),
            jnp.sum(valid * jnp.sum(ff_out * ff_out, axis=-1)),
            jnp.sum(valid),
        ]
    )
    table_part = jnp.dot(
        line_grad.reshape(head_count, 2 * row_length), bucket_table, precision=PRECISE
    )
    full_table = lax.dynamic_update_slice_in_dim(
        jnp.zeros(rel_table.shape, jnp.float32), table_part, seq_place * head_count, 0
    )
    packed = jnp.concatenate([full_table.reshape(-1), jnp.pad(stat_terms, (0, TILE - 4))])
    gate_up_near, packed, output_grad, attn_in_own, result = both(
        gate_up_near, packed, output_grad, attn_in_own, result
    )
    output_owned = scatter_grads(output_grad, groups)
    gate_up_pieces = gather_end(gate_up_owned, gate_up_near)
    down_pieces = gather_end(down_owned, down_near)
    (down_out,) = place_columns(down_pieces, place, [(0, 0, 0, unit_count)], [unit_count])
    summed = jnp.sum(lax.all_gather(packed.reshape(-1, TILE), "fsdp"), axis=0)
    summed, attn_in_parts = both(summed, attn_in_parts)
    summed = seq_sum(summed)
    attn_owned, summed, down_out, gate_up_pieces, attn_in_parts = both(
        attn_owned, summed, down_out, gate_up_pieces, attn_in_parts
    )
    attn_near = gather_begin(attn_owned)
    attn_in_grad = add_parts(attn_in_own, attn_in_parts)
    stream_grad = resid_grad + norm_back(attn_in_grad * attn_gain, normed_attn, scale_attn)
    stream_grad = stream_grad.astype(jnp.bfloat16)
    gate_out, up_out, ffn_sums = place_columns(
        gate_up_pieces, place, unit_moves, [unit_count] * 2, (w_gate, w_up)
    )
    attn_near, stream_grad, gate_out, up_out = both(attn_near, stream_grad, gate_out, up_out)
    attn_pieces = gather_end(attn_owned, attn_near)
    attn_pieces[-1][0], output_owned = both(attn_pieces[-1][0], output_owned)
    summed = summed.reshape(-1)
    output_near = gather_begin(output_owned, relay=False)
    attn_outs = place_columns(
        attn_pieces,
        place,
        qkv_moves[:-1],
        [column_count] * 3,
        (w_query, w_key, w_value),
    )
    query_out, key_out, value_out, attn_sums = attn_outs
    gain_attn_grad = jnp.sum(attn_sums, axis=1) / gain_attn.astype(jnp.float32)
    gain_ffn_grad = jnp.sum(ffn_sums, axis=1) / gain_ffn.astype(jnp.float32)
    output_near, gain_attn_grad, gain_ffn_grad = both(output_near, gain_attn_grad, gain_ffn_grad)
    (output_out,) = place_columns(
        gather_end(output_owned, output_near), place, [(0, 0, 0, column_count)], [column_count]
    )
    stat_totals = summed[rel_table.size : rel_table.size + 4]
    rms_stats = jnp.sqrt(stat_totals[0:3] / (stat_totals[3] * model_width))
    table_share = rel_table.shape[0] // fsdp_count
    rel_table_grad = lax.dynamic_slice_in_dim(
        summed[: rel_table.size].reshape(rel_table.shape),
        fsdp_place * table_share,
        table_share,
        0,
    )
    return (
        result.astype(jnp.bfloat16)[None],
        stream_grad[None],
        query_out,
        key_out,
        value_out,
        output_out,
        gain_attn_grad,
        rel_table_grad,
        gate_out,
        up_out,
        down_out,
        gain_ffn_grad,
        rms_stats,
    )


def solution(mesh):
    in_specs = (
        P("fsdp", "seq", None),
        P("fsdp", None),
        P(),
        P("fsdp", None),
        P("fsdp", None),
        P("fsdp", None),
        P("fsdp", None),
        P("fsdp"),
        P(),
        P("fsdp", None),
        P("fsdp", None),
        P("fsdp", None),
        P("fsdp"),
        P("fsdp", "seq", None),
    )
    out_specs = (
        P("fsdp", "seq", None),
        P("fsdp", "seq", None),
        P("fsdp", None),
        P("fsdp", None),
        P("fsdp", None),
        P("fsdp", None),
        P("fsdp"),
        P("fsdp", None),
        P("fsdp", None),
        P("fsdp", None),
        P("fsdp", None),
        P("fsdp"),
        P(),
    )
    return jax.shard_map(
        on_device, mesh=mesh, in_specs=in_specs, out_specs=out_specs, check_vma=False
    )
```
